32 devices in a mesh: dom: 16 (over z, y, x), cell: 2 (over core).
Axes of the slice: x: 2, y: 2, z: 4, core: 2. Of those that a mesh axis runs over, the one named last changes fastest.
Arguments:
- features: bfloat16 [8192, 128], P(('cell', 'dom')), parts along dimension 0, may hold values from -6 to 6
- positions: float32 [3, 8192], P(None, ('cell', 'dom')), parts along dimension 1, may hold values from 0 to 80, as said below
- neighbours: int32 [8192, 64], P(('cell', 'dom')), parts along dimension 0, may hold values from 0 to 767, as said below
- neighbour_count: int32 [8192], P(('cell', 'dom')), parts along dimension 0, may hold values from 16 to 64, as said below
- ghost_sends: int32 [2, 8192], P(None, ('cell', 'dom')), parts along dimension 1, may hold values from 0 to 255, as said below
- species: int32 [8192], P(('cell', 'dom')), parts along dimension 0, may hold values from 0 to 5
- wave_index: int32 [3, 1024], replicated, may hold values from -8 to 8, as said below
- force_ref: float32 [3, 8192], P(None, ('cell', 'dom')), parts along dimension 1, may hold values from -6 to 6
- radial_weight: bfloat16 [16, 128], replicated, may hold values from -1.5 to 1.5
- mix_weight: bfloat16 [128, 128], replicated, may hold values from -0.5 to 0.5
- charge_weight: bfloat16 [128, 64], replicated, may hold values from -0.5 to 0.5
- species_charge: float32 [6, 64], replicated, may hold values from -4 to 4
Outputs:
- forces: float32 [3, 8192], P(None, ('cell', 'dom')), parts along dimension 1
- radial_step: float32 [32, 128], P('cell'), parts along dimension 0
- mix_step: float32 [256, 128], P('cell'), parts along dimension 0
- charge_step: float32 [256, 64], P('cell'), parts along dimension 0
- species_step: float32 [12, 64], P('cell'), parts along dimension 0
The draws below stay inside these ranges and needn't reach their ends.
There are 2 independent parts, one for each index of `cell`. The reference program is written for one: setup_inputs(seed, part) draws one part's arguments, and reference() takes and returns one part's arrays. A program takes and returns all parts, laid end to end along the dimension named above; an argument that names none is the same for every part. Nothing has to cross between parts.
Inputs may be any that keep to these rules, and one draw needn't show every extreme that they name: `neighbours`: in the shard of domain d, an entry e below 256 names the domain's own atom e; 256 + g names the atom at position g of row 1 of ghost_sends of domain d - 1; 512 + g names the atom at position g of row 0 of ghost_sends of domain d + 1 (domains cyclic). Entries of a row are distinct and never the atom itself. `neighbour_count`: slots below the count are live; in every domain some atom has all 64 slots live. `ghost_sends`: positions within the domain's shard; the entries of one row of one domain are distinct. `wave_index`: columns are distinct and their first component is 1 or more. `positions`: coordinates in a periodic box of 80 along the first axis and 20 along the other two.
All inputs are finite; a program needn't handle non-finite values.
Results may differ from the reference program's by a relative error of at most 0.0051.
Values may be sent and summed in bfloat16 or wider, within the bound.
No kernel may reach another device: no remote copies, remote signals or barrier semaphores. Data moves between devices by JAX's collectives and lax.ppermute only.
A program may use at most 64 MiB of HBM per device.

```python
import jax
import jax.numpy as jnp
import numpy as np
from jax import lax

C = 128
Q = 64
K = 1024
NRBF = 16
NB = 64
SPEC = 6
GHOST = 256
ATOM_DEV = 256
ATOMS = 4096


def offset_table():
    rows_list = []
    for step_x in range(-4, 5):
        for step_y in range(-2, 3):
            for step_z in range(-2, 3):
                if step_x != 0 or step_y != 0 or step_z != 0:
                    if step_x * step_x + 4 * (step_y * step_y + step_z * step_z) <= 20:
                        rows_list.append((step_x, step_y, step_z))
    return np.array(rows_list, dtype=np.int32)


def lattice_layout(key):
    domains = ATOMS // ATOM_DEV
    layers = ATOM_DEV // 64
    ghost_layers = GHOST // 64
    order_scores = jax.random.randint(jax.random.fold_in(key, 101), (domains, ATOM_DEV), 0, 1 << 16) * ATOM_DEV + jnp.arange(ATOM_DEV, dtype=jnp.int32)
    site_of_slot = jnp.argsort(order_scores, axis=1).astype(jnp.int32)
    slot_of_site = jnp.argsort(site_of_slot, axis=1).astype(jnp.int32)
    ghost_scores = jax.random.randint(jax.random.fold_in(key, 102), (domains, 2, GHOST), 0, 1 << 16) * GHOST + jnp.arange(GHOST, dtype=jnp.int32)
    ghost_order = jnp.argsort(ghost_scores, axis=2).astype(jnp.int32)
    ghost_rank = jnp.argsort(ghost_order, axis=2).astype(jnp.int32)
    sends_low = jnp.take_along_axis(slot_of_site, ghost_order[:, 0, :], axis=1)
    sends_high = jnp.take_along_axis(slot_of_site, ATOM_DEV - GHOST + ghost_order[:, 1, :], axis=1)
    sends = jnp.stack([sends_low, sends_high], axis=0).reshape(2, domains * GHOST)
    offsets = jnp.asarray(offset_table())
    options_count = offsets.shape[0]
    pick_scores = jax.random.randint(jax.random.fold_in(key, 103), (domains, ATOM_DEV, options_count), 0, 1 << 16) * options_count + jnp.arange(options_count, dtype=jnp.int32)
    picked = jnp.argsort(pick_scores, axis=2)[:, :, :NB]
    moves = offsets[picked]
    sites = site_of_slot[:, :, None]
    target = sites // 64 + moves[..., 0]
    new_y = (sites // 8 % 8 + moves[..., 1]) % 8
    new_z = (sites % 8 + moves[..., 2]) % 8
    column = new_y * 8 + new_z
    inside_site = jnp.clip(target, 0, layers - 1) * 64 + column
    inside = jnp.take_along_axis(slot_of_site, inside_site.reshape(domains, -1), axis=1).reshape(target.shape)
    domain_ids = jnp.arange(domains, dtype=jnp.int32)[:, None, None]
    lower_domain = (domain_ids - 1) % domains
    upper_domain = (domain_ids + 1) % domains
    low_offset = jnp.clip(target + ghost_layers, 0, ghost_layers - 1) * 64 + column
    high_offset = jnp.clip(target - layers, 0, ghost_layers - 1) * 64 + column
    from_lower = ATOM_DEV + ghost_rank[:, 1, :][lower_domain, low_offset]
    from_upper = ATOM_DEV + GHOST + ghost_rank[:, 0, :][upper_domain, high_offset]
    listed = jnp.where(target < 0, from_lower, jnp.where(target >= layers, from_upper, inside))
    lowest = jax.random.randint(jax.random.fold_in(key, 104), (domains, 1), NB // 4, NB + 1)
    spread = jax.random.randint(jax.random.fold_in(key, 105), (domains, ATOM_DEV), 0, NB + 1)
    counts = lowest + spread % (NB - lowest + 1)
    counts = counts.at[:, 0].set(NB)
    return (site_of_slot, sends.astype(jnp.int32), listed.reshape(ATOMS, NB).astype(jnp.int32), counts.reshape(ATOMS).astype(jnp.int32))


def draw_neighbours(key, part):
    return lattice_layout(key)[2]


def draw_neighbour_count(key, part):
    return lattice_layout(key)[3]


def draw_ghost_sends(key, part):
    return lattice_layout(key)[1]


def draw_positions(key, part):
    domains = ATOMS // ATOM_DEV
    layers = ATOM_DEV // 64
    sites = lattice_layout(key)[0]
    domain_ids = jnp.arange(domains, dtype=jnp.int32)[:, None]
    base_x = ((domain_ids * layers + sites // 64).astype(jnp.float32) + 0.5) * 1.25
    base_y = ((sites // 8 % 8).astype(jnp.float32) + 0.5) * 2.5
    base_z = ((sites % 8).astype(jnp.float32) + 0.5) * 2.5
    jitter_key = jax.random.fold_in(key, 201)
    jitter = jax.random.uniform(jitter_key, (3, domains, ATOM_DEV), jnp.float32, -0.3, 0.3)
    coords = jnp.stack([base_x, base_y, base_z], axis=0) + jitter
    return coords.reshape(3, ATOMS).astype(jnp.float32)


def draw_wave_index(key, part):
    scores = jax.random.randint(jax.random.fold_in(key, 301), (2048,), 0, 1 << 16) * 2048 + jnp.arange(2048, dtype=jnp.int32)
    chosen = jnp.argsort(scores)[:K].astype(jnp.int32)
    along_x = 1 + chosen // 256
    along_y = chosen // 16 % 16 - 8
    along_z = chosen % 16 - 8
    return jnp.stack([along_x, along_y, along_z], axis=0).astype(jnp.int32)


def with_ends(entries, stream_key, least, largest):
    index_at = [jax.random.randint(jax.random.fold_in(stream_key, axis), (), 0, length) for axis, length in enumerate(entries.shape)]
    longest = entries.shape.index(max(entries.shape))
    beside = index_at[:longest] + [(index_at[longest] + 1) % entries.shape[longest]] + index_at[longest + 1:]
    return entries.at[tuple(index_at)].set(least).at[tuple(beside)].set(largest)


def steps_of(stream_key, dims, shards, low, high):
    factor_of, own = 1.0, jax.random.fold_in(stream_key, 6)
    for dim, shards_of in shards:
        steps = jnp.exp(jax.random.uniform(jax.random.fold_in(own, dim), (shards_of,), jnp.float32, low / len(shards), high / len(shards)))
        factor_of = factor_of * jnp.repeat(steps, dims[dim] // shards_of).reshape([-1 if axis == dim else 1 for axis in range(len(dims))])
    return factor_of


def gaussian(key, dims, scale, reach, shards=(), kind=jnp.bfloat16):
    values = scale * jax.random.normal(key, dims, jnp.float32)
    if shards:
        values = values * steps_of(key, dims, shards, -0.22, 0.18)
    return jnp.clip(values, -reach, reach).astype(kind)


def setup_inputs(seed: int = 0, part: int = 0) -> dict:
    key_of = jax.random.split(jax.random.key(seed), 13)
    part_splits = jax.random.split(jax.random.fold_in(key_of[12], part), 13)
    features = gaussian(part_splits[0], (ATOMS, C), 1.0, 6.0, ((0, 16),))
    positions = draw_positions(jax.random.fold_in(jax.random.fold_in(key_of[12], part), 71), part)
    neighbours = draw_neighbours(jax.random.fold_in(jax.random.fold_in(key_of[12], part), 71), part)
    neighbour_count = draw_neighbour_count(jax.random.fold_in(jax.random.fold_in(key_of[12], part), 71), part)
    ghost_sends = draw_ghost_sends(jax.random.fold_in(jax.random.fold_in(key_of[12], part), 71), part)
    species = with_ends(jax.random.randint(part_splits[5], (ATOMS,), 0, SPEC), jax.random.fold_in(part_splits[5], 1), 0, SPEC - 1).astype(jnp.int32)
    wave_index = draw_wave_index(jax.random.fold_in(key_of[12], 71), part)
    force_ref = gaussian(part_splits[7], (3, ATOMS), 1.0, 6.0, ((1, 16),), jnp.float32)
    radial_weight = gaussian(key_of[8], (NRBF, C), NRBF ** -0.5, 1.5)
    mix_weight = gaussian(key_of[9], (C, C), C ** -0.5, 0.5)
    charge_weight = gaussian(key_of[10], (C, Q), C ** -0.5, 0.5)
    species_charge = gaussian(key_of[11], (SPEC, Q), 1.0, 4.0, (), jnp.float32)
    return {"features": features, "positions": positions, "neighbours": neighbours, "neighbour_count": neighbour_count, "ghost_sends": ghost_sends, "species": species, "wave_index": wave_index, "force_ref": force_ref, "radial_weight": radial_weight, "mix_weight": mix_weight, "charge_weight": charge_weight, "species_charge": species_charge}


cutoff_radius = 5.0
kernel_width = 1.0
basis_width = 0.5
box_side = 20.0
two_pi = 6.283185307179586
highest = lax.Precision.HIGHEST

def contract_first(left, right):
    return lax.dot_general(left, right, (((0,), (0,)), ((), ())), precision=highest, preferred_element_type=jnp.float32)

def contract_last(left, right):
    return lax.dot_general(left, right, (((1,), (1,)), ((), ())), precision=highest, preferred_element_type=jnp.float32)

def product(left, right):
    return jnp.dot(left, right, precision=highest, preferred_element_type=jnp.float32)

def edge_terms(own_coords, other_coords, live_count, box_lengths, basis_count):
    slots_count = other_coords.shape[2]
    displacement = other_coords - own_coords[:, :, None]
    displacement = displacement - box_lengths[:, None, None] * jnp.floor(displacement / box_lengths[:, None, None] + 0.5)
    distance = jnp.sqrt(lax.optimization_barrier(jnp.sum(displacement * displacement, axis=0)))
    is_live = (jnp.arange(slots_count, dtype=jnp.int32)[None, :] < live_count[:, None]).astype(jnp.float32)
    cutoff_fade = 0.5 * (jnp.cos(jnp.pi * jnp.minimum(distance, cutoff_radius) / cutoff_radius) + 1.0)
    centers = 0.5 + (cutoff_radius - 0.5) * jnp.arange(basis_count, dtype=jnp.float32) / (basis_count - 1)
    basis_rows = jnp.exp(-jnp.square((distance[..., None] - centers) / basis_width)).astype(jnp.bfloat16)
    return (basis_rows, is_live * cutoff_fade)

def silu_slope(value):
    sigmoid = jax.nn.sigmoid(value)
    return sigmoid * (1.0 + value * (1.0 - sigmoid))

def normalized(gradient):
    return gradient / jnp.sqrt(jnp.mean(gradient * gradient) + 1e-06)

def global_slots(neighbours, ghost_sends):
    domains = ATOMS // ATOM_DEV
    owner = (jnp.arange(ATOMS, dtype=jnp.int32) // ATOM_DEV)[:, None]
    lower = (owner - 1) % domains
    upper = (owner + 1) % domains
    low_slot = jnp.clip(neighbours - ATOM_DEV, 0, GHOST - 1)
    high_slot = jnp.clip(neighbours - ATOM_DEV - GHOST, 0, GHOST - 1)
    from_lower = lower * ATOM_DEV + ghost_sends[1][lower * GHOST + low_slot]
    from_upper = upper * ATOM_DEV + ghost_sends[0][upper * GHOST + high_slot]
    local = owner * ATOM_DEV + jnp.clip(neighbours, 0, ATOM_DEV - 1)
    return jnp.where(neighbours < ATOM_DEV, local, jnp.where(neighbours < ATOM_DEV + GHOST, from_lower, from_upper)).astype(jnp.int32)

def reference(features, positions, neighbours, neighbour_count, ghost_sends, species, wave_index, force_ref, radial_weight, mix_weight, charge_weight, species_charge):
    width = features.shape[1]
    slots_count = neighbours.shape[1]
    basis_count = radial_weight.shape[0]
    charges_width = charge_weight.shape[1]
    blocks = ATOMS // ATOM_DEV
    box_lengths = jnp.array([1.25 * ATOMS / 64, box_side, box_side], dtype=jnp.float32)
    slot_blocks = global_slots(neighbours, ghost_sends).reshape(blocks, ATOM_DEV, slots_count)
    own_blocks = positions.reshape(3, blocks, ATOM_DEV).transpose(1, 0, 2)
    count_blocks = neighbour_count.reshape(blocks, ATOM_DEV)

    def message_block(block_args):
        slot_rows, own_coords, live_count = block_args
        basis_rows, edge_weight = edge_terms(own_coords, positions[:, slot_rows], live_count, box_lengths, basis_count)
        filters = jnp.dot(basis_rows.reshape(-1, basis_count), radial_weight, preferred_element_type=jnp.float32)
        filters = filters.reshape(ATOM_DEV, slots_count, width)
        return lax.optimization_barrier(jnp.sum(edge_weight[..., None] * filters * features[slot_rows].astype(jnp.float32), axis=1))
    messages = lax.map(message_block, (slot_blocks, own_blocks, count_blocks)).reshape(ATOMS, width).astype(jnp.bfloat16)
    before = jnp.dot(messages, mix_weight, preferred_element_type=jnp.float32)
    hidden = (features.astype(jnp.float32) + jax.nn.silu(before)).astype(jnp.bfloat16)
    charges = jnp.dot(hidden, charge_weight, preferred_element_type=jnp.float32) + species_charge[species]
    wave_vectors = two_pi * wave_index.astype(jnp.float32) / box_lengths[:, None]
    damping = jnp.exp(-0.5 * kernel_width * kernel_width * lax.optimization_barrier(jnp.sum(wave_vectors * wave_vectors, axis=0))) / ATOMS
    charge_blocks = charges.reshape(blocks, ATOM_DEV, charges_width)

    def structure_block(block_args):
        own_coords, block_charges = block_args
        phases = contract_first(own_coords, wave_vectors)
        return jnp.concatenate([contract_first(jnp.cos(phases), block_charges), contract_first(jnp.sin(phases), block_charges)], axis=1)
    structure = lax.optimization_barrier(jnp.sum(lax.map(structure_block, (own_blocks, charge_blocks)), axis=0))
    coefficients = damping[:, None] * structure

    def force_block(block_args):
        own_coords, block_charges = block_args
        phases = contract_first(own_coords, wave_vectors)
        along_cos = contract_last(block_charges, coefficients[:, :charges_width])
        along_sin = contract_last(block_charges, coefficients[:, charges_width:])
        mixture = jnp.sin(phases) * along_cos - jnp.cos(phases) * along_sin
        return contract_last(wave_vectors, mixture)
    forces = lax.map(force_block, (own_blocks, charge_blocks)).transpose(1, 0, 2).reshape(3, ATOMS)
    errors = 2.0 * (forces - force_ref)
    error_blocks = errors.reshape(3, blocks, ATOM_DEV).transpose(1, 0, 2)

    def gradient_block(block_args):
        own_coords, block_charges, block_errors = block_args
        phases = contract_first(own_coords, wave_vectors)
        cosines = jnp.cos(phases)
        sines = jnp.sin(phases)
        slopes = contract_first(block_errors, wave_vectors)
        direct = product(slopes * sines, coefficients[:, :charges_width]) - product(slopes * cosines, coefficients[:, charges_width:])
        wave_term = jnp.concatenate([contract_first(slopes * sines, block_charges), -contract_first(slopes * cosines, block_charges)], axis=1)
        return (direct, wave_term)
    direct, wave_terms = lax.map(gradient_block, (own_blocks, charge_blocks, error_blocks))
    gradient_waves = lax.optimization_barrier(jnp.sum(wave_terms, axis=0))
    back_waves = damping[:, None] * gradient_waves

    def indirect_block(own_coords):
        phases = contract_first(own_coords, wave_vectors)
        return product(jnp.cos(phases), back_waves[:, :charges_width]) + product(jnp.sin(phases), back_waves[:, charges_width:])
    indirect = lax.map(indirect_block, own_blocks)
    charge_grad = direct.reshape(ATOMS, charges_width) + indirect.reshape(ATOMS, charges_width)
    charge_rounded = charge_grad.astype(jnp.bfloat16)
    charge_sum = contract_first(hidden, charge_rounded)
    one_hot = (species[:, None] == jnp.arange(SPEC, dtype=jnp.int32)[None, :]).astype(jnp.float32)
    species_sum = contract_first(one_hot, charge_grad)
    upstream = contract_last(charge_rounded, charge_weight)
    before_grad = (upstream * silu_slope(before)).astype(jnp.bfloat16)
    mix_sum = contract_first(messages, before_grad)
    message_grad = contract_last(before_grad, mix_weight).astype(jnp.bfloat16)

    def radial_block(running, block_args):
        slot_rows, own_coords, live_count, rows_grad = block_args
        basis_rows, edge_weight = edge_terms(own_coords, positions[:, slot_rows], live_count, box_lengths, basis_count)
        edge_term = (edge_weight[..., None] * rows_grad.astype(jnp.float32)[:, None, :] * features[slot_rows].astype(jnp.float32)).astype(jnp.bfloat16)
        return (running + contract_first(basis_rows.reshape(-1, basis_count), edge_term.reshape(-1, width)), None)
    radial_sum, _ = lax.scan(radial_block, jnp.zeros((basis_count, width), jnp.float32), (slot_blocks, own_blocks, count_blocks, message_grad.reshape(blocks, ATOM_DEV, width)))
    return (forces, normalized(radial_sum), normalized(mix_sum), normalized(charge_sum), normalized(species_sum))
```

```python
import math

import jax
import jax.numpy as jnp
import numpy as np
from jax import lax
from jax.experimental import pallas as pl
from jax.experimental.pallas import tpu as pltpu
from jax.sharding import PartitionSpec as P

cutoff_radius = 5.0
kernel_width = 1.0
basis_width = 0.5
box_side = 20.0
two_pi = 6.283185307179586
highest = lax.Precision.HIGHEST
f32 = jnp.float32
bf16 = jnp.bfloat16
vmem_limit = 56 * 1024 * 1024


def fitted(function, degrees, reach):
    nodes = reach * np.cos((np.arange(400) + 0.5) * np.pi / 400)
    powers = np.stack([nodes**d for d in degrees], axis=1)
    return [float(c) for c in np.linalg.lstsq(powers, function(nodes), rcond=None)[0]]


sine_terms = fitted(lambda x: np.sin(np.pi * x), (1, 3, 5, 7, 9), 0.5)
cosine_terms = fitted(lambda x: np.cos(np.pi * x), (0, 2, 4, 6, 8), 0.5)


def horner(terms, square):
    value = terms[-1]
    for term in terms[-2::-1]:
        value = value * square + term
    return value


def matmul(left, right, precision=None):
    return lax.dot_general(
        left, right, (((1,), (0,)), ((), ())), precision=precision, preferred_element_type=f32
    )


def matmul_nt(left, right, precision=None):
    return lax.dot_general(
        left, right, (((1,), (1,)), ((), ())), precision=precision, preferred_element_type=f32
    )


def turned(value):
    return jnp.transpose(value.astype(f32)).astype(value.dtype)


def sigmoid(value):
    return 1.0 / (1.0 + jnp.exp(-value))


def edge_kernel(
    where_ref,
    feat_ref,
    low_ref,
    up_ref,
    small_ref,
    slots_ref,
    count_ref,
    species_ref,
    radial_ref,
    mix_ref,
    charge_ref,
    offset_ref,
    filtered_ref,
    messages_ref,
    before_ref,
    hidden_ref,
    charges_ref,
    words_ref,
    coords_ref,
    table_ref,
    pair_ref,
    *,
    box_x,
):
    atoms, width = feat_ref.shape
    slots = slots_ref.shape[1]
    basis_count = radial_ref.shape[0]
    low, own, up = where_ref[0], where_ref[1], where_ref[2]
    ghosts = atoms
    entries = atoms + 2 * ghosts
    own_rows = small_ref[own]
    site = lax.broadcasted_iota(jnp.int32, (atoms, ghosts), 0)

    own_feat = turned(feat_ref[...])
    table_ref[:, 0:atoms] = own_feat
    coords_ref[0:atoms, :] = jnp.transpose(own_rows)
    for place, ref, side, row in ((0, low_ref, low, 7), (1, up_ref, up, 6)):
        rows = small_ref[side]
        chosen = (site.astype(f32) == rows[row : row + 1, :]).astype(bf16)
        first = atoms + place * ghosts
        table_ref[:, first : first + ghosts] = matmul(turned(ref[...]), chosen).astype(bf16)
        part = rows.astype(bf16)
        rest = rows - part.astype(f32)
        second = rest.astype(bf16)
        third = (rest - second.astype(f32)).astype(bf16)
        moved = matmul(part, chosen) + (matmul(second, chosen) + matmul(third, chosen))
        coords_ref[first : first + ghosts, :] = jnp.transpose(moved)

    listed = jnp.transpose(slots_ref[...])
    live = lax.broadcasted_iota(jnp.int32, (slots, atoms), 0) < count_ref[...]
    word_of = jnp.where(live, listed >> 5, -1)
    bit = jnp.left_shift(jnp.ones_like(listed), listed & 31)
    for word in range(entries // 32):
        value = jnp.where(word_of == word, bit, 0)
        rows = slots
        while rows > 1:
            rows //= 2
            value = value[:rows] | value[rows:]
        words_ref[word : word + 1, :] = value

    centers = [
        0.5 + (cutoff_radius - 0.5) * float(b) / (basis_count - 1) for b in range(basis_count)
    ]
    scale = -math.log2(math.e) / (basis_width * basis_width)
    own_x, own_y, own_z = own_rows[0:1, :], own_rows[1:2, :], own_rows[2:3, :]
    step = 32

    def block(index, carry):
        first = pl.multiple_of(index * step, step)
        coords = coords_ref[pl.ds(first, step), :]
        total = jnp.zeros((step, atoms), f32)
        for axis, (mine, length) in enumerate(
            ((own_x, box_x), (own_y, box_side), (own_z, box_side))
        ):
            away = coords[:, axis : axis + 1] - mine
            away = away - length * jnp.floor(away * (1.0 / length) + 0.5)
            total = total + away * away
        distance = jnp.sqrt(total)
        word = words_ref[pl.ds(index, 1), :]
        sublane = lax.broadcasted_iota(jnp.int32, (step, atoms), 0)
        is_live = (jnp.right_shift(jnp.broadcast_to(word, (step, atoms)), sublane) & 1) != 0
        half = jnp.minimum(distance, cutoff_radius) * (1.0 / cutoff_radius) - 0.5
        fade = 0.5 - 0.5 * (half * horner(sine_terms, half * half))
        weight = jnp.where(is_live, fade, 0.0)
        for b in range(basis_count):
            offset = distance - centers[b]
            basis = jnp.exp2(offset * offset * scale).astype(bf16).astype(f32)
            pair_ref[b, pl.ds(first, step), :] = (weight * basis).astype(bf16)
        return carry

    lax.fori_loop(0, entries // step, block, 0)

    radial = jnp.transpose(radial_ref[...].astype(f32))
    messages = jnp.zeros((width, atoms), f32)
    for b in range(basis_count):
        filtered = matmul(table_ref[...], pair_ref[b])
        filtered_ref[b] = filtered
        messages = messages + radial[:, b : b + 1] * filtered
    messages = messages.astype(bf16)
    messages_ref[...] = messages
    before = matmul(turned(mix_ref[...]), messages)
    before_ref[...] = before
    hidden = (own_feat.astype(f32) + before * sigmoid(before)).astype(bf16)
    hidden_ref[...] = hidden
    kinds = offset_ref.shape[0]
    one_hot = (
        lax.broadcasted_iota(jnp.int32, (kinds, atoms), 0) == species_ref[...]
    ).astype(f32)
    charges = matmul(turned(charge_ref[...]), hidden) + matmul(
        jnp.transpose(offset_ref[...]), one_hot, highest
    )
    rounded = charges.astype(bf16)
    for copy in range(charges_ref.shape[0]):
        charges_ref[copy] = rounded


def wave_rows(wave_ref, first, count, box_x, total_atoms):
    index = wave_ref[:, pl.ds(first, count)].astype(f32)
    scales = (two_pi / box_x, two_pi / box_side, two_pi / box_side)
    waves = [index[a : a + 1, :] * scales[a] for a in range(3)]
    squares = waves[0] * waves[0] + waves[1] * waves[1] + waves[2] * waves[2]
    damping = jnp.exp(-0.5 * kernel_width * kernel_width * squares) * (1.0 / total_atoms)
    return index, waves, damping


def structure_kernel(
    where_ref,
    small_ref,
    charges_ref,
    wave_ref,
    cos_ref,
    sin_ref,
    field_ref,
    forces_ref,
    *,
    box_x,
):
    domains, charge_count, atoms = charges_ref.shape
    share = cos_ref.shape[1]
    group = forces_ref.shape[0]
    first = pl.multiple_of(where_ref[3] * share, share)
    index, waves, damping = wave_rows(wave_ref, first, share, box_x, domains * atoms)
    columns = jnp.transpose(jnp.concatenate([index, jnp.zeros((5, share), f32)], axis=0))
    lengths = (box_x, box_side, box_side)

    def gather(d, carry):
        rows = small_ref[d]
        turns = jnp.zeros((share, atoms), f32)
        for a in range(3):
            turns = turns + columns[:, a : a + 1] * (rows[a : a + 1, :] * (1.0 / lengths[a]))
        turns = turns - jnp.floor(turns + 0.5)
        square = turns * turns
        half_sine = turns * horner(sine_terms, square)
        half_cosine = horner(cosine_terms, square)
        cosine = (1.0 - 2.0 * half_sine * half_sine).astype(bf16)
        sine = (2.0 * half_sine * half_cosine).astype(bf16)
        cos_ref[d] = cosine
        sin_ref[d] = sine
        charges = charges_ref[d]
        return carry[0] + matmul_nt(charges, cosine), carry[1] + matmul_nt(charges, sine)

    zero = jnp.zeros((charge_count, share), f32)
    along_cos, along_sin = lax.fori_loop(0, domains, gather, (zero, zero))
    along_cos = along_cos * damping
    along_sin = along_sin * damping
    to_sine = jnp.concatenate([along_cos * waves[a] for a in range(3)], axis=0).astype(bf16)
    to_cosine = jnp.concatenate([-along_sin * waves[a] for a in range(3)], axis=0).astype(bf16)
    quad_first = where_ref[4]

    def force(d, carry):
        field = matmul(to_sine, sin_ref[d]) + matmul(to_cosine, cos_ref[d])
        charges = charges_ref[d].astype(f32)
        inside = jnp.logical_and(d >= quad_first, d < quad_first + group)

        @pl.when(inside)
        def _():
            field_ref[d - quad_first] = field

        for a in range(3):
            row = jnp.sum(
                field[a * charge_count : (a + 1) * charge_count, :] * charges,
                axis=0,
                keepdims=True,
            )
            for copy in range(group):
                forces_ref[copy, a, pl.ds(d, 1), :] = row
        return carry

    lax.fori_loop(0, domains, force, 0)


def gradient_kernel(
    where_ref,
    small_ref,
    charges_ref,
    wave_ref,
    cos_ref,
    sin_ref,
    field_ref,
    parts_ref,
    forces_ref,
    grad_ref,
    total_ref,
    *,
    box_x,
):
    domains, charge_count, atoms = charges_ref.shape
    share = cos_ref.shape[1]
    group = parts_ref.shape[0]
    first = pl.multiple_of(where_ref[3] * share, share)
    _, waves, damping = wave_rows(wave_ref, first, share, box_x, domains * atoms)
    total = parts_ref[0]
    for part in range(1, group):
        total = total + parts_ref[part]
    total_ref[...] = total
    own = where_ref[1]
    for a in range(3):
        forces_ref[a : a + 1, :] = total_ref[a, pl.ds(own, 1), :]

    def errors_of(d):
        rows = small_ref[d]
        return [2.0 * (total_ref[a, pl.ds(d, 1), :] - rows[3 + a : 4 + a, :]) for a in range(3)]

    def gather(d, carry):
        charges = charges_ref[d].astype(f32)
        errors = errors_of(d)
        scaled = jnp.concatenate([errors[a] * charges for a in range(3)], axis=0).astype(bf16)
        return carry[0] + matmul_nt(scaled, sin_ref[d]), carry[1] + matmul_nt(scaled, cos_ref[d])

    zero = jnp.zeros((3 * charge_count, share), f32)
    by_sine, by_cosine = lax.fori_loop(0, domains, gather, (zero, zero))

    def along(value):
        return sum(
            waves[a] * value[a * charge_count : (a + 1) * charge_count, :] for a in range(3)
        )

    back_cos = (damping * along(by_sine)).astype(bf16)
    back_sin = (-damping * along(by_cosine)).astype(bf16)
    quad_first = where_ref[4]
    for member in range(group):
        d = quad_first + member
        errors = errors_of(d)
        grad = matmul(back_cos, cos_ref[d]) + matmul(back_sin, sin_ref[d])
        for a in range(3):
            grad = grad + errors[a] * field_ref[
                member, a * charge_count : (a + 1) * charge_count, :
            ]
        grad_ref[member] = grad


def weights_kernel(
    parts_ref,
    filtered_ref,
    messages_ref,
    before_ref,
    hidden_ref,
    species_ref,
    mix_ref,
    charge_ref,
    packed_ref,
    *,
    kinds,
):
    group, charge_count, atoms = parts_ref.shape
    basis_count, width, _ = filtered_ref.shape
    grad = parts_ref[0]
    for part in range(1, group):
        grad = grad + parts_ref[part]
    rounded = grad.astype(bf16)
    before = before_ref[...]
    gate = sigmoid(before)
    upstream = matmul(charge_ref[...], rounded)
    before_grad = (upstream * (gate * (1.0 + before * (1.0 - gate)))).astype(bf16)
    message_grad = matmul(mix_ref[...], before_grad).astype(bf16).astype(f32)
    packed_ref[...] = jnp.zeros_like(packed_ref)
    columns = [
        jnp.sum(message_grad * filtered_ref[b], axis=1, keepdims=True) for b in range(basis_count)
    ]
    radial = jnp.concatenate(columns, axis=1)
    row = 0
    packed_ref[row : row + basis_count, :] = jnp.transpose(radial)
    row += basis_count
    packed_ref[row : row + width, :] = matmul_nt(messages_ref[...], before_grad)
    row += width
    packed_ref[row : row + charge_count, :] = matmul_nt(rounded, hidden_ref[...])
    row += charge_count
    one_hot = (
        lax.broadcasted_iota(jnp.int32, (kinds, atoms), 0) == species_ref[...]
    ).astype(f32)
    packed_ref[row : row + kinds, 0:charge_count] = matmul_nt(one_hot, grad, highest)


def step_kernel(total_ref, radial_ref, mix_ref, charge_ref, species_ref):
    basis_count, width = radial_ref.shape
    charge_count = charge_ref.shape[1]
    kinds = species_ref.shape[0]

    def normalized(gradient):
        mean = jnp.sum(gradient * gradient, keepdims=True) * (1.0 / gradient.size)
        return gradient * lax.rsqrt(mean + 1e-06)

    row = 0
    radial_ref[...] = normalized(total_ref[row : row + basis_count, :])
    row += basis_count
    mix_ref[...] = normalized(total_ref[row : row + width, :])
    row += width
    charge_ref[...] = normalized(jnp.transpose(total_ref[row : row + charge_count, :]))
    row += charge_count
    species_ref[...] = normalized(total_ref[row : row + kinds, 0:charge_count])


def in_smem():
    return pl.BlockSpec(memory_space=pltpu.SMEM)


def in_vmem(count):
    return [pl.BlockSpec(memory_space=pltpu.VMEM) for _ in range(count)]


def shaped(*dims, kind=f32):
    return jax.ShapeDtypeStruct(dims, kind)


def on_device(
    features,
    positions,
    neighbours,
    neighbour_count,
    ghost_sends,
    species,
    wave_index,
    force_ref,
    radial_weight,
    mix_weight,
    charge_weight,
    species_charge,
):
    atoms, width = features.shape
    basis_count = radial_weight.shape[0]
    charge_count = charge_weight.shape[1]
    kinds = species_charge.shape[0]
    wave_count = wave_index.shape[1]
    domains = lax.axis_size("dom")
    box_x = 1.25 * (atoms * domains) / 64
    group = 4 if domains % 4 == 0 else 1
    share = wave_count // group
    quads = [[group * q + m for m in range(group)] for q in range(domains // group)]
    entries = atoms + 2 * ghost_sends.shape[1]
    params = pltpu.CompilerParams(vmem_limit_bytes=vmem_limit)

    me = lax.axis_index("dom")
    where = jnp.stack(
        [
            (me + domains - 1) % domains,
            me,
            (me + 1) % domains,
            me % group,
            me // group * group,
        ]
    ).astype(jnp.int32)
    small = jnp.concatenate([positions, force_ref, ghost_sends.astype(f32)], axis=0)
    upward = [(i, (i + 1) % domains) for i in range(domains)]
    downward = [(j, i) for i, j in upward]
    from_low = lax.ppermute(features, "dom", upward)
    from_up = lax.ppermute(features, "dom", downward)
    small_all = lax.all_to_all(
        jnp.broadcast_to(small[None], (domains,) + small.shape), "dom", 0, 0
    )
    species_row = species[None, :]

    filtered, messages, before, hidden, charges = pl.pallas_call(
        lambda *refs: edge_kernel(*refs, box_x=box_x),
        out_shape=(
            shaped(basis_count, width, atoms),
            shaped(width, atoms, kind=bf16),
            shaped(width, atoms),
            shaped(width, atoms, kind=bf16),
            shaped(domains, charge_count, atoms, kind=bf16),
        ),
        in_specs=[in_smem()] + in_vmem(11),
        out_specs=tuple(in_vmem(5)),
        scratch_shapes=[
            pltpu.VMEM((entries // 32, atoms), jnp.int32),
            pltpu.VMEM((entries, small.shape[0]), f32),
            pltpu.VMEM((width, entries), bf16),
            pltpu.VMEM((basis_count, entries, atoms), bf16),
        ],
        compiler_params=params,
        name="edges",
    )(
        where,
        features,
        from_low,
        from_up,
        small_all,
        neighbours,
        neighbour_count[None, :],
        species_row,
        radial_weight,
        mix_weight,
        charge_weight,
        species_charge,
    )
    charges_all = lax.all_to_all(charges, "dom", 0, 0)

    cosines, sines, field, force_parts = pl.pallas_call(
        lambda *refs: structure_kernel(*refs, box_x=box_x),
        out_shape=(
            shaped(domains, share, atoms, kind=bf16),
            shaped(domains, share, atoms, kind=bf16),
            shaped(group, 3 * charge_count, atoms),
            shaped(group, 3, domains, atoms),
        ),
        in_specs=[in_smem()] + in_vmem(3),
        out_specs=tuple(in_vmem(4)),
        compiler_params=params,
        name="structure",
    )(where, small_all, charges_all, wave_index)
    force_parts = lax.all_to_all(force_parts, "dom", 0, 0, axis_index_groups=quads)

    forces, grad_parts = pl.pallas_call(
        lambda *refs: gradient_kernel(*refs, box_x=box_x),
        out_shape=(shaped(3, atoms), shaped(group, charge_count, atoms)),
        in_specs=[in_smem()] + in_vmem(7),
        out_specs=tuple(in_vmem(2)),
        scratch_shapes=[pltpu.VMEM((3, domains, atoms), f32)],
        compiler_params=params,
        name="gradient",
    )(where, small_all, charges_all, wave_index, cosines, sines, field, force_parts)
    grad_parts = lax.all_to_all(grad_parts, "dom", 0, 0, axis_index_groups=quads)

    rows = basis_count + width + charge_count + kinds
    rows = -(-rows // (8 * domains)) * (8 * domains)
    packed = pl.pallas_call(
        lambda *refs: weights_kernel(*refs, kinds=kinds),
        out_shape=shaped(rows, width),
        in_specs=in_vmem(8),
        out_specs=in_vmem(1)[0],
        compiler_params=params,
        name="weights",
    )(
        grad_parts,
        filtered,
        messages,
        before,
        hidden,
        species_row,
        mix_weight,
        charge_weight,
    )
    pieces = lax.all_to_all(packed.reshape(domains, rows // domains, width), "dom", 0, 0)
    piece = jnp.sum(pieces, axis=0)
    total = lax.all_to_all(jnp.broadcast_to(piece[None], pieces.shape), "dom", 0, 0)
    steps = pl.pallas_call(
        step_kernel,
        out_shape=(
            shaped(basis_count, width),
            shaped(width, width),
            shaped(width, charge_count),
            shaped(kinds, charge_count),
        ),
        in_specs=in_vmem(1),
        out_specs=tuple(in_vmem(4)),
        compiler_params=params,
        name="steps",
    )(total.reshape(rows, width))
    return (forces, *steps)


def solution(mesh):
    placed = (
        P(("cell", "dom"), None),
        P(None, ("cell", "dom")),
        P(("cell", "dom"), None),
        P(("cell", "dom")),
        P(None, ("cell", "dom")),
        P(("cell", "dom")),
        P(),
        P(None, ("cell", "dom")),
        P(),
        P(),
        P(),
        P(),
    )
    return jax.shard_map(
        on_device,
        mesh=mesh,
        in_specs=placed,
        out_specs=(
            P(None, ("cell", "dom")),
            P("cell", None),
            P("cell", None),
            P("cell", None),
            P("cell", None),
        ),
        check_vma=False,
    )
```

```python
import math

import jax
import jax.numpy as jnp
import numpy as np
from jax import lax
from jax.experimental import pallas as pl
from jax.experimental.pallas import tpu as pltpu
from jax.sharding import PartitionSpec as P

cutoff_radius = 5.0
kernel_width = 1.0
basis_width = 0.5
box_side = 20.0
two_pi = 6.283185307179586
highest = lax.Precision.HIGHEST
f32 = jnp.float32
bf16 = jnp.bfloat16
spare_vmem = 8 * 1024 * 1024


def fitted(function, degrees, reach):
    nodes = reach * np.cos((np.arange(400) + 0.5) * np.pi / 400)
    powers = np.stack([nodes**d for d in degrees], axis=1)
    return [float(c) for c in np.linalg.lstsq(powers, function(nodes), rcond=None)[0]]


sine_terms = fitted(lambda x: np.sin(np.pi * x), (1, 3, 5, 7, 9), 0.5)
cosine_terms = fitted(lambda x: np.cos(np.pi * x), (0, 2, 4, 6, 8), 0.5)


def horner(terms, square):
    value = terms[-1]
    for term in terms[-2::-1]:
        value = value * square + term
    return value


def matmul(left, right, precision=None):
    return lax.dot_general(
        left, right, (((1,), (0,)), ((), ())), precision=precision, preferred_element_type=f32
    )


def matmul_nt(left, right, precision=None):
    return lax.dot_general(
        left, right, (((1,), (1,)), ((), ())), precision=precision, preferred_element_type=f32
    )


def turned(value):
    return jnp.transpose(value.astype(f32)).astype(value.dtype)


def sigmoid(value):
    return 1.0 / (1.0 + jnp.exp(-value))


def edge_kernel(
    where_ref,
    feat_ref,
    low_ref,
    up_ref,
    small_ref,
    slots_ref,
    count_ref,
    species_ref,
    radial_ref,
    mix_ref,
    charge_ref,
    offset_ref,
    filtered_ref,
    messages_ref,
    before_ref,
    hidden_ref,
    charges_ref,
    words_ref,
    coords_ref,
    table_ref,
    pair_ref,
    *,
    box_x,
):
    atoms, width = feat_ref.shape
    slots = slots_ref.shape[0]
    basis_count = radial_ref.shape[0]
    low, own, up = where_ref[0], where_ref[1], where_ref[2]
    ghosts = atoms
    entries = atoms + 2 * ghosts
    own_rows = small_ref[own]
    site = lax.broadcasted_iota(jnp.int32, (atoms, ghosts), 0)

    own_feat = turned(feat_ref[...])
    table_ref[:, 0:atoms] = own_feat
    coords_ref[0:atoms, :] = jnp.transpose(own_rows)
    for place, ref, side, row in ((0, low_ref, low, 7), (1, up_ref, up, 6)):
        rows = small_ref[side]
        chosen = (site.astype(f32) == rows[row : row + 1, :]).astype(bf16)
        first = atoms + place * ghosts
        table_ref[:, first : first + ghosts] = matmul(turned(ref[...]), chosen).astype(bf16)
        part = rows.astype(bf16)
        rest = rows - part.astype(f32)
        second = rest.astype(bf16)
        third = (rest - second.astype(f32)).astype(bf16)
        moved = matmul(part, chosen) + (matmul(second, chosen) + matmul(third, chosen))
        coords_ref[first : first + ghosts, :] = jnp.transpose(moved)

    listed = slots_ref[...]
    live = lax.broadcasted_iota(jnp.int32, (slots, atoms), 0) < count_ref[...]
    word_of = jnp.where(live, listed >> 5, -1)
    bit = jnp.left_shift(jnp.ones_like(listed), listed & 31)
    for word in range(entries // 32):
        value = jnp.where(word_of == word, bit, 0)
        rows = slots
        while rows > 1:
            rows //= 2
            value = value[:rows] | value[rows:]
        words_ref[word : word + 1, :] = value

    centers = [
        0.5 + (cutoff_radius - 0.5) * float(b) / (basis_count - 1) for b in range(basis_count)
    ]
    scale = -math.log2(math.e) / (basis_width * basis_width)
    own_x, own_y, own_z = own_rows[0:1, :], own_rows[1:2, :], own_rows[2:3, :]
    step = 32

    def block(index, carry):
        first = pl.multiple_of(index * step, step)
        coords = coords_ref[pl.ds(first, step), :]
        total = jnp.zeros((step, atoms), f32)
        for axis, (mine, length) in enumerate(
            ((own_x, box_x), (own_y, box_side), (own_z, box_side))
        ):
            away = coords[:, axis : axis + 1] - mine
            away = away - length * jnp.floor(away * (1.0 / length) + 0.5)
            total = total + away * away
        distance = jnp.sqrt(total)
        word = words_ref[pl.ds(index, 1), :]
        sublane = lax.broadcasted_iota(jnp.int32, (step, atoms), 0)
        is_live = (jnp.right_shift(jnp.broadcast_to(word, (step, atoms)), sublane) & 1) != 0
        half = jnp.minimum(distance, cutoff_radius) * (1.0 / cutoff_radius) - 0.5
        fade = 0.5 - 0.5 * (half * horner(sine_terms, half * half))
        weight = jnp.where(is_live, fade, 0.0)
        for b in range(basis_count):
            offset = distance - centers[b]
            basis = jnp.exp2(offset * offset * scale).astype(bf16).astype(f32)
            pair_ref[b, pl.ds(first, step), :] = (weight * basis).astype(bf16)
        return carry

    lax.fori_loop(0, entries // step, block, 0)

    radial = jnp.transpose(radial_ref[...].astype(f32))
    messages = jnp.zeros((width, atoms), f32)
    for b in range(basis_count):
        filtered = matmul(table_ref[...], pair_ref[b])
        filtered_ref[b] = filtered
        messages = messages + radial[:, b : b + 1] * filtered
    messages_ref[...] = messages
    before = matmul(jnp.transpose(mix_ref[...].astype(f32)), messages, highest)
    before_ref[...] = before
    hidden = (own_feat.astype(f32) + before * sigmoid(before)).astype(bf16)
    hidden_ref[...] = hidden
    kinds = offset_ref.shape[0]
    one_hot = (
        lax.broadcasted_iota(jnp.int32, (kinds, atoms), 0) == species_ref[...]
    ).astype(f32)
    charges = matmul(charge_ref[...], hidden) + matmul(
        jnp.transpose(offset_ref[...]), one_hot, highest
    )
    rounded = charges.astype(bf16)
    for copy in range(charges_ref.shape[0]):
        charges_ref[copy] = rounded


def wave_rows(wave_ref, first, count, box_x, total_atoms):
    index = wave_ref[:, pl.ds(first, count)].astype(f32)
    scales = (two_pi / box_x, two_pi / box_side, two_pi / box_side)
    waves = [index[a : a + 1, :] * scales[a] for a in range(3)]
    squares = waves[0] * waves[0] + waves[1] * waves[1] + waves[2] * waves[2]
    damping = jnp.exp(-0.5 * kernel_width * kernel_width * squares) * (1.0 / total_atoms)
    return index, waves, damping


def pieces_of(value):
    first = value.astype(bf16).astype(f32)
    rest = value - first
    second = rest.astype(bf16).astype(f32)
    return first, second, rest - second


def phase_kernel(where_ref, small_ref, wave_ref, waves_ref, *, box_x):
    domains, _, atoms = small_ref.shape
    share = waves_ref.shape[0] // 2
    first = pl.multiple_of(where_ref[3] * share, share)
    index = wave_ref[:, pl.ds(first, share)].astype(f32)
    columns = jnp.transpose(
        jnp.concatenate([index] * 3 + [jnp.zeros((7, share), f32)], axis=0)
    ).astype(bf16)
    lengths = (box_x, box_side, box_side)
    shift = 12582912.0

    def block(d, carry):
        rows = small_ref[d]
        turns = jnp.concatenate(
            [rows[a : a + 1, :] * (1.0 / lengths[a]) for a in range(3)], axis=0
        )
        parts = jnp.concatenate(pieces_of(turns) + (jnp.zeros((7, atoms), f32),), axis=0)
        turns = matmul(columns, parts.astype(bf16))
        turns = turns - ((turns + shift) - shift)
        square = turns * turns
        half_sine = turns * horner(sine_terms, square)
        half_cosine = horner(cosine_terms, square)
        place = pl.ds(pl.multiple_of(d * atoms, atoms), atoms)
        waves_ref[0:share, place] = (2.0 * half_sine * half_cosine).astype(bf16)
        waves_ref[share : 2 * share, place] = (1.0 - 2.0 * half_sine * half_sine).astype(bf16)
        return carry

    lax.fori_loop(0, domains, block, 0, unroll=4)


def structure_kernel(
    where_ref,
    charges_ref,
    wave_ref,
    waves_ref,
    weights_ref,
    forces_ref,
    rows_ref,
    *,
    box_x,
):
    domains, charge_count, atoms = charges_ref.shape
    share = waves_ref.shape[0] // 2
    group = forces_ref.shape[0]
    first = pl.multiple_of(where_ref[3] * share, share)
    _, waves, damping = wave_rows(wave_ref, first, share, box_x, domains * atoms)
    structure = jnp.zeros((charge_count, 2 * share), f32)
    for d in range(domains):
        structure = structure + matmul_nt(
            charges_ref[d], waves_ref[:, d * atoms : (d + 1) * atoms]
        )
    along_sin = structure[:, :share] * damping
    along_cos = structure[:, share:] * damping
    to_sine = jnp.concatenate([along_cos * waves[a] for a in range(3)], axis=0)
    to_cosine = jnp.concatenate([-along_sin * waves[a] for a in range(3)], axis=0)
    weights = jnp.concatenate([to_sine, to_cosine], axis=1)
    weights_ref[...] = weights
    weights = weights.astype(bf16)
    for d in range(domains):
        field = matmul(weights, waves_ref[:, d * atoms : (d + 1) * atoms])
        charges = charges_ref[d].astype(f32)
        for a in range(3):
            rows_ref[a, d : d + 1, :] = jnp.sum(
                field[a * charge_count : (a + 1) * charge_count, :] * charges,
                axis=0,
                keepdims=True,
            )
    for copy in range(group):
        forces_ref[copy] = rows_ref[...]


def gradient_kernel(
    where_ref,
    small_ref,
    charges_ref,
    wave_ref,
    waves_ref,
    weights_ref,
    parts_ref,
    forces_ref,
    grad_ref,
    total_ref,
    *,
    box_x,
):
    domains, charge_count, atoms = charges_ref.shape
    share = waves_ref.shape[0] // 2
    group = parts_ref.shape[0]
    first = pl.multiple_of(where_ref[3] * share, share)
    _, waves, damping = wave_rows(wave_ref, first, share, box_x, domains * atoms)
    total = parts_ref[0]
    for part in range(1, group):
        total = total + parts_ref[part]
    total_ref[...] = total
    own = where_ref[1]
    for a in range(3):
        forces_ref[a : a + 1, :] = total_ref[a, pl.ds(own, 1), :]

    def errors_of(d):
        rows = small_ref[d]
        return [2.0 * (total_ref[a, pl.ds(d, 1), :] - rows[3 + a : 4 + a, :]) for a in range(3)]

    summed = jnp.zeros((3 * charge_count, 2 * share), f32)
    for d in range(domains):
        charges = charges_ref[d].astype(f32)
        errors = errors_of(d)
        scaled = jnp.concatenate([errors[a] * charges for a in range(3)], axis=0).astype(bf16)
        summed = summed + matmul_nt(scaled, waves_ref[:, d * atoms : (d + 1) * atoms])

    def along(value):
        return sum(
            waves[a] * value[a * charge_count : (a + 1) * charge_count, :] for a in range(3)
        )

    back_cos = damping * along(summed[:, :share])
    back_sin = -damping * along(summed[:, share:])
    back = jnp.concatenate([back_sin, back_cos], axis=1)
    back_high = back.astype(bf16)
    back_low = (back - back_high.astype(f32)).astype(bf16)
    weights = weights_ref[...]
    weights_high = weights.astype(bf16)
    weights_low = (weights - weights_high.astype(f32)).astype(bf16)
    quad_first = where_ref[4]
    for member in range(group):
        d = quad_first + member
        errors = errors_of(d)
        block = waves_ref[:, pl.ds(pl.multiple_of(d * atoms, atoms), atoms)]
        grad = matmul(back_high, block) + matmul(back_low, block)
        field = matmul(weights_high, block) + matmul(weights_low, block)
        for a in range(3):
            grad = grad + errors[a] * field[a * charge_count : (a + 1) * charge_count, :]
        grad_ref[member] = grad.astype(grad_ref.dtype)


def weights_kernel(
    parts_ref,
    filtered_ref,
    messages_ref,
    before_ref,
    hidden_ref,
    species_ref,
    mix_ref,
    charge_ref,
    packed_ref,
    *,
    kinds,
):
    group, charge_count, atoms = parts_ref.shape
    basis_count, width, _ = filtered_ref.shape
    grad = parts_ref[0].astype(f32)
    for part in range(1, group):
        grad = grad + parts_ref[part].astype(f32)
    before = before_ref[...]
    gate = sigmoid(before)
    upstream = matmul(jnp.transpose(charge_ref[...].astype(f32)), grad, highest)
    before_grad = upstream * (gate * (1.0 + before * (1.0 - gate)))
    message_grad = matmul(mix_ref[...].astype(f32), before_grad, highest)
    columns = [
        jnp.sum(message_grad * filtered_ref[b], axis=1, keepdims=True) for b in range(basis_count)
    ]
    radial = jnp.concatenate(columns, axis=1)
    row = 0
    packed_ref[row : row + basis_count, :] = jnp.transpose(radial)
    row += basis_count
    packed_ref[row : row + width, :] = matmul_nt(messages_ref[...], before_grad, highest)
    row += width
    packed_ref[row : row + charge_count, :] = matmul_nt(
        grad, hidden_ref[...].astype(f32), highest
    )
    row += charge_count
    packed_ref[row:, :] = jnp.zeros((packed_ref.shape[0] - row, width), f32)
    one_hot = (
        lax.broadcasted_iota(jnp.int32, (kinds, atoms), 0) == species_ref[...]
    ).astype(f32)
    packed_ref[row : row + kinds, 0:charge_count] = matmul_nt(one_hot, grad, highest)


def step_kernel(total_ref, radial_ref, mix_ref, charge_ref, species_ref):
    basis_count, width = radial_ref.shape
    charge_count = charge_ref.shape[0]
    kinds = species_ref.shape[0]

    def normalized(gradient):
        mean = jnp.sum(gradient * gradient, keepdims=True) * (1.0 / gradient.size)
        return gradient * lax.rsqrt(mean + 1e-06)

    row = 0
    radial_ref[...] = normalized(total_ref[row : row + basis_count, :])
    row += basis_count
    mix_ref[...] = normalized(total_ref[row : row + width, :])
    row += width
    charge_ref[...] = normalized(total_ref[row : row + charge_count, :])
    row += charge_count
    species_ref[...] = normalized(total_ref[row : row + kinds, 0:charge_count])


def shaped(*dims, kind=f32):
    return jax.ShapeDtypeStruct(dims, kind)


def kernel(body, name, out_shape, scratch, nanoseconds, where, *operands):
    outs = out_shape if isinstance(out_shape, tuple) else (out_shape,)
    held = sum(math.prod(x.shape) * x.dtype.itemsize for x in (*outs, *scratch, *operands))
    in_vmem = pl.BlockSpec(memory_space=pltpu.VMEM)
    return pl.pallas_call(
        body,
        out_shape=out_shape,
        in_specs=[pl.BlockSpec(memory_space=pltpu.SMEM)] + [in_vmem] * len(operands),
        out_specs=tuple(in_vmem for _ in outs) if isinstance(out_shape, tuple) else in_vmem,
        scratch_shapes=[pltpu.VMEM(x.shape, x.dtype) for x in scratch],
        compiler_params=pltpu.CompilerParams(vmem_limit_bytes=2 * held + spare_vmem),
        cost_estimate=pl.CostEstimate(
            flops=nanoseconds * 1_000_000, bytes_accessed=held, transcendentals=0
        ),
        name=name,
    )(where, *operands)


def on_device(
    features,
    positions,
    neighbours,
    neighbour_count,
    ghost_sends,
    species,
    wave_index,
    force_ref,
    radial_weight,
    mix_weight,
    charge_weight,
    species_charge,
):
    atoms, width = features.shape
    basis_count = radial_weight.shape[0]
    charge_count = charge_weight.shape[1]
    kinds = species_charge.shape[0]
    wave_count = wave_index.shape[1]
    domains = lax.axis_size("dom")
    box_x = 1.25 * (atoms * domains) / 64
    group = 4 if domains % 4 == 0 else 1
    share = wave_count // group
    quads = [[group * q + m for m in range(group)] for q in range(domains // group)]
    entries = atoms + 2 * ghost_sends.shape[1]

    me = lax.axis_index("dom")
    where = jnp.stack(
        [
            (me + domains - 1) % domains,
            me,
            (me + 1) % domains,
            me % group,
            me // group * group,
        ]
    ).astype(jnp.int32)
    small = jnp.concatenate([positions, force_ref, ghost_sends.astype(f32)], axis=0)
    upward = [(i, (i + 1) % domains) for i in range(domains)]
    downward = [(j, i) for i, j in upward]
    from_low = lax.ppermute(features, "dom", upward)
    from_up = lax.ppermute(features, "dom", downward)
    small_all = lax.all_to_all(
        jnp.broadcast_to(small[None], (domains,) + small.shape), "dom", 0, 0
    )
    species_row = species[None, :]
    slots = neighbours.T
    charge_rows = charge_weight.T

    filtered, messages, before, hidden, charges = kernel(
        lambda *refs: edge_kernel(*refs, box_x=box_x),
        "edges",
        (
            shaped(basis_count, width, atoms),
            shaped(width, atoms),
            shaped(width, atoms),
            shaped(width, atoms, kind=bf16),
            shaped(domains, charge_count, atoms, kind=bf16),
        ),
        (
            shaped(entries // 32, atoms, kind=jnp.int32),
            shaped(entries, small.shape[0]),
            shaped(width, entries, kind=bf16),
            shaped(basis_count, entries, atoms, kind=bf16),
        ),
        12_000,
        where,
        features,
        from_low,
        from_up,
        small_all,
        slots,
        neighbour_count[None, :],
        species_row,
        radial_weight,
        mix_weight,
        charge_rows,
        species_charge,
    )
    charges_all = lax.all_to_all(charges, "dom", 0, 0)
    waves = kernel(
        lambda *refs: phase_kernel(*refs, box_x=box_x),
        "phases",
        shaped(2 * share, domains * atoms, kind=bf16),
        (),
        8_000,
        where,
        small_all,
        wave_index,
    )
    weights, force_parts = kernel(
        lambda *refs: structure_kernel(*refs, box_x=box_x),
        "structure",
        (
            shaped(3 * charge_count, 2 * share),
            shaped(group, 3, domains, atoms),
        ),
        (shaped(3, domains, atoms),),
        5_000,
        where,
        charges_all,
        wave_index,
        waves,
    )
    force_parts = lax.all_to_all(force_parts, "dom", 0, 0, axis_index_groups=quads)
    forces, grad_parts = kernel(
        lambda *refs: gradient_kernel(*refs, box_x=box_x),
        "gradient",
        (shaped(3, atoms), shaped(group, charge_count, atoms, kind=bf16)),
        (shaped(3, domains, atoms),),
        5_000,
        where,
        small_all,
        charges_all,
        wave_index,
        waves,
        weights,
        force_parts,
    )
    grad_parts = lax.all_to_all(grad_parts, "dom", 0, 0, axis_index_groups=quads)

    rows = basis_count + width + charge_count + kinds
    rows = -(-rows // (8 * domains)) * (8 * domains)
    packed = kernel(
        lambda _, *refs: weights_kernel(*refs, kinds=kinds),
        "weights",
        shaped(rows, width),
        (),
        3_000,
        where,
        grad_parts,
        filtered,
        messages,
        before,
        hidden,
        species_row,
        mix_weight,
        charge_rows,
    )
    pieces = lax.all_to_all(packed.reshape(domains, rows // domains, width), "dom", 0, 0)
    piece = jnp.sum(pieces, axis=0)
    total = lax.all_to_all(jnp.broadcast_to(piece[None], pieces.shape), "dom", 0, 0)
    radial_step, mix_step, charge_step, species_step = kernel(
        lambda _, *refs: step_kernel(*refs),
        "steps",
        (
            shaped(basis_count, width),
            shaped(width, width),
            shaped(charge_count, width),
            shaped(kinds, charge_count),
        ),
        (),
        2_000,
        where,
        total.reshape(rows, width),
    )
    return forces, radial_step, mix_step, charge_step.T, species_step


def solution(mesh):
    placed = (
        P(("cell", "dom"), None),
        P(None, ("cell", "dom")),
        P(("cell", "dom"), None),
        P(("cell", "dom")),
        P(None, ("cell", "dom")),
        P(("cell", "dom")),
        P(),
        P(None, ("cell", "dom")),
        P(),
        P(),
        P(),
        P(),
    )
    return jax.shard_map(
        on_device,
        mesh=mesh,
        in_specs=placed,
        out_specs=(
            P(None, ("cell", "dom")),
            P("cell", None),
            P("cell", None),
            P("cell", None),
            P("cell", None),
        ),
        check_vma=False,
    )
```

```python
import math

import jax
import jax.numpy as jnp
import numpy as np
from jax import lax
from jax.experimental import pallas as pl
from jax.experimental.pallas import tpu as pltpu
from jax.sharding import PartitionSpec as P

cutoff_radius = 5.0
kernel_width = 1.0
basis_width = 0.5
box_side = 20.0
two_pi = 6.283185307179586
highest = lax.Precision.HIGHEST
f32 = jnp.float32
bf16 = jnp.bfloat16
spare_vmem = 4 * 1024 * 1024
waves_bytes = 8 * 1024 * 1024


def fitted(function, degrees, reach):
    nodes = reach * np.cos((np.arange(400) + 0.5) * np.pi / 400)
    powers = np.stack([nodes**d for d in degrees], axis=1)
    return [float(c) for c in np.linalg.lstsq(powers, function(nodes), rcond=None)[0]]


sine_terms = fitted(lambda x: np.sin(np.pi * x), (1, 3, 5, 7, 9), 0.5)
cosine_terms = fitted(lambda x: np.cos(np.pi * x), (0, 2, 4, 6, 8), 0.5)


def horner(terms, square):
    value = terms[-1]
    for term in terms[-2::-1]:
        value = value * square + term
    return value


def matmul(left, right, precision=None):
    return lax.dot_general(
        left, right, (((1,), (0,)), ((), ())), precision=precision, preferred_element_type=f32
    )


def matmul_nt(left, right, precision=None):
    return lax.dot_general(
        left, right, (((1,), (1,)), ((), ())), precision=precision, preferred_element_type=f32
    )


def turned(value):
    return jnp.transpose(value.astype(f32)).astype(value.dtype)


def sigmoid(value):
    return 1.0 / (1.0 + jnp.exp(-value))


def pieces_of(value):
    first = value.astype(bf16).astype(f32)
    rest = value - first
    second = rest.astype(bf16).astype(f32)
    return first, second, rest - second


def pack_kernel(feat_ref, positions_ref, ghost_ref, packed_ref):
    atoms, width = feat_ref.shape
    packed_ref[0:atoms, :] = feat_ref[...]
    extra = jnp.concatenate(
        pieces_of(positions_ref[...])
        + (ghost_ref[...].astype(f32), jnp.zeros((5, atoms), f32)),
        axis=0,
    ).astype(bf16)
    for part in range(atoms // width):
        first = atoms + part * 16
        packed_ref[first : first + 16, :] = extra[:, part * width : (part + 1) * width]


def edge_kernel(
    where_ref,
    feat_ref,
    positions_ref,
    force_ref,
    near_ref,
    far_ref,
    slots_ref,
    count_ref,
    species_ref,
    radial_ref,
    mix_ref,
    charge_ref,
    offset_ref,
    filtered_ref,
    messages_ref,
    before_ref,
    hidden_ref,
    shared_ref,
    words_ref,
    coords_ref,
    table_ref,
    pair_ref,
    *,
    box_x,
):
    atoms, width = feat_ref.shape
    slots = slots_ref.shape[0]
    basis_count = radial_ref.shape[0]
    ghosts = atoms
    entries = atoms + 2 * ghosts
    own_rows = positions_ref[...]
    site = lax.broadcasted_iota(jnp.int32, (atoms, ghosts), 0).astype(f32)

    own_feat = turned(feat_ref[...])
    table_ref[:, 0:atoms] = own_feat
    padding = jnp.zeros((5, atoms), f32)
    coords_ref[0:atoms, :] = jnp.transpose(jnp.concatenate([own_rows, padding], axis=0))
    for ref, is_low in ((near_ref, where_ref[0] == 1), (far_ref, where_ref[0] == 0)):
        extra = jnp.concatenate(
            [ref[atoms + part * 16 : atoms + part * 16 + 16, :] for part in range(atoms // width)],
            axis=1,
        )
        sends = extra[8:16, :].astype(f32)
        sends = jnp.where(is_low, sends[2:3, :], sends[1:2, :])
        chosen = (site == sends).astype(bf16)
        first = pl.multiple_of(jnp.where(is_low, atoms, atoms + ghosts), ghosts)
        places = pl.ds(first, ghosts)
        table_ref[:, places] = matmul(turned(ref[0:atoms, :]), chosen).astype(bf16)
        moved = matmul(extra, chosen)
        moved = moved[0:3, :] + (moved[3:6, :] + moved[6:9, :])
        coords_ref[places, :] = jnp.transpose(jnp.concatenate([moved, padding], axis=0))

    listed = slots_ref[...]
    live = lax.broadcasted_iota(jnp.int32, (slots, atoms), 0) < count_ref[...]
    word_of = jnp.where(live, listed >> 5, -1)
    bit = jnp.left_shift(jnp.ones_like(listed), listed & 31)
    for word in range(entries // 32):
        value = jnp.where(word_of == word, bit, 0)
        rows = slots
        while rows > 1:
            rows //= 2
            value = value[:rows] | value[rows:]
        words_ref[word : word + 1, :] = value

    centers = [
        0.5 + (cutoff_radius - 0.5) * float(b) / (basis_count - 1) for b in range(basis_count)
    ]
    scale = -math.log2(math.e) / (basis_width * basis_width)
    own_x, own_y, own_z = own_rows[0:1, :], own_rows[1:2, :], own_rows[2:3, :]
    step = 32

    def block(index, carry):
        first = pl.multiple_of(index * step, step)
        coords = coords_ref[pl.ds(first, step), :]
        total = jnp.zeros((step, atoms), f32)
        for axis, (mine, length) in enumerate(
            ((own_x, box_x), (own_y, box_side), (own_z, box_side))
        ):
            away = coords[:, axis : axis + 1] - mine
            away = away - length * jnp.floor(away * (1.0 / length) + 0.5)
            total = total + away * away
        distance = jnp.sqrt(total)
        word = words_ref[pl.ds(index, 1), :]
        sublane = lax.broadcasted_iota(jnp.int32, (step, atoms), 0)
        is_live = (jnp.right_shift(jnp.broadcast_to(word, (step, atoms)), sublane) & 1) != 0
        half = jnp.minimum(distance, cutoff_radius) * (1.0 / cutoff_radius) - 0.5
        fade = 0.5 - 0.5 * (half * horner(sine_terms, half * half))
        weight = jnp.where(is_live, fade, 0.0)
        for b in range(basis_count):
            offset = distance - centers[b]
            basis = jnp.exp2(offset * offset * scale).astype(bf16).astype(f32)
            pair_ref[b, pl.ds(first, step), :] = (weight * basis).astype(bf16)
        return carry

    lax.fori_loop(0, entries // step, block, 0)

    radial = jnp.transpose(radial_ref[...].astype(f32))
    messages = jnp.zeros((width, atoms), f32)
    for b in range(basis_count):
        filtered = matmul(table_ref[...], pair_ref[b])
        filtered_ref[b] = filtered
        messages = messages + radial[:, b : b + 1] * filtered
    messages_ref[...] = messages
    before = matmul(jnp.transpose(mix_ref[...].astype(f32)), messages, highest)
    before_ref[...] = before
    hidden = (own_feat.astype(f32) + before * sigmoid(before)).astype(bf16)
    hidden_ref[...] = hidden
    kinds = offset_ref.shape[0]
    one_hot = (
        lax.broadcasted_iota(jnp.int32, (kinds, atoms), 0) == species_ref[...]
    ).astype(f32)
    charges = matmul(charge_ref[...], hidden) + matmul(
        jnp.transpose(offset_ref[...]), one_hot, highest
    )
    lengths = (box_x, box_side, box_side)
    turns = jnp.concatenate([own_rows[a : a + 1, :] * (1.0 / lengths[a]) for a in range(3)], axis=0)
    target = force_ref[...]
    high = target.astype(bf16).astype(f32)
    rows = jnp.concatenate(
        (charges,) + pieces_of(turns) + (high, target - high, jnp.zeros((1, atoms), f32)), axis=0
    ).astype(bf16)
    shared_ref[0] = rows


def wave_rows(wave_ref, first, count, box_x, total_atoms):
    index = wave_ref[:, pl.ds(first, count)].astype(f32)
    scales = (two_pi / box_x, two_pi / box_side, two_pi / box_side)
    waves = [index[a : a + 1, :] * scales[a] for a in range(3)]
    squares = waves[0] * waves[0] + waves[1] * waves[1] + waves[2] * waves[2]
    damping = jnp.exp(-0.5 * kernel_width * kernel_width * squares) * (1.0 / total_atoms)
    return index, waves, damping


def structure_kernel(
    where_ref, *refs, group, blocks, charge_count, box_x
):
    shared_refs, (wave_ref, waves_ref, weights_ref, *force_refs) = refs[:blocks], refs[blocks:]
    columns_count, _, atoms = shared_refs[0].shape
    share = waves_ref.shape[1] // 2
    first = pl.multiple_of(where_ref[1] * share, share)
    index, waves, damping = wave_rows(
        wave_ref, first, share, box_x, blocks * columns_count * atoms
    )
    columns = jnp.transpose(
        jnp.concatenate([index] * 3 + [jnp.zeros((7, share), f32)], axis=0)
    ).astype(bf16)
    shift = 12582912.0

    def block(j, carry):
        for r in range(blocks):
            turns = matmul(columns, shared_refs[r][j, charge_count : charge_count + 16, :])
            turns = turns - ((turns + shift) - shift)
            square = turns * turns
            half_sine = turns * horner(sine_terms, square)
            half_cosine = horner(cosine_terms, square)
            d = j * blocks + r
            waves_ref[d, 0:share, :] = (2.0 * half_sine * half_cosine).astype(bf16)
            waves_ref[d, share : 2 * share, :] = (1.0 - 2.0 * half_sine * half_sine).astype(bf16)
        return carry

    lax.fori_loop(0, columns_count, block, 0)
    structure = jnp.zeros((charge_count, 2 * share), f32)
    for d in range(blocks * columns_count):
        j, r = divmod(d, blocks)
        structure = structure + matmul_nt(shared_refs[r][j, 0:charge_count, :], waves_ref[d])
    along_sin = structure[:, :share] * damping
    along_cos = structure[:, share:] * damping
    to_sine = jnp.concatenate([along_cos * waves[a] for a in range(3)], axis=0)
    to_cosine = jnp.concatenate([-along_sin * waves[a] for a in range(3)], axis=0)
    weights = jnp.concatenate([to_sine, to_cosine], axis=1)
    weights_ref[...] = weights
    weights = weights.astype(bf16)
    for d in range(blocks * columns_count):
        j, r = divmod(d, blocks)
        field = matmul(weights, waves_ref[d])
        charges = shared_refs[r][j, 0:charge_count, :].astype(f32)
        for a in range(3):
            row = jnp.sum(
                field[a * charge_count : (a + 1) * charge_count, :] * charges,
                axis=0,
                keepdims=True,
            )
            for m in range(group):
                force_refs[m][a, d ^ m : (d ^ m) + 1, :] = row


def gradient_kernel(where_ref, *refs, group, blocks, charge_count, box_x):
    shared_refs, part_refs = refs[:blocks], refs[blocks : blocks + group]
    wave_ref, waves_ref, weights_ref, forces_ref, *grad_refs, total_ref = refs[blocks + group :]
    columns_count, _, atoms = shared_refs[0].shape
    share = waves_ref.shape[1] // 2
    first = pl.multiple_of(where_ref[1] * share, share)
    _, waves, damping = wave_rows(wave_ref, first, share, box_x, blocks * columns_count * atoms)
    total = part_refs[0][...]
    for m in range(1, group):
        total = total + part_refs[m][...]
    total_ref[...] = total
    for a in range(3):
        forces_ref[a : a + 1, :] = total[a, 0:1, :]

    def errors_of(d):
        j, r = divmod(d, blocks)
        target = shared_refs[r][j, charge_count : charge_count + 16, :].astype(f32)
        target = target[9:12, :] + target[12:15, :]
        return [2.0 * (total_ref[a, d : d + 1, :] - target[a : a + 1, :]) for a in range(3)]

    summed = jnp.zeros((3 * charge_count, 2 * share), f32)
    for d in range(blocks * columns_count):
        j, r = divmod(d, blocks)
        charges = shared_refs[r][j, 0:charge_count, :].astype(f32)
        errors = errors_of(d)
        scaled = jnp.concatenate([errors[a] * charges for a in range(3)], axis=0).astype(bf16)
        summed = summed + matmul_nt(scaled, waves_ref[d])

    def along(value):
        return sum(
            waves[a] * value[a * charge_count : (a + 1) * charge_count, :] for a in range(3)
        )

    back_cos = damping * along(summed[:, :share])
    back_sin = -damping * along(summed[:, share:])
    back = jnp.concatenate([back_sin, back_cos], axis=1)
    back_high = back.astype(bf16)
    back_low = (back - back_high.astype(f32)).astype(bf16)
    weights = weights_ref[...]
    weights_high = weights.astype(bf16)
    weights_low = (weights - weights_high.astype(f32)).astype(bf16)
    for m in range(group):
        errors = errors_of(m)
        grad = matmul(back_high, waves_ref[m]) + matmul(back_low, waves_ref[m])
        field = matmul(weights_high, waves_ref[m]) + matmul(weights_low, waves_ref[m])
        for a in range(3):
            grad = grad + errors[a] * field[a * charge_count : (a + 1) * charge_count, :]
        grad_refs[m][...] = grad.astype(grad_refs[m].dtype)


def weights_kernel(*refs, group, kinds):
    part_refs = refs[:group]
    (
        filtered_ref,
        messages_ref,
        before_ref,
        hidden_ref,
        species_ref,
        mix_ref,
        charge_ref,
        packed_ref,
    ) = refs[group:]
    charge_count, atoms = part_refs[0].shape
    basis_count, width, _ = filtered_ref.shape
    grad = part_refs[0][...].astype(f32)
    for m in range(1, group):
        grad = grad + part_refs[m][...].astype(f32)
    before = before_ref[...]
    gate = sigmoid(before)
    upstream = matmul(jnp.transpose(charge_ref[...].astype(f32)), grad, highest)
    before_grad = upstream * (gate * (1.0 + before * (1.0 - gate)))
    message_grad = matmul(mix_ref[...].astype(f32), before_grad, highest)
    columns = [
        jnp.sum(message_grad * filtered_ref[b], axis=1, keepdims=True) for b in range(basis_count)
    ]
    radial = jnp.concatenate(columns, axis=1)
    row = 0
    packed_ref[row : row + basis_count, :] = jnp.transpose(radial)
    row += basis_count
    packed_ref[row : row + width, :] = matmul_nt(messages_ref[...], before_grad, highest)
    row += width
    packed_ref[row : row + charge_count, :] = matmul_nt(
        grad, hidden_ref[...].astype(f32), highest
    )
    row += charge_count
    packed_ref[row:, :] = jnp.zeros((packed_ref.shape[0] - row, width), f32)
    one_hot = (
        lax.broadcasted_iota(jnp.int32, (kinds, atoms), 0) == species_ref[...]
    ).astype(f32)
    packed_ref[row : row + kinds, 0:charge_count] = matmul_nt(one_hot, grad, highest)


def step_kernel(total_ref, radial_ref, mix_ref, charge_ref, species_ref):
    basis_count, width = radial_ref.shape
    charge_count = charge_ref.shape[0]
    kinds = species_ref.shape[0]

    def normalized(gradient):
        mean = jnp.sum(gradient * gradient, keepdims=True) * (1.0 / gradient.size)
        return gradient * lax.rsqrt(mean + 1e-06)

    row = 0
    radial_ref[...] = normalized(total_ref[row : row + basis_count, :])
    row += basis_count
    mix_ref[...] = normalized(total_ref[row : row + width, :])
    row += width
    charge_ref[...] = normalized(total_ref[row : row + charge_count, :])
    row += charge_count
    species_ref[...] = normalized(total_ref[row : row + kinds, 0:charge_count])


def shaped(*dims, kind=f32):
    return jax.ShapeDtypeStruct(dims, kind)


def kernel(body, name, out_shape, scratch, nanoseconds, *operands, scalars=(), wanted=0):
    outs = out_shape if isinstance(out_shape, tuple) else (out_shape,)
    held = sum(math.prod(x.shape) * x.dtype.itemsize for x in (*outs, *scratch, *operands))
    in_vmem = pl.BlockSpec(memory_space=pltpu.VMEM)
    in_smem = pl.BlockSpec(memory_space=pltpu.SMEM)
    return pl.pallas_call(
        body,
        out_shape=out_shape,
        in_specs=[in_smem] * len(scalars) + [in_vmem] * len(operands),
        out_specs=tuple(in_vmem for _ in outs) if isinstance(out_shape, tuple) else in_vmem,
        scratch_shapes=[pltpu.VMEM(x.shape, x.dtype) for x in scratch],
        compiler_params=pltpu.CompilerParams(vmem_limit_bytes=max(held + spare_vmem, wanted)),
        cost_estimate=pl.CostEstimate(
            flops=nanoseconds * 1_000_000, bytes_accessed=held, transcendentals=0
        ),
        name=name,
    )(*scalars, *operands)


def across(value, bits):
    domains = lax.axis_size("dom")
    return lax.ppermute(value, "dom", [(i, i ^ bits) for i in range(domains)])


def on_device(
    features,
    positions,
    neighbours,
    neighbour_count,
    ghost_sends,
    species,
    wave_index,
    force_ref,
    radial_weight,
    mix_weight,
    charge_weight,
    species_charge,
):
    atoms, width = features.shape
    basis_count = radial_weight.shape[0]
    charge_count = charge_weight.shape[1]
    kinds = species_charge.shape[0]
    wave_count = wave_index.shape[1]
    domains = lax.axis_size("dom")
    box_x = 1.25 * (atoms * domains) / 64
    group = 2 if domains % 2 == 0 else 1
    while group < domains and 4 * wave_count // group * atoms * domains > waves_bytes:
        group *= 2
    share = wave_count // group
    entries = atoms + 2 * ghost_sends.shape[1]

    me = lax.axis_index("dom")
    where = jnp.stack([me % 2, me % group]).astype(jnp.int32)
    packed = kernel(
        pack_kernel,
        "pack",
        shaped(atoms + 16 * (atoms // width), width, kind=bf16),
        (),
        1_000,
        features,
        positions,
        ghost_sends,
        wanted=60 * 1024 * 1024,
    )
    near = across(packed, 1)
    beyond = [(i, (i + 1 if i % 2 else i - 1) % domains) for i in range(domains)]
    far = lax.ppermute(packed, "dom", beyond)
    species_row = species[None, :]
    slots = neighbours.T
    charge_rows = charge_weight.T

    filtered, messages, before, hidden, shared = kernel(
        lambda *refs: edge_kernel(*refs, box_x=box_x),
        "edges",
        (
            shaped(basis_count, width, atoms),
            shaped(width, atoms),
            shaped(width, atoms),
            shaped(width, atoms, kind=bf16),
            shaped(1, charge_count + 16, atoms, kind=bf16),
        ),
        (
            shaped(entries // 32, atoms, kind=jnp.int32),
            shaped(entries, 8),
            shaped(width, entries, kind=bf16),
            shaped(basis_count, entries, atoms, kind=bf16),
        ),
        12_000,
        features,
        positions,
        force_ref,
        near,
        far,
        slots,
        neighbour_count[None, :],
        species_row,
        radial_weight,
        mix_weight,
        charge_rows,
        species_charge,
        scalars=(where,),
        wanted=60 * 1024 * 1024,
    )
    blocks = 4 if domains % 4 == 0 else 2
    column = jnp.concatenate(
        [shared] + [across(shared, bits) for bits in range(blocks, domains, blocks)], axis=0
    )
    columns = [column] + [across(column, bits) for bits in range(1, blocks)]
    waves, weights, *force_parts = kernel(
        lambda *refs: structure_kernel(
            *refs, group=group, blocks=blocks, charge_count=charge_count, box_x=box_x
        ),
        "structure",
        (
            shaped(domains, 2 * share, atoms, kind=bf16),
            shaped(3 * charge_count, 2 * share),
        )
        + (shaped(3, domains, atoms),) * group,
        (),
        10_000,
        *columns,
        wave_index,
        scalars=(where,),
    )
    force_parts = force_parts[:1] + [across(force_parts[m], m) for m in range(1, group)]
    forces, *grad_parts = kernel(
        lambda *refs: gradient_kernel(
            *refs, group=group, blocks=blocks, charge_count=charge_count, box_x=box_x
        ),
        "gradient",
        (shaped(3, atoms),) + (shaped(charge_count, atoms, kind=bf16),) * group,
        (shaped(3, domains, atoms),),
        5_000,
        *columns,
        *force_parts,
        wave_index,
        waves,
        weights,
        scalars=(where,),
    )
    grad_parts = grad_parts[:1] + [across(grad_parts[m], m) for m in range(1, group)]

    rows = basis_count + width + charge_count + kinds
    rows = -(-rows // (8 * domains)) * (8 * domains)
    packed = kernel(
        lambda *refs: weights_kernel(*refs, group=group, kinds=kinds),
        "weights",
        shaped(rows, width),
        (),
        3_000,
        *grad_parts,
        filtered,
        messages,
        before,
        hidden,
        species_row,
        mix_weight,
        charge_rows,
    )
    pieces = lax.all_to_all(packed.reshape(domains, rows // domains, width), "dom", 0, 0)
    piece = jnp.sum(pieces, axis=0)
    total = lax.all_to_all(jnp.broadcast_to(piece[None], pieces.shape), "dom", 0, 0)
    radial_step, mix_step, charge_step, species_step = kernel(
        step_kernel,
        "steps",
        (
            shaped(basis_count, width),
            shaped(width, width),
            shaped(charge_count, width),
            shaped(kinds, charge_count),
        ),
        (),
        2_000,
        total.reshape(rows, width),
    )
    return forces, radial_step, mix_step, charge_step.T, species_step


def solution(mesh):
    placed = (
        P(("cell", "dom"), None),
        P(None, ("cell", "dom")),
        P(("cell", "dom"), None),
        P(("cell", "dom")),
        P(None, ("cell", "dom")),
        P(("cell", "dom")),
        P(),
        P(None, ("cell", "dom")),
        P(),
        P(),
        P(),
        P(),
    )
    return jax.shard_map(
        on_device,
        mesh=mesh,
        in_specs=placed,
        out_specs=(
            P(None, ("cell", "dom")),
            P("cell", None),
            P("cell", None),
            P("cell", None),
            P("cell", None),
        ),
        check_vma=False,
    )
```

```python
import math

import jax
import jax.numpy as jnp
import numpy as np
from jax import lax
from jax.experimental import pallas as pl
from jax.experimental.pallas import tpu as pltpu
from jax.sharding import PartitionSpec as P

cutoff_radius = 5.0
kernel_width = 1.0
basis_width = 0.5
box_side = 20.0
two_pi = 6.283185307179586
highest = lax.Precision.HIGHEST
f32 = jnp.float32
bf16 = jnp.bfloat16
spare_vmem = 4 * 1024 * 1024
waves_bytes = 4 * 1024 * 1024


def fitted(function, degrees, reach):
    nodes = reach * np.cos((np.arange(400) + 0.5) * np.pi / 400)
    powers = np.stack([nodes**d for d in degrees], axis=1)
    return [float(c) for c in np.linalg.lstsq(powers, function(nodes), rcond=None)[0]]


sine_terms = fitted(lambda x: np.sin(np.pi * x), (1, 3, 5, 7, 9), 0.5)
short_sine = fitted(lambda x: np.sin(np.pi * x), (1, 3, 5, 7), 0.5)
short_cosine = fitted(lambda x: np.cos(np.pi * x), (0, 2, 4, 6), 0.5)


def horner(terms, square):
    value = terms[-1]
    for term in terms[-2::-1]:
        value = value * square + term
    return value


def matmul(left, right, precision=None):
    return lax.dot_general(
        left, right, (((1,), (0,)), ((), ())), precision=precision, preferred_element_type=f32
    )


def matmul_nt(left, right, precision=None):
    return lax.dot_general(
        left, right, (((1,), (1,)), ((), ())), precision=precision, preferred_element_type=f32
    )


def turned(value):
    return jnp.transpose(value.astype(f32)).astype(value.dtype)


def sigmoid(value):
    return 1.0 / (1.0 + jnp.exp(-value))


def pieces_of(value):
    first = value.astype(bf16).astype(f32)
    rest = value - first
    second = rest.astype(bf16).astype(f32)
    return first, second, rest - second


def pack_kernel(feat_ref, positions_ref, ghost_ref, packed_ref):
    atoms, width = feat_ref.shape
    packed_ref[0:atoms, :] = feat_ref[...]
    extra = jnp.concatenate(
        pieces_of(positions_ref[...])
        + (ghost_ref[...].astype(f32), jnp.zeros((5, atoms), f32)),
        axis=0,
    ).astype(bf16)
    for part in range(atoms // width):
        first = atoms + part * 16
        packed_ref[first : first + 16, :] = extra[:, part * width : (part + 1) * width]


def edge_kernel(
    where_ref,
    feat_ref,
    positions_ref,
    force_ref,
    near_ref,
    far_ref,
    slots_ref,
    count_ref,
    species_ref,
    radial_ref,
    mix_ref,
    charge_ref,
    offset_ref,
    filtered_ref,
    messages_ref,
    before_ref,
    hidden_ref,
    shared_ref,
    words_ref,
    coords_ref,
    table_ref,
    pair_ref,
    *,
    box_x,
):
    atoms, width = feat_ref.shape
    slots = slots_ref.shape[0]
    basis_count = radial_ref.shape[0]
    ghosts = atoms
    entries = atoms + 2 * ghosts
    own_rows = positions_ref[...]
    site = lax.broadcasted_iota(jnp.int32, (atoms, ghosts), 0).astype(f32)

    own_feat = turned(feat_ref[...])
    table_ref[:, 0:atoms] = own_feat
    padding = jnp.zeros((5, atoms), f32)
    coords_ref[0:atoms, :] = jnp.transpose(jnp.concatenate([own_rows, padding], axis=0))
    for ref, is_low in ((near_ref, where_ref[0] == 1), (far_ref, where_ref[0] == 0)):
        extra = jnp.concatenate(
            [ref[atoms + part * 16 : atoms + part * 16 + 16, :] for part in range(atoms // width)],
            axis=1,
        )
        sends = extra[8:16, :].astype(f32)
        sends = jnp.where(is_low, sends[2:3, :], sends[1:2, :])
        chosen = (site == sends).astype(bf16)
        first = pl.multiple_of(jnp.where(is_low, atoms, atoms + ghosts), ghosts)
        places = pl.ds(first, ghosts)
        table_ref[:, places] = matmul(turned(ref[0:atoms, :]), chosen).astype(bf16)
        moved = matmul(extra, chosen)
        moved = moved[0:3, :] + (moved[3:6, :] + moved[6:9, :])
        coords_ref[places, :] = jnp.transpose(jnp.concatenate([moved, padding], axis=0))

    listed = slots_ref[...]
    live = lax.broadcasted_iota(jnp.int32, (slots, atoms), 0) < count_ref[...]
    word_of = jnp.where(live, listed >> 5, -1)
    bit = jnp.left_shift(jnp.ones_like(listed), listed & 31)
    for word in range(entries // 32):
        value = jnp.where(word_of == word, bit, 0)
        rows = slots
        while rows > 1:
            rows //= 2
            value = value[:rows] | value[rows:]
        words_ref[word : word + 1, :] = value

    centers = [
        0.5 + (cutoff_radius - 0.5) * float(b) / (basis_count - 1) for b in range(basis_count)
    ]
    scale = -math.log2(math.e) / (basis_width * basis_width)
    middle = basis_count // 2
    gap = centers[1] - centers[0]
    own_x, own_y, own_z = own_rows[0:1, :], own_rows[1:2, :], own_rows[2:3, :]
    step = 32

    def block(index, carry):
        first = pl.multiple_of(index * step, step)
        coords = coords_ref[pl.ds(first, step), :]
        total = jnp.zeros((step, atoms), f32)
        for axis, (mine, length) in enumerate(
            ((own_x, box_x), (own_y, box_side), (own_z, box_side))
        ):
            away = coords[:, axis : axis + 1] - mine
            away = away - length * jnp.floor(away * (1.0 / length) + 0.5)
            total = total + away * away
        distance = jnp.sqrt(total)
        word = words_ref[pl.ds(index, 1), :]
        sublane = lax.broadcasted_iota(jnp.int32, (step, atoms), 0)
        is_live = (jnp.right_shift(jnp.broadcast_to(word, (step, atoms)), sublane) & 1) != 0
        half = jnp.minimum(distance, cutoff_radius) * (1.0 / cutoff_radius) - 0.5
        fade = 0.5 - 0.5 * (half * horner(sine_terms, half * half))
        weight = jnp.where(jnp.logical_and(is_live, distance < cutoff_radius), fade, 0.0)
        offset = jnp.minimum(distance, cutoff_radius) - centers[middle]
        value = jnp.exp2(offset * offset * scale)
        for direction in (1, -1):
            ratio = jnp.exp2(offset * (-2.0 * direction * gap * scale))
            running = value
            for b in range(middle, basis_count) if direction == 1 else range(middle - 1, -1, -1):
                if b != middle:
                    running = running * ratio
                basis = running * math.exp(-(((b - middle) * gap / basis_width) ** 2))
                basis = basis.astype(bf16).astype(f32)
                pair_ref[b, pl.ds(first, step), :] = (weight * basis).astype(bf16)
        return carry

    lax.fori_loop(0, entries // step, block, 0, unroll=8)

    radial = jnp.transpose(radial_ref[...].astype(f32))
    messages = jnp.zeros((width, atoms), f32)
    for b in range(basis_count):
        filtered = matmul(table_ref[...], pair_ref[b])
        filtered_ref[b] = filtered
        messages = messages + radial[:, b : b + 1] * filtered
    messages_ref[...] = messages
    before = matmul(jnp.transpose(mix_ref[...].astype(f32)), messages, highest)
    before_ref[...] = before
    hidden = (own_feat.astype(f32) + before * sigmoid(before)).astype(bf16)
    hidden_ref[...] = hidden
    kinds = offset_ref.shape[0]
    one_hot = (
        lax.broadcasted_iota(jnp.int32, (kinds, atoms), 0) == species_ref[...]
    ).astype(f32)
    charges = matmul(charge_ref[...], hidden) + matmul(
        jnp.transpose(offset_ref[...]), one_hot, highest
    )
    lengths = (box_x, box_side, box_side)
    turns = jnp.concatenate([own_rows[a : a + 1, :] * (1.0 / lengths[a]) for a in range(3)], axis=0)
    target = force_ref[...]
    high = target.astype(bf16).astype(f32)
    rows = jnp.concatenate(
        (charges,) + pieces_of(turns) + (high, target - high, jnp.zeros((1, atoms), f32)), axis=0
    ).astype(bf16)
    shared_ref[0] = rows


def wave_rows(wave_ref, first, count, box_x, total_atoms):
    index = wave_ref[:, pl.ds(first, count)].astype(f32)
    scales = (two_pi / box_x, two_pi / box_side, two_pi / box_side)
    waves = [index[a : a + 1, :] * scales[a] for a in range(3)]
    squares = waves[0] * waves[0] + waves[1] * waves[1] + waves[2] * waves[2]
    damping = jnp.exp(-0.5 * kernel_width * kernel_width * squares) * (1.0 / total_atoms)
    return index, waves, damping


def structure_kernel(
    where_ref, *refs, group, blocks, charge_count, box_x
):
    shared_refs, (wave_ref, waves_ref, weights_ref, *force_refs) = refs[:blocks], refs[blocks:]
    columns_count, _, atoms = shared_refs[0].shape
    share = waves_ref.shape[1] // 2
    first = pl.multiple_of(where_ref[1] * share, share)
    index, waves, damping = wave_rows(
        wave_ref, first, share, box_x, blocks * columns_count * atoms
    )
    columns = jnp.transpose(
        jnp.concatenate([index] * 3 + [jnp.zeros((7, share), f32)], axis=0)
    ).astype(bf16)
    shift = 12582912.0

    def block(j, carry):
        for r in range(blocks):
            turns = matmul(columns, shared_refs[r][j, charge_count : charge_count + 16, :])
            turns = turns - ((turns + shift) - shift)
            square = turns * turns
            half_sine = turns * horner(short_sine, square)
            half_cosine = horner(short_cosine, square)
            d = j * blocks + r
            waves_ref[d, 0:share, :] = (2.0 * half_sine * half_cosine).astype(bf16)
            waves_ref[d, share : 2 * share, :] = (1.0 - 2.0 * half_sine * half_sine).astype(bf16)
        return carry

    lax.fori_loop(0, columns_count, block, 0, unroll=4)
    structure = jnp.zeros((charge_count, 2 * share), f32)
    for d in range(blocks * columns_count):
        j, r = divmod(d, blocks)
        structure = structure + matmul_nt(shared_refs[r][j, 0:charge_count, :], waves_ref[d])
    along_sin = structure[:, :share] * damping
    along_cos = structure[:, share:] * damping
    to_sine = jnp.concatenate([along_cos * waves[a] for a in range(3)], axis=0)
    to_cosine = jnp.concatenate([-along_sin * waves[a] for a in range(3)], axis=0)
    weights = jnp.concatenate([to_sine, to_cosine], axis=1)
    weights_ref[...] = weights
    weights = weights.astype(bf16)
    for d in range(blocks * columns_count):
        j, r = divmod(d, blocks)
        field = matmul(weights, waves_ref[d])
        charges = shared_refs[r][j, 0:charge_count, :].astype(f32)
        for a in range(3):
            row = jnp.sum(
                field[a * charge_count : (a + 1) * charge_count, :] * charges,
                axis=0,
                keepdims=True,
            )
            for m in range(group):
                force_refs[m][a, d ^ m : (d ^ m) + 1, :] = row


def gradient_kernel(where_ref, *refs, group, blocks, charge_count, box_x):
    shared_refs, part_refs = refs[:blocks], refs[blocks : blocks + group]
    wave_ref, waves_ref, weights_ref, forces_ref, *grad_refs, total_ref = refs[blocks + group :]
    columns_count, _, atoms = shared_refs[0].shape
    share = waves_ref.shape[1] // 2
    first = pl.multiple_of(where_ref[1] * share, share)
    _, waves, damping = wave_rows(wave_ref, first, share, box_x, blocks * columns_count * atoms)
    total = part_refs[0][...]
    for m in range(1, group):
        total = total + part_refs[m][...]
    total_ref[...] = total
    for a in range(3):
        forces_ref[a : a + 1, :] = total[a, 0:1, :]

    def errors_of(d):
        j, r = divmod(d, blocks)
        target = shared_refs[r][j, charge_count : charge_count + 16, :].astype(f32)
        target = target[9:12, :] + target[12:15, :]
        return [2.0 * (total_ref[a, d : d + 1, :] - target[a : a + 1, :]) for a in range(3)]

    summed = jnp.zeros((3 * charge_count, 2 * share), f32)
    for d in range(blocks * columns_count):
        j, r = divmod(d, blocks)
        charges = shared_refs[r][j, 0:charge_count, :].astype(f32)
        errors = errors_of(d)
        scaled = jnp.concatenate([errors[a] * charges for a in range(3)], axis=0).astype(bf16)
        summed = summed + matmul_nt(scaled, waves_ref[d])

    def along(value):
        return sum(
            waves[a] * value[a * charge_count : (a + 1) * charge_count, :] for a in range(3)
        )

    back_cos = damping * along(summed[:, :share])
    back_sin = -damping * along(summed[:, share:])
    back = jnp.concatenate([back_sin, back_cos], axis=1)
    back_high = back.astype(bf16)
    back_low = (back - back_high.astype(f32)).astype(bf16)
    weights = weights_ref[...]
    weights_high = weights.astype(bf16)
    weights_low = (weights - weights_high.astype(f32)).astype(bf16)
    for m in range(group):
        errors = errors_of(m)
        grad = matmul(back_high, waves_ref[m]) + matmul(back_low, waves_ref[m])
        field = matmul(weights_high, waves_ref[m]) + matmul(weights_low, waves_ref[m])
        for a in range(3):
            grad = grad + errors[a] * field[a * charge_count : (a + 1) * charge_count, :]
        grad_refs[m][...] = grad.astype(grad_refs[m].dtype)


def weights_kernel(where_ref, *refs, group, kinds):
    part_refs = refs[:group]
    (
        filtered_ref,
        messages_ref,
        before_ref,
        hidden_ref,
        species_ref,
        mix_ref,
        charge_ref,
        *piece_refs,
        packed_ref,
    ) = refs[group:]
    charge_count, atoms = part_refs[0].shape
    basis_count, width, _ = filtered_ref.shape
    grad = part_refs[0][...].astype(f32)
    for m in range(1, group):
        grad = grad + part_refs[m][...].astype(f32)
    before = before_ref[...]
    gate = sigmoid(before)
    upstream = matmul(jnp.transpose(charge_ref[...].astype(f32)), grad, highest)
    before_grad = upstream * (gate * (1.0 + before * (1.0 - gate)))
    message_grad = matmul(mix_ref[...].astype(f32), before_grad, highest)
    columns = [
        jnp.sum(message_grad * filtered_ref[b], axis=1, keepdims=True) for b in range(basis_count)
    ]
    radial = jnp.concatenate(columns, axis=1)
    row = 0
    packed_ref[row : row + basis_count, :] = jnp.transpose(radial)
    row += basis_count
    packed_ref[row : row + width, :] = matmul_nt(messages_ref[...], before_grad, highest)
    row += width
    packed_ref[row : row + charge_count, :] = matmul_nt(
        grad, hidden_ref[...].astype(f32), highest
    )
    row += charge_count
    packed_ref[row:, :] = jnp.zeros((packed_ref.shape[0] - row, width), f32)
    one_hot = (
        lax.broadcasted_iota(jnp.int32, (kinds, atoms), 0) == species_ref[...]
    ).astype(f32)
    packed_ref[row : row + kinds, 0:charge_count] = matmul_nt(one_hot, grad, highest)
    count = piece_refs[0].shape[0]
    for r, ref in enumerate(piece_refs):
        ref[...] = packed_ref[pl.ds(pl.multiple_of((where_ref[2] ^ r) * count, 8), count), :]


def step_kernel(where_ref, *refs):
    *piece_refs, radial_ref, mix_ref, charge_ref, species_ref, total_ref = refs
    basis_count, width = radial_ref.shape
    charge_count = charge_ref.shape[0]
    kinds = species_ref.shape[0]

    count = piece_refs[0].shape[0]
    for r, ref in enumerate(piece_refs):
        total_ref[pl.ds(pl.multiple_of((where_ref[2] ^ r) * count, 8), count), :] = ref[...]

    def normalized(gradient):
        mean = jnp.sum(gradient * gradient, keepdims=True) * (1.0 / gradient.size)
        return gradient * lax.rsqrt(mean + 1e-06)

    row = 0
    radial_ref[...] = normalized(total_ref[row : row + basis_count, :])
    row += basis_count
    mix_ref[...] = normalized(total_ref[row : row + width, :])
    row += width
    charge_ref[...] = normalized(total_ref[row : row + charge_count, :])
    row += charge_count
    species_ref[...] = normalized(total_ref[row : row + kinds, 0:charge_count])


def shaped(*dims, kind=f32):
    return jax.ShapeDtypeStruct(dims, kind)


def kernel(body, name, out_shape, scratch, nanoseconds, *operands, scalars=(), wanted=0):
    outs = out_shape if isinstance(out_shape, tuple) else (out_shape,)
    held = sum(math.prod(x.shape) * x.dtype.itemsize for x in (*outs, *scratch, *operands))
    in_vmem = pl.BlockSpec(memory_space=pltpu.VMEM)
    in_smem = pl.BlockSpec(memory_space=pltpu.SMEM)
    return pl.pallas_call(
        body,
        out_shape=out_shape,
        in_specs=[in_smem] * len(scalars) + [in_vmem] * len(operands),
        out_specs=tuple(in_vmem for _ in outs) if isinstance(out_shape, tuple) else in_vmem,
        scratch_shapes=[pltpu.VMEM(x.shape, x.dtype) for x in scratch],
        compiler_params=pltpu.CompilerParams(vmem_limit_bytes=max(held + spare_vmem, wanted)),
        cost_estimate=pl.CostEstimate(
            flops=nanoseconds * 1_000_000, bytes_accessed=held, transcendentals=0
        ),
        name=name,
    )(*scalars, *operands)


def across(value, bits):
    domains = lax.axis_size("dom")
    return lax.ppermute(value, "dom", [(i, i ^ bits) for i in range(domains)])


def summed(values):
    while len(values) > 1:
        values = [values[i] + values[i + 1] for i in range(0, len(values), 2)]
    return values[0]


def on_device(
    features,
    positions,
    neighbours,
    neighbour_count,
    ghost_sends,
    species,
    wave_index,
    force_ref,
    radial_weight,
    mix_weight,
    charge_weight,
    species_charge,
):
    atoms, width = features.shape
    basis_count = radial_weight.shape[0]
    charge_count = charge_weight.shape[1]
    kinds = species_charge.shape[0]
    wave_count = wave_index.shape[1]
    domains = lax.axis_size("dom")
    box_x = 1.25 * (atoms * domains) / 64
    group = 2 if domains % 2 == 0 else 1
    while (
        group < domains
        and 4 * wave_count // group * atoms * domains > waves_bytes
        and wave_count % (256 * group) == 0
    ):
        group *= 2
    share = wave_count // group
    entries = atoms + 2 * ghost_sends.shape[1]

    me = lax.axis_index("dom")
    blocks = 4 if domains % 4 == 0 else 2
    where = jnp.stack([me % 2, me % group, me % blocks]).astype(jnp.int32)
    packed = kernel(
        pack_kernel,
        "pack",
        shaped(atoms + 16 * (atoms // width), width, kind=bf16),
        (),
        1_000,
        features,
        positions,
        ghost_sends,
        wanted=60 * 1024 * 1024,
    )
    near = across(packed, 1)
    beyond = [(i, (i + 1 if i % 2 else i - 1) % domains) for i in range(domains)]
    far = lax.ppermute(packed, "dom", beyond)
    species_row = species[None, :]
    slots = neighbours.T
    charge_rows = charge_weight.T

    filtered, messages, before, hidden, shared = kernel(
        lambda *refs: edge_kernel(*refs, box_x=box_x),
        "edges",
        (
            shaped(basis_count, width, atoms),
            shaped(width, atoms),
            shaped(width, atoms),
            shaped(width, atoms, kind=bf16),
            shaped(1, charge_count + 16, atoms, kind=bf16),
        ),
        (
            shaped(entries // 32, atoms, kind=jnp.int32),
            shaped(entries, 8),
            shaped(width, entries, kind=bf16),
            shaped(basis_count, entries, atoms, kind=bf16),
        ),
        12_000,
        features,
        positions,
        force_ref,
        near,
        far,
        slots,
        neighbour_count[None, :],
        species_row,
        radial_weight,
        mix_weight,
        charge_rows,
        species_charge,
        scalars=(where,),
        wanted=60 * 1024 * 1024,
    )
    column = jnp.concatenate(
        [shared] + [across(shared, bits) for bits in range(blocks, domains, blocks)], axis=0
    )
    columns = [column] + [across(column, bits) for bits in range(1, blocks)]
    waves, weights, *force_parts = kernel(
        lambda *refs: structure_kernel(
            *refs, group=group, blocks=blocks, charge_count=charge_count, box_x=box_x
        ),
        "structure",
        (
            shaped(domains, 2 * share, atoms, kind=bf16),
            shaped(3 * charge_count, 2 * share),
        )
        + (shaped(3, domains, atoms),) * group,
        (),
        10_000,
        *columns,
        wave_index,
        scalars=(where,),
    )
    force_parts = force_parts[:1] + [across(force_parts[m], m) for m in range(1, group)]
    forces, *grad_parts = kernel(
        lambda *refs: gradient_kernel(
            *refs, group=group, blocks=blocks, charge_count=charge_count, box_x=box_x
        ),
        "gradient",
        (shaped(3, atoms),) + (shaped(charge_count, atoms, kind=bf16),) * group,
        (shaped(3, domains, atoms),),
        5_000,
        *columns,
        *force_parts,
        wave_index,
        waves,
        weights,
        scalars=(where,),
    )
    grad_parts = grad_parts[:1] + [across(grad_parts[m], m) for m in range(1, group)]

    rows = basis_count + width + charge_count + kinds
    rows = -(-rows // (8 * blocks)) * 8
    pieces = kernel(
        lambda *refs: weights_kernel(*refs, group=group, kinds=kinds),
        "weights",
        (shaped(rows, width),) * blocks,
        (shaped(blocks * rows, width),),
        3_000,
        *grad_parts,
        filtered,
        messages,
        before,
        hidden,
        species_row,
        mix_weight,
        charge_rows,
        scalars=(where,),
    )
    piece = summed([pieces[0]] + [across(pieces[r], r) for r in range(1, blocks)])
    piece = summed([piece] + [across(piece, bits) for bits in range(blocks, domains, blocks)])
    pieces = [piece] + [across(piece, r) for r in range(1, blocks)]
    radial_step, mix_step, charge_step, species_step = kernel(
        step_kernel,
        "steps",
        (
            shaped(basis_count, width),
            shaped(width, width),
            shaped(charge_count, width),
            shaped(kinds, charge_count),
        ),
        (shaped(blocks * rows, width),),
        2_000,
        *pieces,
        scalars=(where,),
    )
    return forces, radial_step, mix_step, charge_step.T, species_step


def solution(mesh):
    placed = (
        P(("cell", "dom"), None),
        P(None, ("cell", "dom")),
        P(("cell", "dom"), None),
        P(("cell", "dom")),
        P(None, ("cell", "dom")),
        P(("cell", "dom")),
        P(),
        P(None, ("cell", "dom")),
        P(),
        P(),
        P(),
        P(),
    )
    return jax.shard_map(
        on_device,
        mesh=mesh,
        in_specs=placed,
        out_specs=(
            P(None, ("cell", "dom")),
            P("cell", None),
            P("cell", None),
            P("cell", None),
            P("cell", None),
        ),
        check_vma=False,
    )
```

```python
import math

import jax
import jax.numpy as jnp
import numpy as np
from jax import lax
from jax.experimental import pallas as pl
from jax.experimental.pallas import tpu as pltpu
from jax.sharding import PartitionSpec as P

cutoff_radius = 5.0
kernel_width = 1.0
basis_width = 0.5
box_side = 20.0
two_pi = 6.283185307179586
highest = lax.Precision.HIGHEST
f32 = jnp.float32
bf16 = jnp.bfloat16
spare_vmem = 4 * 1024 * 1024
waves_bytes = 8 * 1024 * 1024
own_vmem = 50 * 1024 * 1024


def fitted(function, degrees, reach):
    nodes = reach * np.cos((np.arange(400) + 0.5) * np.pi / 400)
    powers = np.stack([nodes**d for d in degrees], axis=1)
    return [float(c) for c in np.linalg.lstsq(powers, function(nodes), rcond=None)[0]]


sine_terms = fitted(lambda x: np.sin(np.pi * x), (1, 3, 5, 7, 9), 0.5)
short_sine = fitted(lambda x: np.sin(np.pi * x), (1, 3, 5, 7), 0.5)
short_cosine = fitted(lambda x: np.cos(np.pi * x), (0, 2, 4, 6), 0.5)


def horner(terms, square):
    value = terms[-1]
    for term in terms[-2::-1]:
        value = value * square + term
    return value


def matmul(left, right, precision=None):
    return lax.dot_general(
        left, right, (((1,), (0,)), ((), ())), precision=precision, preferred_element_type=f32
    )


def matmul_nt(left, right, precision=None):
    return lax.dot_general(
        left, right, (((1,), (1,)), ((), ())), precision=precision, preferred_element_type=f32
    )


def turned(value):
    return jnp.transpose(value.astype(f32)).astype(value.dtype)


def sigmoid(value):
    return 1.0 / (1.0 + jnp.exp(-value))


def pieces_of(value):
    first = value.astype(bf16).astype(f32)
    rest = value - first
    second = rest.astype(bf16).astype(f32)
    return first, second, rest - second


def pack_kernel(feat_ref, positions_ref, ghost_ref, packed_ref):
    atoms, width = feat_ref.shape
    packed_ref[0:atoms, :] = feat_ref[...]
    extra = jnp.concatenate(
        pieces_of(positions_ref[...])
        + (ghost_ref[...].astype(f32), jnp.zeros((5, atoms), f32)),
        axis=0,
    ).astype(bf16)
    for part in range(atoms // width):
        first = atoms + part * 16
        packed_ref[first : first + 16, :] = extra[:, part * width : (part + 1) * width]


def pair_blocks(count, coords_ref, own_rows, words_ref, pair_ref, box_x):
    basis_count, _, atoms = pair_ref.shape
    centers = [
        0.5 + (cutoff_radius - 0.5) * float(b) / (basis_count - 1) for b in range(basis_count)
    ]
    scale = -math.log2(math.e) / (basis_width * basis_width)
    middle = basis_count // 2
    gap = centers[1] - centers[0]
    own_x, own_y, own_z = own_rows[0:1, :], own_rows[1:2, :], own_rows[2:3, :]
    step = 32

    def block(index, carry):
        places = pl.ds(pl.multiple_of(index * step, step), step)
        coords = coords_ref[places, :]
        total = jnp.zeros((step, atoms), f32)
        for axis, (mine, length) in enumerate(
            ((own_x, box_x), (own_y, box_side), (own_z, box_side))
        ):
            away = coords[:, axis : axis + 1] - mine
            away = away - length * jnp.floor(away * (1.0 / length) + 0.5)
            total = total + away * away
        distance = jnp.sqrt(total)
        word = words_ref[pl.ds(index, 1), :]
        sublane = lax.broadcasted_iota(jnp.int32, (step, atoms), 0)
        is_live = (jnp.right_shift(jnp.broadcast_to(word, (step, atoms)), sublane) & 1) != 0
        half = jnp.minimum(distance, cutoff_radius) * (1.0 / cutoff_radius) - 0.5
        fade = 0.5 - 0.5 * (half * horner(sine_terms, half * half))
        weight = jnp.where(jnp.logical_and(is_live, distance < cutoff_radius), fade, 0.0)
        offset = jnp.minimum(distance, cutoff_radius) - centers[middle]
        value = jnp.exp2(offset * offset * scale)
        for direction in (1, -1):
            ratio = jnp.exp2(offset * (-2.0 * direction * gap * scale))
            running = value
            for b in range(middle, basis_count) if direction == 1 else range(middle - 1, -1, -1):
                if b != middle:
                    running = running * ratio
                basis = running * math.exp(-(((b - middle) * gap / basis_width) ** 2))
                basis = basis.astype(bf16).astype(f32)
                pair_ref[b, places, :] = (weight * basis).astype(bf16)
        return carry

    lax.fori_loop(0, count // step, block, 0, unroll=8)


def own_kernel(
    feat_ref,
    positions_ref,
    force_ref,
    slots_ref,
    count_ref,
    species_ref,
    radial_ref,
    mix_ref,
    charge_ref,
    offset_ref,
    filtered_ref,
    words_ref,
    own_ref,
    shift_ref,
    weights_ref,
    extra_ref,
    coords_ref,
    pair_ref,
    *,
    box_x,
):
    atoms, width = feat_ref.shape
    slots = slots_ref.shape[0]
    basis_count = radial_ref.shape[0]
    own_rows = positions_ref[...]
    own_feat = turned(feat_ref[...])
    own_ref[...] = own_feat
    coords_ref[...] = jnp.transpose(
        jnp.concatenate([own_rows, jnp.zeros((5, atoms), f32)], axis=0)
    )

    listed = slots_ref[...]
    live = lax.broadcasted_iota(jnp.int32, (slots, atoms), 0) < count_ref[...]
    word_of = jnp.where(live, listed >> 5, -1)
    bit = jnp.left_shift(jnp.ones_like(listed), listed & 31)
    for word in range(words_ref.shape[0]):
        value = jnp.where(word_of == word, bit, 0)
        rows = slots
        while rows > 1:
            rows //= 2
            value = value[:rows] | value[rows:]
        words_ref[word : word + 1, :] = value

    pair_blocks(atoms, coords_ref, own_rows, words_ref, pair_ref, box_x)
    for b in range(basis_count):
        filtered_ref[b] = matmul(own_feat, pair_ref[b])

    kinds = offset_ref.shape[0]
    one_hot = (
        lax.broadcasted_iota(jnp.int32, (kinds, atoms), 0) == species_ref[...]
    ).astype(f32)
    shift_ref[...] = matmul(jnp.transpose(offset_ref[...]), one_hot, highest)
    charge_count = charge_ref.shape[0]
    weights_ref[0:width, :] = jnp.transpose(mix_ref[...].astype(f32))
    weights_ref[width : width + charge_count, :] = charge_ref[...].astype(f32)
    weights_ref[width + charge_count :, 0:basis_count] = jnp.transpose(
        radial_ref[...].astype(f32)
    )
    lengths = (box_x, box_side, box_side)
    turns = jnp.concatenate([own_rows[a : a + 1, :] * (1.0 / lengths[a]) for a in range(3)], axis=0)
    target = force_ref[...]
    high = target.astype(bf16).astype(f32)
    extra_ref[0:16, :] = jnp.concatenate(
        pieces_of(turns) + (high, target - high, jnp.zeros((1, atoms), f32)), axis=0
    )
    extra_ref[16:24, :] = jnp.concatenate([own_rows, jnp.zeros((5, atoms), f32)], axis=0)


def ghost_pairs(ref, is_low, words_ref, extra_ref, ghost_words_ref, coords_ref, pair_ref, box_x):
    _, ghosts, atoms = pair_ref.shape
    width = ref.shape[1]
    extra = jnp.concatenate(
        [ref[atoms + part * 16 : atoms + part * 16 + 16, :] for part in range(atoms // width)],
        axis=1,
    )
    sends = extra[8:16, :].astype(f32)
    sends = jnp.where(is_low, sends[2:3, :], sends[1:2, :])
    site = lax.broadcasted_iota(jnp.int32, (atoms, ghosts), 0).astype(f32)
    chosen = (site == sends).astype(bf16)
    moved = matmul(extra, chosen)
    moved = moved[0:3, :] + (moved[3:6, :] + moved[6:9, :])
    coords_ref[...] = jnp.transpose(jnp.concatenate([moved, jnp.zeros((5, ghosts), f32)], axis=0))
    count = ghosts // 32
    first = jnp.where(is_low, atoms // 32, atoms // 32 + count)
    ghost_words_ref[...] = words_ref[pl.ds(pl.multiple_of(first, 8), count), :]
    pair_blocks(ghosts, coords_ref, extra_ref[16:24, :], ghost_words_ref, pair_ref, box_x)
    return matmul(turned(ref[0:atoms, :]), chosen).astype(bf16)


def near_kernel(
    where_ref,
    near_ref,
    sofar_ref,
    words_ref,
    extra_ref,
    filtered_ref,
    ghost_words_ref,
    coords_ref,
    pair_ref,
    *,
    box_x,
):
    feat = ghost_pairs(
        near_ref,
        where_ref[0] == 1,
        words_ref,
        extra_ref,
        ghost_words_ref,
        coords_ref,
        pair_ref,
        box_x,
    )
    for b in range(filtered_ref.shape[0]):
        filtered_ref[b] = sofar_ref[b] + matmul(feat, pair_ref[b])


def edge_kernel(
    where_ref,
    far_ref,
    sofar_ref,
    words_ref,
    own_ref,
    shift_ref,
    weights_ref,
    extra_ref,
    filtered_ref,
    messages_ref,
    before_ref,
    hidden_ref,
    shared_ref,
    ghost_words_ref,
    coords_ref,
    pair_ref,
    *,
    box_x,
):
    width, atoms = own_ref.shape
    charge_count = shift_ref.shape[0]
    feat = ghost_pairs(
        far_ref,
        where_ref[0] == 0,
        words_ref,
        extra_ref,
        ghost_words_ref,
        coords_ref,
        pair_ref,
        box_x,
    )
    messages = jnp.zeros((width, atoms), f32)
    for b in range(filtered_ref.shape[0]):
        filtered = sofar_ref[b] + matmul(feat, pair_ref[b])
        filtered_ref[b] = filtered
        messages = messages + weights_ref[width + charge_count :, b : b + 1] * filtered
    messages_ref[...] = messages
    before = matmul(weights_ref[0:width, :], messages, highest)
    before_ref[...] = before
    hidden = (own_ref[...].astype(f32) + before * sigmoid(before)).astype(bf16)
    hidden_ref[...] = hidden
    charges = matmul(weights_ref[width : width + charge_count, :].astype(bf16), hidden)
    shared_ref[0, 0:charge_count, :] = (charges + shift_ref[...]).astype(bf16)
    shared_ref[0, charge_count : charge_count + 16, :] = extra_ref[0:16, :].astype(bf16)


def wave_rows(wave_ref, first, count, box_x, total_atoms):
    index = wave_ref[:, pl.ds(first, count)].astype(f32)
    scales = (two_pi / box_x, two_pi / box_side, two_pi / box_side)
    waves = [index[a : a + 1, :] * scales[a] for a in range(3)]
    squares = waves[0] * waves[0] + waves[1] * waves[1] + waves[2] * waves[2]
    damping = jnp.exp(-0.5 * kernel_width * kernel_width * squares) * (1.0 / total_atoms)
    return index, waves, damping


def wave_columns(wave_ref, first, share):
    index = wave_ref[:, pl.ds(first, share)].astype(f32)
    return jnp.transpose(
        jnp.concatenate([index] * 3 + [jnp.zeros((7, share), f32)], axis=0)
    ).astype(bf16)


def fill_waves(columns, shared_ref, j, charge_count, waves_ref, place):
    share = columns.shape[0]
    shift = 12582912.0
    turns = matmul(columns, shared_ref[j, charge_count : charge_count + 16, :])
    turns = turns - ((turns + shift) - shift)
    square = turns * turns
    half_sine = turns * horner(short_sine, square)
    half_cosine = horner(short_cosine, square)
    waves_ref[place, 0:share, :] = (2.0 * half_sine * half_cosine).astype(bf16)
    waves_ref[place, share : 2 * share, :] = (1.0 - 2.0 * half_sine * half_sine).astype(bf16)


def phase_kernel(where_ref, shared_ref, wave_ref, waves_ref, part_ref, *, charge_count):
    count = shared_ref.shape[0]
    share = waves_ref.shape[1] // 2
    columns = wave_columns(wave_ref, pl.multiple_of(where_ref[1] * share, share), share)

    def block(j, carry):
        fill_waves(columns, shared_ref, j, charge_count, waves_ref, j)
        return carry

    lax.fori_loop(0, count, block, 0, unroll=4)
    part = jnp.zeros(part_ref.shape, f32)
    for j in range(count):
        part = part + matmul_nt(shared_ref[j, 0:charge_count, :], waves_ref[j])
    part_ref[...] = part


def structure_kernel(where_ref, *refs, group, blocks, charge_count, box_x):
    shared_refs = refs[:blocks]
    early_ref, part_ref, wave_ref, waves_ref, weights_ref, *force_refs = refs[blocks:]
    count, _, atoms = shared_refs[0].shape
    share = waves_ref.shape[1] // 2
    first = pl.multiple_of(where_ref[1] * share, share)
    _, waves, damping = wave_rows(wave_ref, first, share, box_x, blocks * count * atoms)
    columns = wave_columns(wave_ref, first, share)

    def block(j, carry):
        for r in range(1, blocks):
            fill_waves(
                columns, shared_refs[r], j, charge_count, waves_ref, j * (blocks - 1) + r - 1
            )
        return carry

    lax.fori_loop(0, count, block, 0, unroll=4)
    waves_of = [
        waves_ref.at[j * (blocks - 1) + r - 1] if r else early_ref.at[j]
        for j in range(count)
        for r in range(blocks)
    ]
    structure = part_ref[...]
    for d in range(blocks * count):
        j, r = divmod(d, blocks)
        if r:
            structure = structure + matmul_nt(
                shared_refs[r][j, 0:charge_count, :], waves_of[d][...]
            )
    along_sin = structure[:, :share] * damping
    along_cos = structure[:, share:] * damping
    to_sine = jnp.concatenate([along_cos * waves[a] for a in range(3)], axis=0)
    to_cosine = jnp.concatenate([-along_sin * waves[a] for a in range(3)], axis=0)
    weights = jnp.concatenate([to_sine, to_cosine], axis=1)
    weights_ref[...] = weights
    weights = weights.astype(bf16)
    for d in range(blocks * count):
        j, r = divmod(d, blocks)
        field = matmul(weights, waves_of[d][...])
        charges = shared_refs[r][j, 0:charge_count, :].astype(f32)
        for a in range(3):
            row = jnp.sum(
                field[a * charge_count : (a + 1) * charge_count, :] * charges,
                axis=0,
                keepdims=True,
            )
            for m in range(group):
                force_refs[m][a, d ^ m : (d ^ m) + 1, :] = row


def gradient_kernel(where_ref, *refs, group, blocks, charge_count, box_x):
    shared_refs, part_refs = refs[:blocks], refs[blocks : blocks + group]
    wave_ref, early_ref, waves_ref, weights_ref, forces_ref, *grad_refs, total_ref = refs[
        blocks + group :
    ]
    count, _, atoms = shared_refs[0].shape
    share = waves_ref.shape[1] // 2
    first = pl.multiple_of(where_ref[1] * share, share)
    _, waves, damping = wave_rows(wave_ref, first, share, box_x, blocks * count * atoms)
    waves_of = [
        waves_ref.at[j * (blocks - 1) + r - 1] if r else early_ref.at[j]
        for j in range(count)
        for r in range(blocks)
    ]
    total = part_refs[0][...]
    for m in range(1, group):
        total = total + part_refs[m][...]
    total_ref[...] = total
    for a in range(3):
        forces_ref[a : a + 1, :] = total[a, 0:1, :]

    def errors_of(d):
        j, r = divmod(d, blocks)
        target = shared_refs[r][j, charge_count : charge_count + 16, :].astype(f32)
        target = target[9:12, :] + target[12:15, :]
        return [2.0 * (total_ref[a, d : d + 1, :] - target[a : a + 1, :]) for a in range(3)]

    summed = jnp.zeros((3 * charge_count, 2 * share), f32)
    for d in range(blocks * count):
        j, r = divmod(d, blocks)
        charges = shared_refs[r][j, 0:charge_count, :].astype(f32)
        errors = errors_of(d)
        scaled = jnp.concatenate([errors[a] * charges for a in range(3)], axis=0).astype(bf16)
        summed = summed + matmul_nt(scaled, waves_of[d][...])

    def along(value):
        return sum(
            waves[a] * value[a * charge_count : (a + 1) * charge_count, :] for a in range(3)
        )

    back_cos = damping * along(summed[:, :share])
    back_sin = -damping * along(summed[:, share:])
    back = jnp.concatenate([back_sin, back_cos], axis=1)
    back_high = back.astype(bf16)
    back_low = (back - back_high.astype(f32)).astype(bf16)
    weights = weights_ref[...]
    weights_high = weights.astype(bf16)
    weights_low = (weights - weights_high.astype(f32)).astype(bf16)
    for m in range(group):
        errors = errors_of(m)
        block = waves_of[m][...]
        grad = matmul(back_high, block) + matmul(back_low, block)
        field = matmul(weights_high, block) + matmul(weights_low, block)
        for a in range(3):
            grad = grad + errors[a] * field[a * charge_count : (a + 1) * charge_count, :]
        grad_refs[m][...] = grad.astype(grad_refs[m].dtype)


def weights_kernel(where_ref, *refs, group, kinds):
    part_refs = refs[:group]
    (
        filtered_ref,
        messages_ref,
        before_ref,
        hidden_ref,
        species_ref,
        mix_ref,
        charge_ref,
        *piece_refs,
        packed_ref,
    ) = refs[group:]
    charge_count, atoms = part_refs[0].shape
    basis_count, width, _ = filtered_ref.shape
    grad = part_refs[0][...].astype(f32)
    for m in range(1, group):
        grad = grad + part_refs[m][...].astype(f32)
    before = before_ref[...]
    gate = sigmoid(before)
    upstream = matmul(jnp.transpose(charge_ref[...].astype(f32)), grad, highest)
    before_grad = upstream * (gate * (1.0 + before * (1.0 - gate)))
    message_grad = matmul(mix_ref[...].astype(f32), before_grad, highest)
    columns = [
        jnp.sum(message_grad * filtered_ref[b], axis=1, keepdims=True) for b in range(basis_count)
    ]
    radial = jnp.concatenate(columns, axis=1)
    row = 0
    packed_ref[row : row + basis_count, :] = jnp.transpose(radial)
    row += basis_count
    packed_ref[row : row + width, :] = matmul_nt(messages_ref[...], before_grad, highest)
    row += width
    packed_ref[row : row + charge_count, :] = matmul_nt(
        grad, hidden_ref[...].astype(f32), highest
    )
    row += charge_count
    packed_ref[row:, :] = jnp.zeros((packed_ref.shape[0] - row, width), f32)
    one_hot = (
        lax.broadcasted_iota(jnp.int32, (kinds, atoms), 0) == species_ref[...]
    ).astype(f32)
    packed_ref[row : row + kinds, 0:charge_count] = matmul_nt(one_hot, grad, highest)
    count = piece_refs[0].shape[0]
    for r, ref in enumerate(piece_refs):
        ref[...] = packed_ref[pl.ds(pl.multiple_of((where_ref[2] ^ r) * count, 8), count), :]


def step_kernel(where_ref, *refs):
    *piece_refs, radial_ref, mix_ref, charge_ref, species_ref, total_ref = refs
    basis_count, width = radial_ref.shape
    charge_count = charge_ref.shape[0]
    kinds = species_ref.shape[0]

    count = piece_refs[0].shape[0]
    for r, ref in enumerate(piece_refs):
        total_ref[pl.ds(pl.multiple_of((where_ref[2] ^ r) * count, 8), count), :] = ref[...]

    def normalized(gradient):
        mean = jnp.sum(gradient * gradient, keepdims=True) * (1.0 / gradient.size)
        return gradient * lax.rsqrt(mean + 1e-06)

    row = 0
    radial_ref[...] = normalized(total_ref[row : row + basis_count, :])
    row += basis_count
    mix_ref[...] = normalized(total_ref[row : row + width, :])
    row += width
    charge_ref[...] = normalized(total_ref[row : row + charge_count, :])
    row += charge_count
    species_ref[...] = normalized(total_ref[row : row + kinds, 0:charge_count])


def shaped(*dims, kind=f32):
    return jax.ShapeDtypeStruct(dims, kind)


def kernel(body, name, out_shape, scratch, nanoseconds, *operands, scalars=(), wanted=0):
    outs = out_shape if isinstance(out_shape, tuple) else (out_shape,)
    held = sum(math.prod(x.shape) * x.dtype.itemsize for x in (*outs, *scratch, *operands))
    in_vmem = pl.BlockSpec(memory_space=pltpu.VMEM)
    in_smem = pl.BlockSpec(memory_space=pltpu.SMEM)
    return pl.pallas_call(
        body,
        out_shape=out_shape,
        in_specs=[in_smem] * len(scalars) + [in_vmem] * len(operands),
        out_specs=tuple(in_vmem for _ in outs) if isinstance(out_shape, tuple) else in_vmem,
        scratch_shapes=[pltpu.VMEM(x.shape, x.dtype) for x in scratch],
        compiler_params=pltpu.CompilerParams(vmem_limit_bytes=max(held + spare_vmem, wanted)),
        cost_estimate=pl.CostEstimate(
            flops=nanoseconds * 1_000_000, bytes_accessed=held, transcendentals=0
        ),
        name=name,
    )(*scalars, *operands)


def across(value, bits):
    domains = lax.axis_size("dom")
    return lax.ppermute(value, "dom", [(i, i ^ bits) for i in range(domains)])


def summed(values):
    while len(values) > 1:
        values = [values[i] + values[i + 1] for i in range(0, len(values), 2)]
    return values[0]


def on_device(
    features,
    positions,
    neighbours,
    neighbour_count,
    ghost_sends,
    species,
    wave_index,
    force_ref,
    radial_weight,
    mix_weight,
    charge_weight,
    species_charge,
):
    atoms, width = features.shape
    basis_count = radial_weight.shape[0]
    charge_count = charge_weight.shape[1]
    kinds = species_charge.shape[0]
    wave_count = wave_index.shape[1]
    domains = lax.axis_size("dom")
    box_x = 1.25 * (atoms * domains) / 64
    group = 2 if domains % 2 == 0 else 1
    while (
        group < domains
        and 4 * wave_count // group * atoms * domains > waves_bytes
        and wave_count % (256 * group) == 0
    ):
        group *= 2
    share = wave_count // group
    entries = atoms + 2 * ghost_sends.shape[1]

    me = lax.axis_index("dom")
    blocks = 4 if domains % 4 == 0 else 2
    where = jnp.stack([me % 2, me % group, me % blocks]).astype(jnp.int32)
    packed = kernel(
        pack_kernel,
        "pack",
        shaped(atoms + 16 * (atoms // width), width, kind=bf16),
        (),
        1_000,
        features,
        positions,
        ghost_sends,
        wanted=60 * 1024 * 1024,
    )
    near = across(packed, 1)
    beyond = [(i, (i + 1 if i % 2 else i - 1) % domains) for i in range(domains)]
    far = lax.ppermute(packed, "dom", beyond)
    species_row = species[None, :]
    slots = neighbours.T
    charge_rows = charge_weight.T

    sofar, words, *local, extra = kernel(
        lambda *refs: own_kernel(*refs, box_x=box_x),
        "own",
        (
            shaped(basis_count, width, atoms),
            shaped(entries // 32, atoms, kind=jnp.int32),
            shaped(width, atoms, kind=bf16),
            shaped(charge_count, atoms),
            shaped(2 * width + charge_count, width),
            shaped(24, atoms),
        ),
        (
            shaped(atoms, 8),
            shaped(basis_count, atoms, atoms, kind=bf16),
        ),
        4_000,
        features,
        positions,
        force_ref,
        slots,
        neighbour_count[None, :],
        species_row,
        radial_weight,
        mix_weight,
        charge_rows,
        species_charge,
        wanted=own_vmem,
    )
    ghosts = ghost_sends.shape[1]
    scratch = (
        shaped(ghosts // 32, atoms, kind=jnp.int32),
        shaped(ghosts, 8),
        shaped(basis_count, ghosts, atoms, kind=bf16),
    )
    sofar = kernel(
        lambda *refs: near_kernel(*refs, box_x=box_x),
        "near",
        shaped(basis_count, width, atoms),
        scratch,
        3_000,
        near,
        sofar,
        words,
        extra,
        scalars=(where,),
    )
    filtered, messages, before, hidden, shared = kernel(
        lambda *refs: edge_kernel(*refs, box_x=box_x),
        "edges",
        (
            shaped(basis_count, width, atoms),
            shaped(width, atoms),
            shaped(width, atoms),
            shaped(width, atoms, kind=bf16),
            shaped(1, charge_count + 16, atoms, kind=bf16),
        ),
        scratch,
        4_000,
        far,
        sofar,
        words,
        *local,
        extra,
        scalars=(where,),
    )
    column = jnp.concatenate(
        [shared] + [across(shared, bits) for bits in range(blocks, domains, blocks)], axis=0
    )
    columns = [column] + [across(column, bits) for bits in range(1, blocks)]
    early, part = kernel(
        lambda *refs: phase_kernel(*refs, charge_count=charge_count),
        "phases",
        (
            shaped(domains // blocks, 2 * share, atoms, kind=bf16),
            shaped(charge_count, 2 * share),
        ),
        (),
        3_000,
        column,
        wave_index,
        scalars=(where,),
    )
    waves, weights, *force_parts = kernel(
        lambda *refs: structure_kernel(
            *refs, group=group, blocks=blocks, charge_count=charge_count, box_x=box_x
        ),
        "structure",
        (
            shaped(domains - domains // blocks, 2 * share, atoms, kind=bf16),
            shaped(3 * charge_count, 2 * share),
        )
        + (shaped(3, domains, atoms),) * group,
        (),
        8_000,
        *columns,
        early,
        part,
        wave_index,
        scalars=(where,),
    )
    force_parts = force_parts[:1] + [across(force_parts[m], m) for m in range(1, group)]
    forces, *grad_parts = kernel(
        lambda *refs: gradient_kernel(
            *refs, group=group, blocks=blocks, charge_count=charge_count, box_x=box_x
        ),
        "gradient",
        (shaped(3, atoms),) + (shaped(charge_count, atoms, kind=bf16),) * group,
        (shaped(3, domains, atoms),),
        5_000,
        *columns,
        *force_parts,
        wave_index,
        early,
        waves,
        weights,
        scalars=(where,),
    )
    grad_parts = grad_parts[:1] + [across(grad_parts[m], m) for m in range(1, group)]

    rows = basis_count + width + charge_count + kinds
    rows = -(-rows // (8 * blocks)) * 8
    pieces = kernel(
        lambda *refs: weights_kernel(*refs, group=group, kinds=kinds),
        "weights",
        (shaped(rows, width),) * blocks,
        (shaped(blocks * rows, width),),
        3_000,
        *grad_parts,
        filtered,
        messages,
        before,
        hidden,
        species_row,
        mix_weight,
        charge_rows,
        scalars=(where,),
    )
    piece = summed([pieces[0]] + [across(pieces[r], r) for r in range(1, blocks)])
    piece = summed([piece] + [across(piece, bits) for bits in range(blocks, domains, blocks)])
    pieces = [piece] + [across(piece, r) for r in range(1, blocks)]
    radial_step, mix_step, charge_step, species_step = kernel(
        step_kernel,
        "steps",
        (
            shaped(basis_count, width),
            shaped(width, width),
            shaped(charge_count, width),
            shaped(kinds, charge_count),
        ),
        (shaped(blocks * rows, width),),
        2_000,
        *pieces,
        scalars=(where,),
    )
    return forces, radial_step, mix_step, charge_step.T, species_step


def solution(mesh):
    placed = (
        P(("cell", "dom"), None),
        P(None, ("cell", "dom")),
        P(("cell", "dom"), None),
        P(("cell", "dom")),
        P(None, ("cell", "dom")),
        P(("cell", "dom")),
        P(),
        P(None, ("cell", "dom")),
        P(),
        P(),
        P(),
        P(),
    )
    return jax.shard_map(
        on_device,
        mesh=mesh,
        in_specs=placed,
        out_specs=(
            P(None, ("cell", "dom")),
            P("cell", None),
            P("cell", None),
            P("cell", None),
            P("cell", None),
        ),
        check_vma=False,
    )
```

```python
import math

import jax
import jax.numpy as jnp
import numpy as np
from jax import lax
from jax.experimental import pallas as pl
from jax.experimental.pallas import tpu as pltpu
from jax.sharding import PartitionSpec as P

cutoff_radius = 5.0
kernel_width = 1.0
basis_width = 0.5
box_side = 20.0
two_pi = 6.283185307179586
highest = lax.Precision.HIGHEST
f32 = jnp.float32
bf16 = jnp.bfloat16
spare_vmem = 4 * 1024 * 1024
waves_bytes = 8 * 1024 * 1024
own_vmem = 50 * 1024 * 1024


def fitted(function, degrees, reach):
    nodes = reach * np.cos((np.arange(400) + 0.5) * np.pi / 400)
    powers = np.stack([nodes**d for d in degrees], axis=1)
    return [float(c) for c in np.linalg.lstsq(powers, function(nodes), rcond=None)[0]]


sine_terms = fitted(lambda x: np.sin(np.pi * x), (1, 3, 5, 7, 9), 0.5)
short_sine = fitted(lambda x: np.sin(np.pi * x), (1, 3, 5, 7), 0.5)
short_cosine = fitted(lambda x: np.cos(np.pi * x), (0, 2, 4, 6), 0.5)


def horner(terms, square):
    value = terms[-1]
    for term in terms[-2::-1]:
        value = value * square + term
    return value


def matmul(left, right, precision=None):
    return lax.dot_general(
        left, right, (((1,), (0,)), ((), ())), precision=precision, preferred_element_type=f32
    )


def matmul_nt(left, right, precision=None):
    return lax.dot_general(
        left, right, (((1,), (1,)), ((), ())), precision=precision, preferred_element_type=f32
    )


def turned(value):
    return jnp.transpose(value.astype(f32)).astype(value.dtype)


def sigmoid(value):
    return 1.0 / (1.0 + jnp.exp(-value))


def pieces_of(value):
    first = value.astype(bf16).astype(f32)
    rest = value - first
    second = rest.astype(bf16).astype(f32)
    return first, second, rest - second


def pack_kernel(feat_ref, positions_ref, ghost_ref, packed_ref):
    atoms, width = feat_ref.shape
    packed_ref[0:atoms, :] = feat_ref[...]
    extra = jnp.concatenate(
        pieces_of(positions_ref[...])
        + (ghost_ref[...].astype(f32), jnp.zeros((5, atoms), f32)),
        axis=0,
    ).astype(bf16)
    for part in range(atoms // width):
        first = atoms + part * 16
        packed_ref[first : first + 16, :] = extra[:, part * width : (part + 1) * width]


def pair_blocks(count, coords_ref, own_rows, words_ref, pair_ref, box_x):
    basis_count, _, atoms = pair_ref.shape
    centers = [
        0.5 + (cutoff_radius - 0.5) * float(b) / (basis_count - 1) for b in range(basis_count)
    ]
    scale = -math.log2(math.e) / (basis_width * basis_width)
    middle = basis_count // 2
    gap = centers[1] - centers[0]
    own_x, own_y, own_z = own_rows[0:1, :], own_rows[1:2, :], own_rows[2:3, :]
    step = 32

    def block(index, carry):
        places = pl.ds(pl.multiple_of(index * step, step), step)
        coords = coords_ref[places, :]
        total = jnp.zeros((step, atoms), f32)
        for axis, (mine, length) in enumerate(
            ((own_x, box_x), (own_y, box_side), (own_z, box_side))
        ):
            away = coords[:, axis : axis + 1] - mine
            away = away - length * jnp.floor(away * (1.0 / length) + 0.5)
            total = total + away * away
        distance = jnp.sqrt(total)
        word = words_ref[pl.ds(index, 1), :]
        sublane = lax.broadcasted_iota(jnp.int32, (step, atoms), 0)
        is_live = (jnp.right_shift(jnp.broadcast_to(word, (step, atoms)), sublane) & 1) != 0
        half = jnp.minimum(distance, cutoff_radius) * (1.0 / cutoff_radius) - 0.5
        fade = 0.5 - 0.5 * (half * horner(sine_terms, half * half))
        weight = jnp.where(jnp.logical_and(is_live, distance < cutoff_radius), fade, 0.0)
        offset = jnp.minimum(distance, cutoff_radius) - centers[middle]
        value = jnp.exp2(offset * offset * scale)
        for direction in (1, -1):
            ratio = jnp.exp2(offset * (-2.0 * direction * gap * scale))
            running = value
            for b in range(middle, basis_count) if direction == 1 else range(middle - 1, -1, -1):
                if b != middle:
                    running = running * ratio
                basis = running * math.exp(-(((b - middle) * gap / basis_width) ** 2))
                basis = basis.astype(bf16).astype(f32)
                pair_ref[b, places, :] = (weight * basis).astype(bf16)
        return carry

    lax.fori_loop(0, count // step, block, 0, unroll=8)


def own_kernel(
    feat_ref,
    positions_ref,
    force_ref,
    slots_ref,
    count_ref,
    species_ref,
    radial_ref,
    mix_ref,
    charge_ref,
    offset_ref,
    filtered_ref,
    words_ref,
    own_ref,
    shift_ref,
    weights_ref,
    extra_ref,
    coords_ref,
    pair_ref,
    *,
    box_x,
):
    atoms, width = feat_ref.shape
    slots = slots_ref.shape[0]
    basis_count = radial_ref.shape[0]
    own_rows = positions_ref[...]
    own_feat = turned(feat_ref[...])
    own_ref[...] = own_feat
    coords_ref[...] = jnp.transpose(
        jnp.concatenate([own_rows, jnp.zeros((5, atoms), f32)], axis=0)
    )

    listed = slots_ref[...]
    live = lax.broadcasted_iota(jnp.int32, (slots, atoms), 0) < count_ref[...]
    word_of = jnp.where(live, listed >> 5, -1)
    bit = jnp.left_shift(jnp.ones_like(listed), listed & 31)
    for word in range(words_ref.shape[0]):
        value = jnp.where(word_of == word, bit, 0)
        rows = slots
        while rows > 1:
            rows //= 2
            value = value[:rows] | value[rows:]
        words_ref[word : word + 1, :] = value

    pair_blocks(atoms, coords_ref, own_rows, words_ref, pair_ref, box_x)
    for b in range(basis_count):
        filtered_ref[b] = matmul(own_feat, pair_ref[b])

    kinds = offset_ref.shape[0]
    one_hot = (
        lax.broadcasted_iota(jnp.int32, (kinds, atoms), 0) == species_ref[...]
    ).astype(f32)
    shift_ref[...] = matmul(jnp.transpose(offset_ref[...]), one_hot, highest)
    charge_count = charge_ref.shape[0]
    weights_ref[0:width, :] = jnp.transpose(mix_ref[...].astype(f32))
    weights_ref[width : width + charge_count, :] = charge_ref[...].astype(f32)
    weights_ref[width + charge_count :, 0:basis_count] = jnp.transpose(
        radial_ref[...].astype(f32)
    )
    lengths = (box_x, box_side, box_side)
    turns = jnp.concatenate([own_rows[a : a + 1, :] * (1.0 / lengths[a]) for a in range(3)], axis=0)
    target = force_ref[...]
    high = target.astype(bf16).astype(f32)
    extra_ref[0:16, :] = jnp.concatenate(
        pieces_of(turns) + (high, target - high, jnp.zeros((1, atoms), f32)), axis=0
    )
    extra_ref[16:24, :] = jnp.concatenate([own_rows, jnp.zeros((5, atoms), f32)], axis=0)


def ghost_pairs(ref, is_low, words_ref, extra_ref, ghost_words_ref, coords_ref, pair_ref, box_x):
    _, ghosts, atoms = pair_ref.shape
    width = ref.shape[1]
    extra = jnp.concatenate(
        [ref[atoms + part * 16 : atoms + part * 16 + 16, :] for part in range(atoms // width)],
        axis=1,
    )
    sends = extra[8:16, :].astype(f32)
    sends = jnp.where(is_low, sends[2:3, :], sends[1:2, :])
    site = lax.broadcasted_iota(jnp.int32, (atoms, ghosts), 0).astype(f32)
    chosen = (site == sends).astype(bf16)
    moved = matmul(extra, chosen)
    moved = moved[0:3, :] + (moved[3:6, :] + moved[6:9, :])
    coords_ref[...] = jnp.transpose(jnp.concatenate([moved, jnp.zeros((5, ghosts), f32)], axis=0))
    count = ghosts // 32
    first = jnp.where(is_low, atoms // 32, atoms // 32 + count)
    ghost_words_ref[...] = words_ref[pl.ds(pl.multiple_of(first, 8), count), :]
    pair_blocks(ghosts, coords_ref, extra_ref[16:24, :], ghost_words_ref, pair_ref, box_x)
    return matmul(turned(ref[0:atoms, :]), chosen).astype(bf16)


def near_kernel(
    where_ref,
    near_ref,
    sofar_ref,
    words_ref,
    extra_ref,
    filtered_ref,
    ghost_words_ref,
    coords_ref,
    pair_ref,
    *,
    box_x,
):
    feat = ghost_pairs(
        near_ref,
        where_ref[0] == 1,
        words_ref,
        extra_ref,
        ghost_words_ref,
        coords_ref,
        pair_ref,
        box_x,
    )
    for b in range(filtered_ref.shape[0]):
        filtered_ref[b] = sofar_ref[b] + matmul(feat, pair_ref[b])


def edge_kernel(
    where_ref,
    far_ref,
    sofar_ref,
    words_ref,
    own_ref,
    shift_ref,
    weights_ref,
    extra_ref,
    filtered_ref,
    messages_ref,
    before_ref,
    hidden_ref,
    shared_ref,
    ghost_words_ref,
    coords_ref,
    pair_ref,
    *,
    box_x,
):
    width, atoms = own_ref.shape
    charge_count = shift_ref.shape[0]
    feat = ghost_pairs(
        far_ref,
        where_ref[0] == 0,
        words_ref,
        extra_ref,
        ghost_words_ref,
        coords_ref,
        pair_ref,
        box_x,
    )
    messages = jnp.zeros((width, atoms), f32)
    for b in range(filtered_ref.shape[0]):
        filtered = sofar_ref[b] + matmul(feat, pair_ref[b])
        filtered_ref[b] = filtered
        messages = messages + weights_ref[width + charge_count :, b : b + 1] * filtered
    messages_ref[...] = messages
    before = matmul(weights_ref[0:width, :], messages, highest)
    before_ref[...] = before
    hidden = (own_ref[...].astype(f32) + before * sigmoid(before)).astype(bf16)
    hidden_ref[...] = hidden
    charges = matmul(weights_ref[width : width + charge_count, :].astype(bf16), hidden)
    shared_ref[0, 0:charge_count, :] = (charges + shift_ref[...]).astype(bf16)
    shared_ref[0, charge_count : charge_count + 16, :] = extra_ref[0:16, :].astype(bf16)


def wave_rows(wave_ref, first, count, box_x, total_atoms):
    index = wave_ref[:, pl.ds(first, count)].astype(f32)
    scales = (two_pi / box_x, two_pi / box_side, two_pi / box_side)
    waves = [index[a : a + 1, :] * scales[a] for a in range(3)]
    squares = waves[0] * waves[0] + waves[1] * waves[1] + waves[2] * waves[2]
    damping = jnp.exp(-0.5 * kernel_width * kernel_width * squares) * (1.0 / total_atoms)
    return index, waves, damping


def wave_columns(wave_ref, first, share):
    index = wave_ref[:, pl.ds(first, share)].astype(f32)
    return jnp.transpose(
        jnp.concatenate([index] * 3 + [jnp.zeros((7, share), f32)], axis=0)
    ).astype(bf16)


def fill_waves(columns, shared_ref, j, charge_count, waves_ref, place):
    share = columns.shape[0]
    shift = 12582912.0
    turns = matmul(columns, shared_ref[j, charge_count : charge_count + 16, :])
    turns = turns - ((turns + shift) - shift)
    square = turns * turns
    half_sine = turns * horner(short_sine, square)
    half_cosine = horner(short_cosine, square)
    waves_ref[place, 0:share, :] = (2.0 * half_sine * half_cosine).astype(bf16)
    waves_ref[place, share : 2 * share, :] = (1.0 - 2.0 * half_sine * half_sine).astype(bf16)


def phase_kernel(where_ref, shared_ref, wave_ref, waves_ref, part_ref, *, charge_count):
    count = shared_ref.shape[0]
    share = waves_ref.shape[1] // 2
    columns = wave_columns(wave_ref, pl.multiple_of(where_ref[1] * share, share), share)

    def block(j, carry):
        fill_waves(columns, shared_ref, j, charge_count, waves_ref, j)
        return carry

    lax.fori_loop(0, count, block, 0, unroll=4)
    part = jnp.zeros(part_ref.shape, f32)
    for j in range(count):
        part = part + matmul_nt(shared_ref[j, 0:charge_count, :], waves_ref[j])
    part_ref[...] = part


def placed_waves(early, early_refs, late, waves_ref, count):
    return [
        early_refs[early.index(r)].at[j]
        if r in early
        else waves_ref.at[j * len(late) + late.index(r)]
        for j in range(count)
        for r in range(len(early) + len(late))
    ]


def structure_kernel(where_ref, *refs, group, blocks, early, charge_count, box_x):
    shared_refs, early_refs = refs[:blocks], refs[blocks : blocks + len(early)]
    part_refs, refs = refs[blocks + len(early) : blocks + 2 * len(early)], refs[blocks + 2 * len(early) :]
    wave_ref, waves_ref, weights_ref, *force_refs = refs
    late = [r for r in range(blocks) if r not in early]
    count, _, atoms = shared_refs[0].shape
    share = waves_ref.shape[1] // 2
    first = pl.multiple_of(where_ref[1] * share, share)
    _, waves, damping = wave_rows(wave_ref, first, share, box_x, blocks * count * atoms)
    columns = wave_columns(wave_ref, first, share)

    def block(j, carry):
        for i, r in enumerate(late):
            fill_waves(columns, shared_refs[r], j, charge_count, waves_ref, j * len(late) + i)
        return carry

    lax.fori_loop(0, count, block, 0, unroll=4)
    waves_of = placed_waves(early, early_refs, late, waves_ref, count)
    structure = sum(ref[...] for ref in part_refs)
    for d in range(blocks * count):
        j, r = divmod(d, blocks)
        if r in late:
            structure = structure + matmul_nt(
                shared_refs[r][j, 0:charge_count, :], waves_of[d][...]
            )
    along_sin = structure[:, :share] * damping
    along_cos = structure[:, share:] * damping
    to_sine = jnp.concatenate([along_cos * waves[a] for a in range(3)], axis=0)
    to_cosine = jnp.concatenate([-along_sin * waves[a] for a in range(3)], axis=0)
    weights = jnp.concatenate([to_sine, to_cosine], axis=1)
    weights_ref[...] = weights
    weights = weights.astype(bf16)
    for d in range(blocks * count):
        j, r = divmod(d, blocks)
        field = matmul(weights, waves_of[d][...])
        charges = shared_refs[r][j, 0:charge_count, :].astype(f32)
        for a in range(3):
            row = jnp.sum(
                field[a * charge_count : (a + 1) * charge_count, :] * charges,
                axis=0,
                keepdims=True,
            )
            for m in range(group):
                force_refs[m][a, d ^ m : (d ^ m) + 1, :] = row


def gradient_kernel(where_ref, *refs, group, blocks, early, charge_count, box_x):
    shared_refs, part_refs = refs[:blocks], refs[blocks : blocks + group]
    refs = refs[blocks + group :]
    early_refs, refs = refs[: len(early)], refs[len(early) :]
    wave_ref, waves_ref, weights_ref, forces_ref, *grad_refs, total_ref = refs
    late = [r for r in range(blocks) if r not in early]
    count, _, atoms = shared_refs[0].shape
    share = waves_ref.shape[1] // 2
    first = pl.multiple_of(where_ref[1] * share, share)
    _, waves, damping = wave_rows(wave_ref, first, share, box_x, blocks * count * atoms)
    waves_of = placed_waves(early, early_refs, late, waves_ref, count)
    total = part_refs[0][...]
    for m in range(1, group):
        total = total + part_refs[m][...]
    total_ref[...] = total
    for a in range(3):
        forces_ref[a : a + 1, :] = total[a, 0:1, :]

    def errors_of(d):
        j, r = divmod(d, blocks)
        target = shared_refs[r][j, charge_count : charge_count + 16, :].astype(f32)
        target = target[9:12, :] + target[12:15, :]
        return [2.0 * (total_ref[a, d : d + 1, :] - target[a : a + 1, :]) for a in range(3)]

    summed = jnp.zeros((3 * charge_count, 2 * share), f32)
    for d in range(blocks * count):
        j, r = divmod(d, blocks)
        charges = shared_refs[r][j, 0:charge_count, :].astype(f32)
        errors = errors_of(d)
        scaled = jnp.concatenate([errors[a] * charges for a in range(3)], axis=0).astype(bf16)
        summed = summed + matmul_nt(scaled, waves_of[d][...])

    def along(value):
        return sum(
            waves[a] * value[a * charge_count : (a + 1) * charge_count, :] for a in range(3)
        )

    back_cos = damping * along(summed[:, :share])
    back_sin = -damping * along(summed[:, share:])
    back = jnp.concatenate([back_sin, back_cos], axis=1)
    back_high = back.astype(bf16)
    back_low = (back - back_high.astype(f32)).astype(bf16)
    weights = weights_ref[...]
    weights_high = weights.astype(bf16)
    weights_low = (weights - weights_high.astype(f32)).astype(bf16)
    for m in range(group):
        errors = errors_of(m)
        block = waves_of[m][...]
        grad = matmul(back_high, block) + matmul(back_low, block)
        field = matmul(weights_high, block) + matmul(weights_low, block)
        for a in range(3):
            grad = grad + errors[a] * field[a * charge_count : (a + 1) * charge_count, :]
        grad_refs[m][...] = grad.astype(grad_refs[m].dtype)


def weights_kernel(*refs, group, kinds):
    part_refs = refs[:group]
    (
        filtered_ref,
        messages_ref,
        before_ref,
        hidden_ref,
        species_ref,
        mix_ref,
        charge_ref,
        packed_ref,
    ) = refs[group:]
    charge_count, atoms = part_refs[0].shape
    basis_count, width, _ = filtered_ref.shape
    grad = part_refs[0][...].astype(f32)
    for m in range(1, group):
        grad = grad + part_refs[m][...].astype(f32)
    before = before_ref[...]
    gate = sigmoid(before)
    upstream = matmul(jnp.transpose(charge_ref[...].astype(f32)), grad, highest)
    before_grad = upstream * (gate * (1.0 + before * (1.0 - gate)))
    message_grad = matmul(mix_ref[...].astype(f32), before_grad, highest)
    columns = [
        jnp.sum(message_grad * filtered_ref[b], axis=1, keepdims=True) for b in range(basis_count)
    ]
    radial = jnp.concatenate(columns, axis=1)
    row = 0
    packed_ref[row : row + basis_count, :] = jnp.transpose(radial)
    row += basis_count
    packed_ref[row : row + width, :] = matmul_nt(messages_ref[...], before_grad, highest)
    row += width
    packed_ref[row : row + charge_count, :] = matmul_nt(
        grad, hidden_ref[...].astype(f32), highest
    )
    row += charge_count
    packed_ref[row:, :] = jnp.zeros((packed_ref.shape[0] - row, width), f32)
    one_hot = (
        lax.broadcasted_iota(jnp.int32, (kinds, atoms), 0) == species_ref[...]
    ).astype(f32)
    packed_ref[row : row + kinds, 0:charge_count] = matmul_nt(one_hot, grad, highest)


def summed(values):
    while len(values) > 1:
        values = [values[i] + values[i + 1] for i in range(0, len(values), 2)]
    return values[0]


def step_kernel(*refs):
    *total_refs, radial_ref, mix_ref, charge_ref, species_ref, total_ref = refs
    basis_count, width = radial_ref.shape
    charge_count = charge_ref.shape[0]
    kinds = species_ref.shape[0]
    total_ref[...] = summed([ref[...] for ref in total_refs])

    def normalized(gradient):
        mean = jnp.sum(gradient * gradient, keepdims=True) * (1.0 / gradient.size)
        return gradient * lax.rsqrt(mean + 1e-06)

    row = 0
    radial_ref[...] = normalized(total_ref[row : row + basis_count, :])
    row += basis_count
    mix_ref[...] = normalized(total_ref[row : row + width, :])
    row += width
    charge_ref[...] = normalized(total_ref[row : row + charge_count, :])
    row += charge_count
    species_ref[...] = normalized(total_ref[row : row + kinds, 0:charge_count])


def shaped(*dims, kind=f32):
    return jax.ShapeDtypeStruct(dims, kind)


def kernel(body, name, out_shape, scratch, nanoseconds, *operands, scalars=(), wanted=0):
    outs = out_shape if isinstance(out_shape, tuple) else (out_shape,)
    held = sum(math.prod(x.shape) * x.dtype.itemsize for x in (*outs, *scratch, *operands))
    in_vmem = pl.BlockSpec(memory_space=pltpu.VMEM)
    in_smem = pl.BlockSpec(memory_space=pltpu.SMEM)
    return pl.pallas_call(
        body,
        out_shape=out_shape,
        in_specs=[in_smem] * len(scalars) + [in_vmem] * len(operands),
        out_specs=tuple(in_vmem for _ in outs) if isinstance(out_shape, tuple) else in_vmem,
        scratch_shapes=[pltpu.VMEM(x.shape, x.dtype) for x in scratch],
        compiler_params=pltpu.CompilerParams(vmem_limit_bytes=max(held + spare_vmem, wanted)),
        cost_estimate=pl.CostEstimate(
            flops=nanoseconds * 1_000_000, bytes_accessed=held, transcendentals=0
        ),
        name=name,
    )(*scalars, *operands)


def across(value, bits):
    domains = lax.axis_size("dom")
    return lax.ppermute(value, "dom", [(i, i ^ bits) for i in range(domains)])


def on_device(
    features,
    positions,
    neighbours,
    neighbour_count,
    ghost_sends,
    species,
    wave_index,
    force_ref,
    radial_weight,
    mix_weight,
    charge_weight,
    species_charge,
):
    atoms, width = features.shape
    basis_count = radial_weight.shape[0]
    charge_count = charge_weight.shape[1]
    kinds = species_charge.shape[0]
    wave_count = wave_index.shape[1]
    domains = lax.axis_size("dom")
    box_x = 1.25 * (atoms * domains) / 64
    group = 2 if domains % 2 == 0 else 1
    while (
        group < domains
        and 4 * wave_count // group * atoms * domains > waves_bytes
        and wave_count % (256 * group) == 0
    ):
        group *= 2
    share = wave_count // group
    entries = atoms + 2 * ghost_sends.shape[1]

    me = lax.axis_index("dom")
    blocks = 4 if domains % 4 == 0 else 2
    where = jnp.stack([me % 2, me % group, me % blocks]).astype(jnp.int32)
    packed = kernel(
        pack_kernel,
        "pack",
        shaped(atoms + 16 * (atoms // width), width, kind=bf16),
        (),
        1_000,
        features,
        positions,
        ghost_sends,
        wanted=60 * 1024 * 1024,
    )
    near = across(packed, 1)
    beyond = [(i, (i + 1 if i % 2 else i - 1) % domains) for i in range(domains)]
    far = lax.ppermute(packed, "dom", beyond)
    species_row = species[None, :]
    slots = neighbours.T
    charge_rows = charge_weight.T

    sofar, words, *local, extra = kernel(
        lambda *refs: own_kernel(*refs, box_x=box_x),
        "own",
        (
            shaped(basis_count, width, atoms),
            shaped(entries // 32, atoms, kind=jnp.int32),
            shaped(width, atoms, kind=bf16),
            shaped(charge_count, atoms),
            shaped(2 * width + charge_count, width),
            shaped(24, atoms),
        ),
        (
            shaped(atoms, 8),
            shaped(basis_count, atoms, atoms, kind=bf16),
        ),
        4_000,
        features,
        positions,
        force_ref,
        slots,
        neighbour_count[None, :],
        species_row,
        radial_weight,
        mix_weight,
        charge_rows,
        species_charge,
        wanted=own_vmem,
    )
    ghosts = ghost_sends.shape[1]
    scratch = (
        shaped(ghosts // 32, atoms, kind=jnp.int32),
        shaped(ghosts, 8),
        shaped(basis_count, ghosts, atoms, kind=bf16),
    )
    sofar = kernel(
        lambda *refs: near_kernel(*refs, box_x=box_x),
        "near",
        shaped(basis_count, width, atoms),
        scratch,
        3_000,
        near,
        sofar,
        words,
        extra,
        scalars=(where,),
    )
    filtered, messages, before, hidden, shared = kernel(
        lambda *refs: edge_kernel(*refs, box_x=box_x),
        "edges",
        (
            shaped(basis_count, width, atoms),
            shaped(width, atoms),
            shaped(width, atoms),
            shaped(width, atoms, kind=bf16),
            shaped(1, charge_count + 16, atoms, kind=bf16),
        ),
        scratch,
        4_000,
        far,
        sofar,
        words,
        *local,
        extra,
        scalars=(where,),
    )
    column = jnp.concatenate(
        [shared] + [across(shared, bits) for bits in range(blocks, domains, blocks)], axis=0
    )
    columns = [column] + [across(column, bits) for bits in range(1, blocks)]
    early = (0, blocks - 1) if blocks > 2 else (0,)
    waves_early, parts = zip(
        *[
            kernel(
                lambda *refs: phase_kernel(*refs, charge_count=charge_count),
                "phases",
                (
                    shaped(domains // blocks, 2 * share, atoms, kind=bf16),
                    shaped(charge_count, 2 * share),
                ),
                (),
                3_000,
                columns[r],
                wave_index,
                scalars=(where,),
            )
            for r in early
        ]
    )
    waves, weights, *force_parts = kernel(
        lambda *refs: structure_kernel(
            *refs, group=group, blocks=blocks, early=early, charge_count=charge_count, box_x=box_x
        ),
        "structure",
        (
            shaped(domains - len(early) * (domains // blocks), 2 * share, atoms, kind=bf16),
            shaped(3 * charge_count, 2 * share),
        )
        + (shaped(3, domains, atoms),) * group,
        (),
        8_000,
        *columns,
        *waves_early,
        *parts,
        wave_index,
        scalars=(where,),
    )
    force_parts = force_parts[:1] + [across(force_parts[m], m) for m in range(1, group)]
    forces, *grad_parts = kernel(
        lambda *refs: gradient_kernel(
            *refs, group=group, blocks=blocks, early=early, charge_count=charge_count, box_x=box_x
        ),
        "gradient",
        (shaped(3, atoms),) + (shaped(charge_count, atoms, kind=bf16),) * group,
        (shaped(3, domains, atoms),),
        5_000,
        *columns,
        *force_parts,
        *waves_early,
        wave_index,
        waves,
        weights,
        scalars=(where,),
    )
    grad_parts = grad_parts[:1] + [across(grad_parts[m], m) for m in range(1, group)]

    rows = basis_count + width + charge_count + kinds
    rows = -(-rows // 8) * 8
    packed = kernel(
        lambda *refs: weights_kernel(*refs, group=group, kinds=kinds),
        "weights",
        shaped(rows, width),
        (),
        3_000,
        *grad_parts,
        filtered,
        messages,
        before,
        hidden,
        species_row,
        mix_weight,
        charge_rows,
    )
    packed = summed([packed] + [across(packed, r) for r in range(1, blocks)])
    totals = [packed] + [across(packed, bits) for bits in range(blocks, domains, blocks)]
    radial_step, mix_step, charge_step, species_step = kernel(
        step_kernel,
        "steps",
        (
            shaped(basis_count, width),
            shaped(width, width),
            shaped(charge_count, width),
            shaped(kinds, charge_count),
        ),
        (shaped(rows, width),),
        2_000,
        *totals,
    )
    return forces, radial_step, mix_step, charge_step.T, species_step


def solution(mesh):
    placed = (
        P(("cell", "dom"), None),
        P(None, ("cell", "dom")),
        P(("cell", "dom"), None),
        P(("cell", "dom")),
        P(None, ("cell", "dom")),
        P(("cell", "dom")),
        P(),
        P(None, ("cell", "dom")),
        P(),
        P(),
        P(),
        P(),
    )
    return jax.shard_map(
        on_device,
        mesh=mesh,
        in_specs=placed,
        out_specs=(
            P(None, ("cell", "dom")),
            P("cell", None),
            P("cell", None),
            P("cell", None),
            P("cell", None),
        ),
        check_vma=False,
    )
```

```python
import math

import jax
import jax.numpy as jnp
import numpy as np
from jax import lax
from jax.experimental import pallas as pl
from jax.experimental.pallas import tpu as pltpu
from jax.sharding import PartitionSpec as P

cutoff_radius = 5.0
kernel_width = 1.0
basis_width = 0.5
box_side = 20.0
two_pi = 6.283185307179586
highest = lax.Precision.HIGHEST
f32 = jnp.float32
bf16 = jnp.bfloat16
spare_vmem = 4 * 1024 * 1024
waves_bytes = 8 * 1024 * 1024
own_vmem = 50 * 1024 * 1024


def fitted(function, degrees, reach):
    nodes = reach * np.cos((np.arange(400) + 0.5) * np.pi / 400)
    powers = np.stack([nodes**d for d in degrees], axis=1)
    return [float(c) for c in np.linalg.lstsq(powers, function(nodes), rcond=None)[0]]


sine_terms = fitted(lambda x: np.sin(np.pi * x), (1, 3, 5, 7, 9), 0.5)
short_sine = fitted(lambda x: np.sin(np.pi * x), (1, 3, 5, 7), 0.5)
short_cosine = fitted(lambda x: np.cos(np.pi * x), (0, 2, 4, 6), 0.5)


def horner(terms, square):
    value = terms[-1]
    for term in terms[-2::-1]:
        value = value * square + term
    return value


def matmul(left, right, precision=None):
    return lax.dot_general(
        left, right, (((1,), (0,)), ((), ())), precision=precision, preferred_element_type=f32
    )


def matmul_nt(left, right, precision=None):
    return lax.dot_general(
        left, right, (((1,), (1,)), ((), ())), precision=precision, preferred_element_type=f32
    )


def turned(value):
    return jnp.transpose(value.astype(f32)).astype(value.dtype)


def sigmoid(value):
    return 1.0 / (1.0 + jnp.exp(-value))


def pieces_of(value):
    first = value.astype(bf16).astype(f32)
    rest = value - first
    second = rest.astype(bf16).astype(f32)
    return first, second, rest - second


def pack_kernel(feat_ref, positions_ref, ghost_ref, packed_ref):
    atoms, width = feat_ref.shape
    packed_ref[0:atoms, :] = feat_ref[...]
    extra = jnp.concatenate(
        pieces_of(positions_ref[...])
        + (ghost_ref[...].astype(f32), jnp.zeros((5, atoms), f32)),
        axis=0,
    ).astype(bf16)
    for part in range(atoms // width):
        first = atoms + part * 16
        packed_ref[first : first + 16, :] = extra[:, part * width : (part + 1) * width]


def pair_blocks(count, coords_ref, own_rows, words_ref, pair_ref, box_x):
    basis_count, _, atoms = pair_ref.shape
    centers = [
        0.5 + (cutoff_radius - 0.5) * float(b) / (basis_count - 1) for b in range(basis_count)
    ]
    scale = -math.log2(math.e) / (basis_width * basis_width)
    middle = basis_count // 2
    gap = centers[1] - centers[0]
    own_x, own_y, own_z = own_rows[0:1, :], own_rows[1:2, :], own_rows[2:3, :]
    step = 32

    def block(index, carry):
        places = pl.ds(pl.multiple_of(index * step, step), step)
        coords = coords_ref[places, :]
        total = jnp.zeros((step, atoms), f32)
        for axis, (mine, length) in enumerate(
            ((own_x, box_x), (own_y, box_side), (own_z, box_side))
        ):
            away = coords[:, axis : axis + 1] - mine
            away = away - length * jnp.floor(away * (1.0 / length) + 0.5)
            total = total + away * away
        distance = jnp.sqrt(total)
        word = words_ref[pl.ds(index, 1), :]
        sublane = lax.broadcasted_iota(jnp.int32, (step, atoms), 0)
        is_live = (jnp.right_shift(jnp.broadcast_to(word, (step, atoms)), sublane) & 1) != 0
        half = jnp.minimum(distance, cutoff_radius) * (1.0 / cutoff_radius) - 0.5
        fade = 0.5 - 0.5 * (half * horner(sine_terms, half * half))
        weight = jnp.where(jnp.logical_and(is_live, distance < cutoff_radius), fade, 0.0)
        offset = jnp.minimum(distance, cutoff_radius) - centers[middle]
        value = jnp.exp2(offset * offset * scale)
        for direction in (1, -1):
            ratio = jnp.exp2(offset * (-2.0 * direction * gap * scale))
            running = value
            for b in range(middle, basis_count) if direction == 1 else range(middle - 1, -1, -1):
                if b != middle:
                    running = running * ratio
                basis = running * math.exp(-(((b - middle) * gap / basis_width) ** 2))
                basis = basis.astype(bf16).astype(f32)
                pair_ref[b, places, :] = (weight * basis).astype(bf16)
        return carry

    lax.fori_loop(0, count // step, block, 0, unroll=8)


def own_kernel(
    feat_ref,
    positions_ref,
    force_ref,
    slots_ref,
    count_ref,
    species_ref,
    radial_ref,
    mix_ref,
    charge_ref,
    offset_ref,
    filtered_ref,
    words_ref,
    own_ref,
    shift_ref,
    weights_ref,
    extra_ref,
    coords_ref,
    pair_ref,
    *,
    box_x,
):
    atoms, width = feat_ref.shape
    slots = slots_ref.shape[0]
    basis_count = radial_ref.shape[0]
    own_rows = positions_ref[...]
    own_feat = turned(feat_ref[...])
    own_ref[...] = own_feat
    coords_ref[...] = jnp.transpose(
        jnp.concatenate([own_rows, jnp.zeros((5, atoms), f32)], axis=0)
    )

    listed = slots_ref[...]
    live = lax.broadcasted_iota(jnp.int32, (slots, atoms), 0) < count_ref[...]
    word_of = jnp.where(live, listed >> 5, -1)
    bit = jnp.left_shift(jnp.ones_like(listed), listed & 31)
    for word in range(words_ref.shape[0]):
        value = jnp.where(word_of == word, bit, 0)
        rows = slots
        while rows > 1:
            rows //= 2
            value = value[:rows] | value[rows:]
        words_ref[word : word + 1, :] = value

    pair_blocks(atoms, coords_ref, own_rows, words_ref, pair_ref, box_x)
    for b in range(basis_count):
        filtered_ref[b] = matmul(own_feat, pair_ref[b])

    kinds = offset_ref.shape[0]
    one_hot = (
        lax.broadcasted_iota(jnp.int32, (kinds, atoms), 0) == species_ref[...]
    ).astype(f32)
    shift_ref[...] = matmul(jnp.transpose(offset_ref[...]), one_hot, highest)
    charge_count = charge_ref.shape[0]
    weights_ref[0:width, :] = jnp.transpose(mix_ref[...].astype(f32))
    weights_ref[width : width + charge_count, :] = charge_ref[...].astype(f32)
    weights_ref[width + charge_count :, 0:basis_count] = jnp.transpose(
        radial_ref[...].astype(f32)
    )
    lengths = (box_x, box_side, box_side)
    turns = jnp.concatenate([own_rows[a : a + 1, :] * (1.0 / lengths[a]) for a in range(3)], axis=0)
    target = force_ref[...]
    high = target.astype(bf16).astype(f32)
    extra_ref[0:16, :] = jnp.concatenate(
        pieces_of(turns) + (high, target - high, jnp.zeros((1, atoms), f32)), axis=0
    )
    extra_ref[16:24, :] = jnp.concatenate([own_rows, jnp.zeros((5, atoms), f32)], axis=0)


def ghost_pairs(ref, is_low, words_ref, extra_ref, ghost_words_ref, coords_ref, pair_ref, box_x):
    _, ghosts, atoms = pair_ref.shape
    width = ref.shape[1]
    extra = jnp.concatenate(
        [ref[atoms + part * 16 : atoms + part * 16 + 16, :] for part in range(atoms // width)],
        axis=1,
    )
    sends = extra[8:16, :].astype(f32)
    sends = jnp.where(is_low, sends[2:3, :], sends[1:2, :])
    site = lax.broadcasted_iota(jnp.int32, (atoms, ghosts), 0).astype(f32)
    chosen = (site == sends).astype(bf16)
    moved = matmul(extra, chosen)
    moved = moved[0:3, :] + (moved[3:6, :] + moved[6:9, :])
    coords_ref[...] = jnp.transpose(jnp.concatenate([moved, jnp.zeros((5, ghosts), f32)], axis=0))
    count = ghosts // 32
    first = jnp.where(is_low, atoms // 32, atoms // 32 + count)
    ghost_words_ref[...] = words_ref[pl.ds(pl.multiple_of(first, 8), count), :]
    pair_blocks(ghosts, coords_ref, extra_ref[16:24, :], ghost_words_ref, pair_ref, box_x)
    return matmul(turned(ref[0:atoms, :]), chosen).astype(bf16)


def near_kernel(
    where_ref,
    near_ref,
    sofar_ref,
    words_ref,
    extra_ref,
    filtered_ref,
    ghost_words_ref,
    coords_ref,
    pair_ref,
    *,
    box_x,
):
    feat = ghost_pairs(
        near_ref,
        where_ref[0] == 1,
        words_ref,
        extra_ref,
        ghost_words_ref,
        coords_ref,
        pair_ref,
        box_x,
    )
    for b in range(filtered_ref.shape[0]):
        filtered_ref[b] = sofar_ref[b] + matmul(feat, pair_ref[b])


def edge_kernel(
    where_ref,
    far_ref,
    sofar_ref,
    words_ref,
    own_ref,
    shift_ref,
    weights_ref,
    extra_ref,
    filtered_ref,
    messages_ref,
    before_ref,
    hidden_ref,
    shared_ref,
    ghost_words_ref,
    coords_ref,
    pair_ref,
    *,
    box_x,
):
    width, atoms = own_ref.shape
    charge_count = shift_ref.shape[0]
    feat = ghost_pairs(
        far_ref,
        where_ref[0] == 0,
        words_ref,
        extra_ref,
        ghost_words_ref,
        coords_ref,
        pair_ref,
        box_x,
    )
    messages = jnp.zeros((width, atoms), f32)
    for b in range(filtered_ref.shape[0]):
        filtered = sofar_ref[b] + matmul(feat, pair_ref[b])
        filtered_ref[b] = filtered
        messages = messages + weights_ref[width + charge_count :, b : b + 1] * filtered
    messages_ref[...] = messages
    before = matmul(weights_ref[0:width, :], messages, highest)
    before_ref[...] = before
    hidden = (own_ref[...].astype(f32) + before * sigmoid(before)).astype(bf16)
    hidden_ref[...] = hidden
    charges = matmul(weights_ref[width : width + charge_count, :].astype(bf16), hidden)
    shared_ref[0, 0:charge_count, :] = (charges + shift_ref[...]).astype(bf16)
    shared_ref[0, charge_count : charge_count + 16, :] = extra_ref[0:16, :].astype(bf16)


def wave_rows(wave_ref, first, count, box_x, total_atoms):
    index = wave_ref[:, pl.ds(first, count)].astype(f32)
    scales = (two_pi / box_x, two_pi / box_side, two_pi / box_side)
    waves = [index[a : a + 1, :] * scales[a] for a in range(3)]
    squares = waves[0] * waves[0] + waves[1] * waves[1] + waves[2] * waves[2]
    damping = jnp.exp(-0.5 * kernel_width * kernel_width * squares) * (1.0 / total_atoms)
    return index, waves, damping


def wave_columns(wave_ref, first, share):
    index = wave_ref[:, pl.ds(first, share)].astype(f32)
    return jnp.transpose(
        jnp.concatenate([index] * 3 + [jnp.zeros((7, share), f32)], axis=0)
    ).astype(bf16)


def fill_waves(columns, shared_ref, j, charge_count, waves_ref, place):
    share = columns.shape[0]
    shift = 12582912.0
    turns = matmul(columns, shared_ref[j, charge_count : charge_count + 16, :])
    turns = turns - ((turns + shift) - shift)
    square = turns * turns
    half_sine = turns * horner(short_sine, square)
    half_cosine = horner(short_cosine, square)
    waves_ref[place, 0:share, :] = (2.0 * half_sine * half_cosine).astype(bf16)
    waves_ref[place, share : 2 * share, :] = (1.0 - 2.0 * half_sine * half_sine).astype(bf16)


def phase_kernel(where_ref, shared_ref, wave_ref, waves_ref, part_ref, *, charge_count):
    count = shared_ref.shape[0]
    share = waves_ref.shape[1] // 2
    columns = wave_columns(wave_ref, pl.multiple_of(where_ref[1] * share, share), share)

    def block(j, carry):
        fill_waves(columns, shared_ref, j, charge_count, waves_ref, j)
        return carry

    lax.fori_loop(0, count, block, 0, unroll=4)
    part = jnp.zeros(part_ref.shape, f32)
    for j in range(count):
        part = part + matmul_nt(shared_ref[j, 0:charge_count, :], waves_ref[j])
    part_ref[...] = part


def placed_waves(early, early_refs, late, waves_ref, count):
    return [
        early_refs[early.index(r)].at[j]
        if r in early
        else waves_ref.at[j * len(late) + late.index(r)]
        for j in range(count)
        for r in range(len(early) + len(late))
    ]


def structure_kernel(where_ref, *refs, group, blocks, early, charge_count, box_x):
    shared_refs, early_refs = refs[:blocks], refs[blocks : blocks + len(early)]
    part_refs, refs = refs[blocks + len(early) : blocks + 2 * len(early)], refs[blocks + 2 * len(early) :]
    wave_ref, waves_ref, weights_ref, *force_refs = refs
    late = [r for r in range(blocks) if r not in early]
    count, _, atoms = shared_refs[0].shape
    share = waves_ref.shape[1] // 2
    first = pl.multiple_of(where_ref[1] * share, share)
    _, waves, damping = wave_rows(wave_ref, first, share, box_x, blocks * count * atoms)
    columns = wave_columns(wave_ref, first, share)

    def block(j, carry):
        for i, r in enumerate(late):
            fill_waves(columns, shared_refs[r], j, charge_count, waves_ref, j * len(late) + i)
        return carry

    lax.fori_loop(0, count, block, 0, unroll=4)
    waves_of = placed_waves(early, early_refs, late, waves_ref, count)
    structure = sum(ref[...] for ref in part_refs)
    for d in range(blocks * count):
        j, r = divmod(d, blocks)
        if r in late:
            structure = structure + matmul_nt(
                shared_refs[r][j, 0:charge_count, :], waves_of[d][...]
            )
    along_sin = structure[:, :share] * damping
    along_cos = structure[:, share:] * damping
    to_sine = jnp.concatenate([along_cos * waves[a] for a in range(3)], axis=0)
    to_cosine = jnp.concatenate([-along_sin * waves[a] for a in range(3)], axis=0)
    weights = jnp.concatenate([to_sine, to_cosine], axis=1)
    weights_ref[...] = weights
    weights = weights.astype(bf16)
    for d in range(blocks * count):
        j, r = divmod(d, blocks)
        field = matmul(weights, waves_of[d][...])
        charges = shared_refs[r][j, 0:charge_count, :].astype(f32)
        for a in range(3):
            row = jnp.sum(
                field[a * charge_count : (a + 1) * charge_count, :] * charges,
                axis=0,
                keepdims=True,
            )
            for m in range(group):
                force_refs[m][a, d ^ m : (d ^ m) + 1, :] = row


def field_kernel(*refs, group, blocks, early, count):
    weights_ref, refs = refs[0], refs[1:]
    early_refs, waves_ref, field_refs = refs[: len(early)], refs[len(early)], refs[len(early) + 1 :]
    late = [r for r in range(blocks) if r not in early]
    waves_of = placed_waves(early, early_refs, late, waves_ref, count)
    weights = weights_ref[...]
    weights_high = weights.astype(bf16)
    weights_low = (weights - weights_high.astype(f32)).astype(bf16)
    for m in range(group):
        block = waves_of[m][...]
        field_refs[m][...] = matmul(weights_high, block) + matmul(weights_low, block)


def charge_gradient(errors, field, back, block):
    charge_count = back.shape[0]
    high = back.astype(bf16)
    low = (back - high.astype(f32)).astype(bf16)
    grad = matmul(high, block) + matmul(low, block)
    for a in range(3):
        grad = grad + errors[a] * field[a * charge_count : (a + 1) * charge_count, :]
    return grad


def gradient_kernel(where_ref, *refs, group, blocks, early, charge_count, box_x):
    shared_refs, part_refs = refs[:blocks], refs[blocks : blocks + group]
    refs = refs[blocks + group :]
    early_refs, refs = refs[: len(early)], refs[len(early) :]
    field_refs, refs = refs[: group - 1], refs[group - 1 :]
    wave_ref, waves_ref, forces_ref, errors_ref, back_ref, *grad_refs, total_ref = refs
    late = [r for r in range(blocks) if r not in early]
    count, _, atoms = shared_refs[0].shape
    share = waves_ref.shape[1] // 2
    first = pl.multiple_of(where_ref[1] * share, share)
    _, waves, damping = wave_rows(wave_ref, first, share, box_x, blocks * count * atoms)
    waves_of = placed_waves(early, early_refs, late, waves_ref, count)
    total = part_refs[0][...]
    for m in range(1, group):
        total = total + part_refs[m][...]
    total_ref[...] = total
    for a in range(3):
        forces_ref[a : a + 1, :] = total[a, 0:1, :]

    def errors_of(d):
        j, r = divmod(d, blocks)
        target = shared_refs[r][j, charge_count : charge_count + 16, :].astype(f32)
        target = target[9:12, :] + target[12:15, :]
        return [2.0 * (total_ref[a, d : d + 1, :] - target[a : a + 1, :]) for a in range(3)]

    by_wave = jnp.zeros((3 * charge_count, 2 * share), f32)
    for d in range(blocks * count):
        j, r = divmod(d, blocks)
        charges = shared_refs[r][j, 0:charge_count, :].astype(f32)
        errors = errors_of(d)
        scaled = jnp.concatenate([errors[a] * charges for a in range(3)], axis=0).astype(bf16)
        by_wave = by_wave + matmul_nt(scaled, waves_of[d][...])
        if d == 0:
            errors_ref[...] = jnp.concatenate(errors + [jnp.zeros((5, atoms), f32)], axis=0)

    def along(value):
        return sum(
            waves[a] * value[a * charge_count : (a + 1) * charge_count, :] for a in range(3)
        )

    back_cos = damping * along(by_wave[:, :share])
    back_sin = -damping * along(by_wave[:, share:])
    back = jnp.concatenate([back_sin, back_cos], axis=1)
    back_ref[...] = back
    for m in range(1, group):
        grad_refs[m - 1][...] = charge_gradient(
            errors_of(m), field_refs[m - 1][...], back, waves_of[m][...]
        ).astype(bf16)


def own_gradient_kernel(errors_ref, field_ref, back_ref, waves_ref, grad_ref):
    errors = errors_ref[...]
    grad_ref[...] = charge_gradient(
        [errors[a : a + 1, :] for a in range(3)], field_ref[...], back_ref[...], waves_ref[0]
    )


def weights_kernel(*refs, group, kinds):
    part_refs = refs[:group]
    (
        filtered_ref,
        messages_ref,
        before_ref,
        hidden_ref,
        species_ref,
        mix_ref,
        charge_ref,
        packed_ref,
    ) = refs[group:]
    charge_count, atoms = part_refs[0].shape
    basis_count, width, _ = filtered_ref.shape
    grad = part_refs[0][...].astype(f32)
    for m in range(1, group):
        grad = grad + part_refs[m][...].astype(f32)
    before = before_ref[...]
    gate = sigmoid(before)
    upstream = matmul(jnp.transpose(charge_ref[...].astype(f32)), grad, highest)
    before_grad = upstream * (gate * (1.0 + before * (1.0 - gate)))
    message_grad = matmul(mix_ref[...].astype(f32), before_grad, highest)
    columns = [
        jnp.sum(message_grad * filtered_ref[b], axis=1, keepdims=True) for b in range(basis_count)
    ]
    radial = jnp.concatenate(columns, axis=1)
    row = 0
    packed_ref[row : row + basis_count, :] = jnp.transpose(radial)
    row += basis_count
    packed_ref[row : row + width, :] = matmul_nt(messages_ref[...], before_grad, highest)
    row += width
    packed_ref[row : row + charge_count, :] = matmul_nt(
        grad, hidden_ref[...].astype(f32), highest
    )
    row += charge_count
    packed_ref[row:, :] = jnp.zeros((packed_ref.shape[0] - row, width), f32)
    one_hot = (
        lax.broadcasted_iota(jnp.int32, (kinds, atoms), 0) == species_ref[...]
    ).astype(f32)
    packed_ref[row : row + kinds, 0:charge_count] = matmul_nt(one_hot, grad, highest)


def summed(values):
    while len(values) > 1:
        values = [values[i] + values[i + 1] for i in range(0, len(values), 2)]
    return values[0]


def step_kernel(*refs):
    *total_refs, radial_ref, mix_ref, charge_ref, species_ref, total_ref = refs
    basis_count, width = radial_ref.shape
    charge_count = charge_ref.shape[0]
    kinds = species_ref.shape[0]
    total_ref[...] = summed([ref[...].astype(f32) for ref in total_refs])

    def normalized(gradient):
        mean = jnp.sum(gradient * gradient, keepdims=True) * (1.0 / gradient.size)
        return gradient * lax.rsqrt(mean + 1e-06)

    row = 0
    radial_ref[...] = normalized(total_ref[row : row + basis_count, :])
    row += basis_count
    mix_ref[...] = normalized(total_ref[row : row + width, :])
    row += width
    charge_ref[...] = normalized(total_ref[row : row + charge_count, :])
    row += charge_count
    species_ref[...] = normalized(total_ref[row : row + kinds, 0:charge_count])


def shaped(*dims, kind=f32):
    return jax.ShapeDtypeStruct(dims, kind)


def kernel(body, name, out_shape, scratch, nanoseconds, *operands, scalars=(), wanted=0):
    outs = out_shape if isinstance(out_shape, tuple) else (out_shape,)
    held = sum(math.prod(x.shape) * x.dtype.itemsize for x in (*outs, *scratch, *operands))
    in_vmem = pl.BlockSpec(memory_space=pltpu.VMEM)
    in_smem = pl.BlockSpec(memory_space=pltpu.SMEM)
    return pl.pallas_call(
        body,
        out_shape=out_shape,
        in_specs=[in_smem] * len(scalars) + [in_vmem] * len(operands),
        out_specs=tuple(in_vmem for _ in outs) if isinstance(out_shape, tuple) else in_vmem,
        scratch_shapes=[pltpu.VMEM(x.shape, x.dtype) for x in scratch],
        compiler_params=pltpu.CompilerParams(vmem_limit_bytes=max(held + spare_vmem, wanted)),
        cost_estimate=pl.CostEstimate(
            flops=nanoseconds * 1_000_000, bytes_accessed=held, transcendentals=0
        ),
        name=name,
    )(*scalars, *operands)


def across(value, bits):
    domains = lax.axis_size("dom")
    return lax.ppermute(value, "dom", [(i, i ^ bits) for i in range(domains)])


def on_device(
    features,
    positions,
    neighbours,
    neighbour_count,
    ghost_sends,
    species,
    wave_index,
    force_ref,
    radial_weight,
    mix_weight,
    charge_weight,
    species_charge,
):
    atoms, width = features.shape
    basis_count = radial_weight.shape[0]
    charge_count = charge_weight.shape[1]
    kinds = species_charge.shape[0]
    wave_count = wave_index.shape[1]
    domains = lax.axis_size("dom")
    box_x = 1.25 * (atoms * domains) / 64
    group = 2 if domains % 2 == 0 else 1
    while (
        group < domains
        and 4 * wave_count // group * atoms * domains > waves_bytes
        and wave_count % (256 * group) == 0
    ):
        group *= 2
    share = wave_count // group
    entries = atoms + 2 * ghost_sends.shape[1]

    me = lax.axis_index("dom")
    blocks = 4 if domains % 4 == 0 else 2
    where = jnp.stack([me % 2, me % group, me % blocks]).astype(jnp.int32)
    packed = kernel(
        pack_kernel,
        "pack",
        shaped(atoms + 16 * (atoms // width), width, kind=bf16),
        (),
        1_000,
        features,
        positions,
        ghost_sends,
        wanted=60 * 1024 * 1024,
    )
    near = across(packed, 1)
    beyond = [(i, (i + 1 if i % 2 else i - 1) % domains) for i in range(domains)]
    far = lax.ppermute(packed, "dom", beyond)
    species_row = species[None, :]
    slots = neighbours.T
    charge_rows = charge_weight.T

    sofar, words, *local, extra = kernel(
        lambda *refs: own_kernel(*refs, box_x=box_x),
        "own",
        (
            shaped(basis_count, width, atoms),
            shaped(entries // 32, atoms, kind=jnp.int32),
            shaped(width, atoms, kind=bf16),
            shaped(charge_count, atoms),
            shaped(2 * width + charge_count, width),
            shaped(24, atoms),
        ),
        (
            shaped(atoms, 8),
            shaped(basis_count, atoms, atoms, kind=bf16),
        ),
        4_000,
        features,
        positions,
        force_ref,
        slots,
        neighbour_count[None, :],
        species_row,
        radial_weight,
        mix_weight,
        charge_rows,
        species_charge,
        wanted=own_vmem,
    )
    ghosts = ghost_sends.shape[1]
    scratch = (
        shaped(ghosts // 32, atoms, kind=jnp.int32),
        shaped(ghosts, 8),
        shaped(basis_count, ghosts, atoms, kind=bf16),
    )
    sofar = kernel(
        lambda *refs: near_kernel(*refs, box_x=box_x),
        "near",
        shaped(basis_count, width, atoms),
        scratch,
        3_000,
        near,
        sofar,
        words,
        extra,
        scalars=(where,),
    )
    filtered, messages, before, hidden, shared = kernel(
        lambda *refs: edge_kernel(*refs, box_x=box_x),
        "edges",
        (
            shaped(basis_count, width, atoms),
            shaped(width, atoms),
            shaped(width, atoms),
            shaped(width, atoms, kind=bf16),
            shaped(1, charge_count + 16, atoms, kind=bf16),
        ),
        scratch,
        4_000,
        far,
        sofar,
        words,
        *local,
        extra,
        scalars=(where,),
    )
    column = jnp.concatenate(
        [shared] + [across(shared, bits) for bits in range(blocks, domains, blocks)], axis=0
    )
    columns = [column] + [across(column, bits) for bits in range(1, blocks)]
    early = (0, blocks - 1) if blocks > 2 else (0,)
    waves_early, parts = zip(
        *[
            kernel(
                lambda *refs: phase_kernel(*refs, charge_count=charge_count),
                "phases",
                (
                    shaped(domains // blocks, 2 * share, atoms, kind=bf16),
                    shaped(charge_count, 2 * share),
                ),
                (),
                3_000,
                columns[r],
                wave_index,
                scalars=(where,),
            )
            for r in early
        ]
    )
    waves, weights, *force_parts = kernel(
        lambda *refs: structure_kernel(
            *refs, group=group, blocks=blocks, early=early, charge_count=charge_count, box_x=box_x
        ),
        "structure",
        (
            shaped(domains - len(early) * (domains // blocks), 2 * share, atoms, kind=bf16),
            shaped(3 * charge_count, 2 * share),
        )
        + (shaped(3, domains, atoms),) * group,
        (),
        8_000,
        *columns,
        *waves_early,
        *parts,
        wave_index,
        scalars=(where,),
    )
    force_parts = force_parts[:1] + [across(force_parts[m], m) for m in range(1, group)]
    fields = kernel(
        lambda *refs: field_kernel(
            *refs, group=group, blocks=blocks, early=early, count=domains // blocks
        ),
        "fields",
        (shaped(3 * charge_count, atoms),) * group,
        (),
        2_000,
        weights,
        *waves_early,
        waves,
    )
    forces, errors, back, *grad_parts = kernel(
        lambda *refs: gradient_kernel(
            *refs, group=group, blocks=blocks, early=early, charge_count=charge_count, box_x=box_x
        ),
        "gradient",
        (
            shaped(3, atoms),
            shaped(8, atoms),
            shaped(charge_count, 2 * share),
        )
        + (shaped(charge_count, atoms, kind=bf16),) * (group - 1),
        (shaped(3, domains, atoms),),
        5_000,
        *columns,
        *force_parts,
        *waves_early,
        *fields[1:],
        wave_index,
        waves,
        scalars=(where,),
    )
    own_part = kernel(
        own_gradient_kernel,
        "own_gradient",
        shaped(charge_count, atoms),
        (),
        1_500,
        errors,
        fields[0],
        back,
        waves_early[0],
    )
    grad_parts = [own_part] + [across(grad_parts[m - 1], m) for m in range(1, group)]

    rows = basis_count + width + charge_count + kinds
    rows = -(-rows // 16) * 16
    packed = kernel(
        lambda *refs: weights_kernel(*refs, group=group, kinds=kinds),
        "weights",
        shaped(rows, width),
        (),
        3_000,
        *grad_parts,
        filtered,
        messages,
        before,
        hidden,
        species_row,
        mix_weight,
        charge_rows,
    )
    packed = summed([packed] + [across(packed, r) for r in range(1, blocks)]).astype(bf16)
    totals = [packed] + [across(packed, bits) for bits in range(blocks, domains, blocks)]
    radial_step, mix_step, charge_step, species_step = kernel(
        step_kernel,
        "steps",
        (
            shaped(basis_count, width),
            shaped(width, width),
            shaped(charge_count, width),
            shaped(kinds, charge_count),
        ),
        (shaped(rows, width),),
        2_000,
        *totals,
    )
    return forces, radial_step, mix_step, charge_step.T, species_step


def solution(mesh):
    placed = (
        P(("cell", "dom"), None),
        P(None, ("cell", "dom")),
        P(("cell", "dom"), None),
        P(("cell", "dom")),
        P(None, ("cell", "dom")),
        P(("cell", "dom")),
        P(),
        P(None, ("cell", "dom")),
        P(),
        P(),
        P(),
        P(),
    )
    return jax.shard_map(
        on_device,
        mesh=mesh,
        in_specs=placed,
        out_specs=(
            P(None, ("cell", "dom")),
            P("cell", None),
            P("cell", None),
            P("cell", None),
            P("cell", None),
        ),
        check_vma=False,
    )
```

```python
import math

import jax
import jax.numpy as jnp
import numpy as np
from jax import lax
from jax.experimental import pallas as pl
from jax.experimental.pallas import tpu as pltpu
from jax.sharding import PartitionSpec as P

cutoff_radius = 5.0
kernel_width = 1.0
basis_width = 0.5
box_side = 20.0
two_pi = 6.283185307179586
highest = lax.Precision.HIGHEST
f32 = jnp.float32
bf16 = jnp.bfloat16
spare_vmem = 4 * 1024 * 1024
waves_bytes = 8 * 1024 * 1024
own_vmem = 50 * 1024 * 1024


def fitted(function, degrees, reach):
    nodes = reach * np.cos((np.arange(400) + 0.5) * np.pi / 400)
    powers = np.stack([nodes**d for d in degrees], axis=1)
    return [float(c) for c in np.linalg.lstsq(powers, function(nodes), rcond=None)[0]]


sine_terms = fitted(lambda x: np.sin(np.pi * x), (1, 3, 5, 7, 9), 0.5)
short_sine = fitted(lambda x: np.sin(np.pi * x), (1, 3, 5, 7), 0.5)
short_cosine = fitted(lambda x: np.cos(np.pi * x), (0, 2, 4, 6), 0.5)


def horner(terms, square):
    value = terms[-1]
    for term in terms[-2::-1]:
        value = value * square + term
    return value


def matmul(left, right, precision=None):
    return lax.dot_general(
        left, right, (((1,), (0,)), ((), ())), precision=precision, preferred_element_type=f32
    )


def matmul_nt(left, right, precision=None):
    return lax.dot_general(
        left, right, (((1,), (1,)), ((), ())), precision=precision, preferred_element_type=f32
    )


def turned(value):
    return jnp.transpose(value.astype(f32)).astype(value.dtype)


def sigmoid(value):
    return 1.0 / (1.0 + jnp.exp(-value))


def pieces_of(value):
    first = value.astype(bf16).astype(f32)
    rest = value - first
    second = rest.astype(bf16).astype(f32)
    return first, second, rest - second


def pack_kernel(feat_ref, positions_ref, ghost_ref, packed_ref):
    atoms, width = feat_ref.shape
    packed_ref[0:atoms, :] = feat_ref[...]
    extra = jnp.concatenate(
        pieces_of(positions_ref[...])
        + (ghost_ref[...].astype(f32), jnp.zeros((5, atoms), f32)),
        axis=0,
    ).astype(bf16)
    for part in range(atoms // width):
        first = atoms + part * 16
        packed_ref[first : first + 16, :] = extra[:, part * width : (part + 1) * width]


def pair_blocks(count, coords_ref, own_rows, words_ref, pair_ref, box_x):
    basis_count, _, atoms = pair_ref.shape
    centers = [
        0.5 + (cutoff_radius - 0.5) * float(b) / (basis_count - 1) for b in range(basis_count)
    ]
    scale = -math.log2(math.e) / (basis_width * basis_width)
    middle = basis_count // 2
    gap = centers[1] - centers[0]
    own_x, own_y, own_z = own_rows[0:1, :], own_rows[1:2, :], own_rows[2:3, :]
    step = 32

    def block(index, carry):
        places = pl.ds(pl.multiple_of(index * step, step), step)
        coords = coords_ref[places, :]
        total = jnp.zeros((step, atoms), f32)
        for axis, (mine, length) in enumerate(
            ((own_x, box_x), (own_y, box_side), (own_z, box_side))
        ):
            away = coords[:, axis : axis + 1] - mine
            away = away - length * jnp.floor(away * (1.0 / length) + 0.5)
            total = total + away * away
        distance = jnp.sqrt(total)
        word = words_ref[pl.ds(index, 1), :]
        sublane = lax.broadcasted_iota(jnp.int32, (step, atoms), 0)
        is_live = (jnp.right_shift(jnp.broadcast_to(word, (step, atoms)), sublane) & 1) != 0
        half = jnp.minimum(distance, cutoff_radius) * (1.0 / cutoff_radius) - 0.5
        fade = 0.5 - 0.5 * (half * horner(sine_terms, half * half))
        weight = jnp.where(jnp.logical_and(is_live, distance < cutoff_radius), fade, 0.0)
        offset = jnp.minimum(distance, cutoff_radius) - centers[middle]
        value = jnp.exp2(offset * offset * scale)
        for direction in (1, -1):
            ratio = jnp.exp2(offset * (-2.0 * direction * gap * scale))
            running = value
            for b in range(middle, basis_count) if direction == 1 else range(middle - 1, -1, -1):
                if b != middle:
                    running = running * ratio
                basis = running * math.exp(-(((b - middle) * gap / basis_width) ** 2))
                basis = basis.astype(bf16).astype(f32)
                pair_ref[b, places, :] = (weight * basis).astype(bf16)
        return carry

    lax.fori_loop(0, count // step, block, 0, unroll=8)


def own_kernel(
    feat_ref,
    positions_ref,
    force_ref,
    slots_ref,
    count_ref,
    species_ref,
    radial_ref,
    mix_ref,
    charge_ref,
    offset_ref,
    filtered_ref,
    words_ref,
    own_ref,
    shift_ref,
    weights_ref,
    extra_ref,
    coords_ref,
    pair_ref,
    *,
    box_x,
):
    atoms, width = feat_ref.shape
    slots = slots_ref.shape[0]
    basis_count = radial_ref.shape[0]
    own_rows = positions_ref[...]
    own_feat = turned(feat_ref[...])
    own_ref[...] = own_feat
    coords_ref[...] = jnp.transpose(
        jnp.concatenate([own_rows, jnp.zeros((5, atoms), f32)], axis=0)
    )

    listed = slots_ref[...]
    live = lax.broadcasted_iota(jnp.int32, (slots, atoms), 0) < count_ref[...]
    word_of = jnp.where(live, listed >> 5, -1)
    bit = jnp.left_shift(jnp.ones_like(listed), listed & 31)
    for word in range(words_ref.shape[0]):
        value = jnp.where(word_of == word, bit, 0)
        rows = slots
        while rows > 1:
            rows //= 2
            value = value[:rows] | value[rows:]
        words_ref[word : word + 1, :] = value

    pair_blocks(atoms, coords_ref, own_rows, words_ref, pair_ref, box_x)
    for b in range(basis_count):
        filtered_ref[b] = matmul(own_feat, pair_ref[b])

    kinds = offset_ref.shape[0]
    one_hot = (
        lax.broadcasted_iota(jnp.int32, (kinds, atoms), 0) == species_ref[...]
    ).astype(f32)
    shift_ref[...] = matmul(jnp.transpose(offset_ref[...]), one_hot, highest)
    charge_count = charge_ref.shape[0]
    weights_ref[0:width, :] = jnp.transpose(mix_ref[...].astype(f32))
    weights_ref[width : width + charge_count, :] = charge_ref[...].astype(f32)
    weights_ref[width + charge_count :, 0:basis_count] = jnp.transpose(
        radial_ref[...].astype(f32)
    )
    lengths = (box_x, box_side, box_side)
    turns = jnp.concatenate([own_rows[a : a + 1, :] * (1.0 / lengths[a]) for a in range(3)], axis=0)
    target = force_ref[...]
    high = target.astype(bf16).astype(f32)
    extra_ref[0:16, :] = jnp.concatenate(
        pieces_of(turns) + (high, target - high, jnp.zeros((1, atoms), f32)), axis=0
    )
    extra_ref[16:24, :] = jnp.concatenate([own_rows, jnp.zeros((5, atoms), f32)], axis=0)


def ghost_pairs(ref, is_low, words_ref, extra_ref, ghost_words_ref, coords_ref, pair_ref, box_x):
    _, ghosts, atoms = pair_ref.shape
    width = ref.shape[1]
    extra = jnp.concatenate(
        [ref[atoms + part * 16 : atoms + part * 16 + 16, :] for part in range(atoms // width)],
        axis=1,
    )
    sends = extra[8:16, :].astype(f32)
    sends = jnp.where(is_low, sends[2:3, :], sends[1:2, :])
    site = lax.broadcasted_iota(jnp.int32, (atoms, ghosts), 0).astype(f32)
    chosen = (site == sends).astype(bf16)
    moved = matmul(extra, chosen)
    moved = moved[0:3, :] + (moved[3:6, :] + moved[6:9, :])
    coords_ref[...] = jnp.transpose(jnp.concatenate([moved, jnp.zeros((5, ghosts), f32)], axis=0))
    count = ghosts // 32
    first = jnp.where(is_low, atoms // 32, atoms // 32 + count)
    ghost_words_ref[...] = words_ref[pl.ds(pl.multiple_of(first, 8), count), :]
    pair_blocks(ghosts, coords_ref, extra_ref[16:24, :], ghost_words_ref, pair_ref, box_x)
    return matmul(turned(ref[0:atoms, :]), chosen).astype(bf16)


def near_kernel(
    where_ref,
    near_ref,
    sofar_ref,
    words_ref,
    extra_ref,
    filtered_ref,
    ghost_words_ref,
    coords_ref,
    pair_ref,
    *,
    box_x,
):
    feat = ghost_pairs(
        near_ref,
        where_ref[0] == 1,
        words_ref,
        extra_ref,
        ghost_words_ref,
        coords_ref,
        pair_ref,
        box_x,
    )
    for b in range(filtered_ref.shape[0]):
        filtered_ref[b] = sofar_ref[b] + matmul(feat, pair_ref[b])


def edge_kernel(
    where_ref,
    far_ref,
    sofar_ref,
    words_ref,
    own_ref,
    shift_ref,
    weights_ref,
    extra_ref,
    filtered_ref,
    messages_ref,
    before_ref,
    hidden_ref,
    shared_ref,
    ghost_words_ref,
    coords_ref,
    pair_ref,
    *,
    box_x,
):
    width, atoms = own_ref.shape
    charge_count = shift_ref.shape[0]
    feat = ghost_pairs(
        far_ref,
        where_ref[0] == 0,
        words_ref,
        extra_ref,
        ghost_words_ref,
        coords_ref,
        pair_ref,
        box_x,
    )
    messages = jnp.zeros((width, atoms), f32)
    for b in range(filtered_ref.shape[0]):
        filtered = sofar_ref[b] + matmul(feat, pair_ref[b])
        filtered_ref[b] = filtered
        messages = messages + weights_ref[width + charge_count :, b : b + 1] * filtered
    messages_ref[...] = messages
    before = matmul(weights_ref[0:width, :], messages, highest)
    before_ref[...] = before
    hidden = (own_ref[...].astype(f32) + before * sigmoid(before)).astype(bf16)
    hidden_ref[...] = hidden
    charges = matmul(weights_ref[width : width + charge_count, :].astype(bf16), hidden)
    shared_ref[0, 0:charge_count, :] = (charges + shift_ref[...]).astype(bf16)
    shared_ref[0, charge_count : charge_count + 16, :] = extra_ref[0:16, :].astype(bf16)


def wave_rows(wave_ref, first, count, box_x, total_atoms):
    index = wave_ref[:, pl.ds(first, count)].astype(f32)
    scales = (two_pi / box_x, two_pi / box_side, two_pi / box_side)
    waves = [index[a : a + 1, :] * scales[a] for a in range(3)]
    squares = waves[0] * waves[0] + waves[1] * waves[1] + waves[2] * waves[2]
    damping = jnp.exp(-0.5 * kernel_width * kernel_width * squares) * (1.0 / total_atoms)
    return index, waves, damping


def wave_columns(wave_ref, first, share):
    index = wave_ref[:, pl.ds(first, share)].astype(f32)
    return jnp.transpose(
        jnp.concatenate([index] * 3 + [jnp.zeros((7, share), f32)], axis=0)
    ).astype(bf16)


def fill_waves(columns, shared_ref, j, charge_count, waves_ref, place):
    share = columns.shape[0]
    shift = 12582912.0
    turns = matmul(columns, shared_ref[j, charge_count : charge_count + 16, :])
    turns = turns - ((turns + shift) - shift)
    square = turns * turns
    half_sine = turns * horner(short_sine, square)
    half_cosine = horner(short_cosine, square)
    waves_ref[place, 0:share, :] = (2.0 * half_sine * half_cosine).astype(bf16)
    waves_ref[place, share : 2 * share, :] = (1.0 - 2.0 * half_sine * half_sine).astype(bf16)


def phase_kernel(where_ref, shared_ref, wave_ref, waves_ref, part_ref, *, charge_count):
    count = shared_ref.shape[0]
    share = waves_ref.shape[1] // 2
    columns = wave_columns(wave_ref, pl.multiple_of(where_ref[1] * share, share), share)

    def block(j, carry):
        fill_waves(columns, shared_ref, j, charge_count, waves_ref, j)
        return carry

    lax.fori_loop(0, count, block, 0, unroll=4)
    part = jnp.zeros(part_ref.shape, f32)
    for j in range(count):
        part = part + matmul_nt(shared_ref[j, 0:charge_count, :], waves_ref[j])
    part_ref[...] = part


def placed_waves(early, early_refs, late, waves_ref, count):
    return [
        early_refs[early.index(r)].at[j]
        if r in early
        else waves_ref.at[j * len(late) + late.index(r)]
        for j in range(count)
        for r in range(len(early) + len(late))
    ]


def structure_kernel(where_ref, *refs, group, blocks, early, charge_count, box_x):
    shared_refs, early_refs = refs[:blocks], refs[blocks : blocks + len(early)]
    part_refs, refs = refs[blocks + len(early) : blocks + 2 * len(early)], refs[blocks + 2 * len(early) :]
    wave_ref, waves_ref, weights_ref, *force_refs = refs
    late = [r for r in range(blocks) if r not in early]
    count, _, atoms = shared_refs[0].shape
    share = waves_ref.shape[1] // 2
    first = pl.multiple_of(where_ref[1] * share, share)
    _, waves, damping = wave_rows(wave_ref, first, share, box_x, blocks * count * atoms)
    columns = wave_columns(wave_ref, first, share)

    def block(j, carry):
        for i, r in enumerate(late):
            fill_waves(columns, shared_refs[r], j, charge_count, waves_ref, j * len(late) + i)
        return carry

    lax.fori_loop(0, count, block, 0, unroll=4)
    waves_of = placed_waves(early, early_refs, late, waves_ref, count)
    structure = sum(ref[...] for ref in part_refs)
    for d in range(blocks * count):
        j, r = divmod(d, blocks)
        if r in late:
            structure = structure + matmul_nt(
                shared_refs[r][j, 0:charge_count, :], waves_of[d][...]
            )
    along_sin = structure[:, :share] * damping
    along_cos = structure[:, share:] * damping
    to_sine = jnp.concatenate([along_cos * waves[a] for a in range(3)], axis=0)
    to_cosine = jnp.concatenate([-along_sin * waves[a] for a in range(3)], axis=0)
    weights = jnp.concatenate([to_sine, to_cosine], axis=1)
    weights_ref[...] = weights
    weights = weights.astype(bf16)
    for d in range(blocks * count):
        j, r = divmod(d, blocks)
        field = matmul(weights, waves_of[d][...])
        charges = shared_refs[r][j, 0:charge_count, :].astype(f32)
        for a in range(3):
            row = jnp.sum(
                field[a * charge_count : (a + 1) * charge_count, :] * charges,
                axis=0,
                keepdims=True,
            )
            for m in range(group):
                force_refs[m][a, d ^ m : (d ^ m) + 1, :] = row


def field_kernel(*refs, group, blocks, early, count):
    weights_ref, refs = refs[0], refs[1:]
    early_refs, waves_ref, field_refs = refs[: len(early)], refs[len(early)], refs[len(early) + 1 :]
    late = [r for r in range(blocks) if r not in early]
    waves_of = placed_waves(early, early_refs, late, waves_ref, count)
    weights = weights_ref[...]
    weights_high = weights.astype(bf16)
    weights_low = (weights - weights_high.astype(f32)).astype(bf16)
    for m in range(group):
        block = waves_of[m][...]
        field_refs[m][...] = matmul(weights_high, block) + matmul(weights_low, block)


def charge_gradient(errors, field, back, block):
    charge_count = back.shape[0]
    high = back.astype(bf16)
    low = (back - high.astype(f32)).astype(bf16)
    grad = matmul(high, block) + matmul(low, block)
    for a in range(3):
        grad = grad + errors[a] * field[a * charge_count : (a + 1) * charge_count, :]
    return grad


def gradient_kernel(where_ref, *refs, group, blocks, early, charge_count, box_x):
    shared_refs, part_refs = refs[:blocks], refs[blocks : blocks + group]
    refs = refs[blocks + group :]
    early_refs, refs = refs[: len(early)], refs[len(early) :]
    field_refs, refs = refs[: group - 1], refs[group - 1 :]
    wave_ref, waves_ref, forces_ref, errors_ref, back_ref, *grad_refs, total_ref = refs
    late = [r for r in range(blocks) if r not in early]
    count, _, atoms = shared_refs[0].shape
    share = waves_ref.shape[1] // 2
    first = pl.multiple_of(where_ref[1] * share, share)
    _, waves, damping = wave_rows(wave_ref, first, share, box_x, blocks * count * atoms)
    waves_of = placed_waves(early, early_refs, late, waves_ref, count)
    total = part_refs[0][...]
    for m in range(1, group):
        total = total + part_refs[m][...]
    total_ref[...] = total
    for a in range(3):
        forces_ref[a : a + 1, :] = total[a, 0:1, :]

    def errors_of(d):
        j, r = divmod(d, blocks)
        target = shared_refs[r][j, charge_count : charge_count + 16, :].astype(f32)
        target = target[9:12, :] + target[12:15, :]
        return [2.0 * (total_ref[a, d : d + 1, :] - target[a : a + 1, :]) for a in range(3)]

    by_wave = jnp.zeros((3 * charge_count, 2 * share), f32)
    for d in range(blocks * count):
        j, r = divmod(d, blocks)
        charges = shared_refs[r][j, 0:charge_count, :].astype(f32)
        errors = errors_of(d)
        scaled = jnp.concatenate([errors[a] * charges for a in range(3)], axis=0).astype(bf16)
        by_wave = by_wave + matmul_nt(scaled, waves_of[d][...])
        if d == 0:
            errors_ref[...] = jnp.concatenate(errors + [jnp.zeros((5, atoms), f32)], axis=0)

    def along(value):
        return sum(
            waves[a] * value[a * charge_count : (a + 1) * charge_count, :] for a in range(3)
        )

    back_cos = damping * along(by_wave[:, :share])
    back_sin = -damping * along(by_wave[:, share:])
    back = jnp.concatenate([back_sin, back_cos], axis=1)
    back_ref[...] = back
    for m in range(1, group):
        grad_refs[m - 1][...] = charge_gradient(
            errors_of(m), field_refs[m - 1][...], back, waves_of[m][...]
        ).astype(bf16)


def own_gradient_kernel(errors_ref, field_ref, back_ref, waves_ref, grad_ref):
    errors = errors_ref[...]
    grad_ref[...] = charge_gradient(
        [errors[a : a + 1, :] for a in range(3)], field_ref[...], back_ref[...], waves_ref[0]
    )


def weights_kernel(*refs, group, kinds):
    part_refs = refs[:group]
    (
        filtered_ref,
        messages_ref,
        before_ref,
        hidden_ref,
        species_ref,
        mix_ref,
        charge_ref,
        packed_ref,
    ) = refs[group:]
    charge_count, atoms = part_refs[0].shape
    basis_count, width, _ = filtered_ref.shape
    grad = part_refs[0][...].astype(f32)
    for m in range(1, group):
        grad = grad + part_refs[m][...].astype(f32)
    before = before_ref[...]
    gate = sigmoid(before)
    upstream = matmul(jnp.transpose(charge_ref[...].astype(f32)), grad, highest)
    before_grad = upstream * (gate * (1.0 + before * (1.0 - gate)))
    message_grad = matmul(mix_ref[...].astype(f32), before_grad, highest)
    columns = [
        jnp.sum(message_grad * filtered_ref[b], axis=1, keepdims=True) for b in range(basis_count)
    ]
    radial = jnp.concatenate(columns, axis=1)
    row = 0
    packed_ref[row : row + basis_count, :] = jnp.transpose(radial)
    row += basis_count
    packed_ref[row : row + width, :] = matmul_nt(messages_ref[...], before_grad, highest)
    row += width
    packed_ref[row : row + charge_count, :] = matmul_nt(
        grad, hidden_ref[...].astype(f32), highest
    )
    row += charge_count
    packed_ref[row:, :] = jnp.zeros((packed_ref.shape[0] - row, width), f32)
    one_hot = (
        lax.broadcasted_iota(jnp.int32, (kinds, atoms), 0) == species_ref[...]
    ).astype(f32)
    packed_ref[row : row + kinds, 0:charge_count] = matmul_nt(one_hot, grad, highest)


def summed(values):
    while len(values) > 1:
        values = [values[i] + values[i + 1] for i in range(0, len(values), 2)]
    return values[0]


def halves_kernel(*refs, first, count):
    *value_refs, sum_ref = refs
    value = summed([ref[...] for ref in value_refs])
    high = value.astype(bf16)
    sum_ref[0 : value.shape[0], :] = high
    rest = value[first : first + count, :] - high[first : first + count, :].astype(f32)
    sum_ref[value.shape[0] :, :] = rest.astype(bf16)


def step_kernel(*refs):
    *total_refs, radial_ref, mix_ref, charge_ref, species_ref, total_ref = refs
    basis_count, width = radial_ref.shape
    charge_count = charge_ref.shape[0]
    kinds = species_ref.shape[0]
    total = summed([ref[...].astype(f32) for ref in total_refs])
    rows = total_ref.shape[0]
    total_ref[...] = total[0:rows, :]
    total_ref[basis_count : basis_count + width, :] += total[rows:, :]

    def normalized(gradient):
        mean = jnp.sum(gradient * gradient, keepdims=True) * (1.0 / gradient.size)
        return gradient * lax.rsqrt(mean + 1e-06)

    row = 0
    radial_ref[...] = normalized(total_ref[row : row + basis_count, :])
    row += basis_count
    mix_ref[...] = normalized(total_ref[row : row + width, :])
    row += width
    charge_ref[...] = normalized(total_ref[row : row + charge_count, :])
    row += charge_count
    species_ref[...] = normalized(total_ref[row : row + kinds, 0:charge_count])


def shaped(*dims, kind=f32):
    return jax.ShapeDtypeStruct(dims, kind)


def kernel(body, name, out_shape, scratch, nanoseconds, *operands, scalars=(), wanted=0):
    outs = out_shape if isinstance(out_shape, tuple) else (out_shape,)
    held = sum(math.prod(x.shape) * x.dtype.itemsize for x in (*outs, *scratch, *operands))
    in_vmem = pl.BlockSpec(memory_space=pltpu.VMEM)
    in_smem = pl.BlockSpec(memory_space=pltpu.SMEM)
    return pl.pallas_call(
        body,
        out_shape=out_shape,
        in_specs=[in_smem] * len(scalars) + [in_vmem] * len(operands),
        out_specs=tuple(in_vmem for _ in outs) if isinstance(out_shape, tuple) else in_vmem,
        scratch_shapes=[pltpu.VMEM(x.shape, x.dtype) for x in scratch],
        compiler_params=pltpu.CompilerParams(vmem_limit_bytes=max(held + spare_vmem, wanted)),
        cost_estimate=pl.CostEstimate(
            flops=nanoseconds * 1_000_000, bytes_accessed=held, transcendentals=0
        ),
        name=name,
    )(*scalars, *operands)


def across(value, bits):
    domains = lax.axis_size("dom")
    return lax.ppermute(value, "dom", [(i, i ^ bits) for i in range(domains)])


def on_device(
    features,
    positions,
    neighbours,
    neighbour_count,
    ghost_sends,
    species,
    wave_index,
    force_ref,
    radial_weight,
    mix_weight,
    charge_weight,
    species_charge,
):
    atoms, width = features.shape
    basis_count = radial_weight.shape[0]
    charge_count = charge_weight.shape[1]
    kinds = species_charge.shape[0]
    wave_count = wave_index.shape[1]
    domains = lax.axis_size("dom")
    box_x = 1.25 * (atoms * domains) / 64
    group = 2 if domains % 2 == 0 else 1
    while (
        group < domains
        and 4 * wave_count // group * atoms * domains > waves_bytes
        and wave_count % (256 * group) == 0
    ):
        group *= 2
    share = wave_count // group
    entries = atoms + 2 * ghost_sends.shape[1]

    me = lax.axis_index("dom")
    blocks = 4 if domains % 4 == 0 else 2
    where = jnp.stack([me % 2, me % group, me % blocks]).astype(jnp.int32)
    packed = kernel(
        pack_kernel,
        "pack",
        shaped(atoms + 16 * (atoms // width), width, kind=bf16),
        (),
        1_000,
        features,
        positions,
        ghost_sends,
        wanted=60 * 1024 * 1024,
    )
    near = across(packed, 1)
    beyond = [(i, (i + 1 if i % 2 else i - 1) % domains) for i in range(domains)]
    far = lax.ppermute(packed, "dom", beyond)
    species_row = species[None, :]
    slots = neighbours.T
    charge_rows = charge_weight.T

    sofar, words, *local, extra = kernel(
        lambda *refs: own_kernel(*refs, box_x=box_x),
        "own",
        (
            shaped(basis_count, width, atoms),
            shaped(entries // 32, atoms, kind=jnp.int32),
            shaped(width, atoms, kind=bf16),
            shaped(charge_count, atoms),
            shaped(2 * width + charge_count, width),
            shaped(24, atoms),
        ),
        (
            shaped(atoms, 8),
            shaped(basis_count, atoms, atoms, kind=bf16),
        ),
        4_000,
        features,
        positions,
        force_ref,
        slots,
        neighbour_count[None, :],
        species_row,
        radial_weight,
        mix_weight,
        charge_rows,
        species_charge,
        wanted=own_vmem,
    )
    ghosts = ghost_sends.shape[1]
    scratch = (
        shaped(ghosts // 32, atoms, kind=jnp.int32),
        shaped(ghosts, 8),
        shaped(basis_count, ghosts, atoms, kind=bf16),
    )
    sofar = kernel(
        lambda *refs: near_kernel(*refs, box_x=box_x),
        "near",
        shaped(basis_count, width, atoms),
        scratch,
        3_000,
        near,
        sofar,
        words,
        extra,
        scalars=(where,),
    )
    filtered, messages, before, hidden, shared = kernel(
        lambda *refs: edge_kernel(*refs, box_x=box_x),
        "edges",
        (
            shaped(basis_count, width, atoms),
            shaped(width, atoms),
            shaped(width, atoms),
            shaped(width, atoms, kind=bf16),
            shaped(1, charge_count + 16, atoms, kind=bf16),
        ),
        scratch,
        4_000,
        far,
        sofar,
        words,
        *local,
        extra,
        scalars=(where,),
    )
    column = jnp.concatenate(
        [shared] + [across(shared, bits) for bits in range(blocks, domains, blocks)], axis=0
    )
    columns = [column] + [across(column, bits) for bits in range(1, blocks)]
    early = (0, blocks - 1) if blocks > 2 else (0,)
    waves_early, parts = zip(
        *[
            kernel(
                lambda *refs: phase_kernel(*refs, charge_count=charge_count),
                "phases",
                (
                    shaped(domains // blocks, 2 * share, atoms, kind=bf16),
                    shaped(charge_count, 2 * share),
                ),
                (),
                3_000,
                columns[r],
                wave_index,
                scalars=(where,),
            )
            for r in early
        ]
    )
    waves, weights, *force_parts = kernel(
        lambda *refs: structure_kernel(
            *refs, group=group, blocks=blocks, early=early, charge_count=charge_count, box_x=box_x
        ),
        "structure",
        (
            shaped(domains - len(early) * (domains // blocks), 2 * share, atoms, kind=bf16),
            shaped(3 * charge_count, 2 * share),
        )
        + (shaped(3, domains, atoms),) * group,
        (),
        8_000,
        *columns,
        *waves_early,
        *parts,
        wave_index,
        scalars=(where,),
    )
    force_parts = force_parts[:1] + [across(force_parts[m], m) for m in range(1, group)]
    fields = kernel(
        lambda *refs: field_kernel(
            *refs, group=group, blocks=blocks, early=early, count=domains // blocks
        ),
        "fields",
        (shaped(3 * charge_count, atoms),) * group,
        (),
        2_000,
        weights,
        *waves_early,
        waves,
    )
    forces, errors, back, *grad_parts = kernel(
        lambda *refs: gradient_kernel(
            *refs, group=group, blocks=blocks, early=early, charge_count=charge_count, box_x=box_x
        ),
        "gradient",
        (
            shaped(3, atoms),
            shaped(8, atoms),
            shaped(charge_count, 2 * share),
        )
        + (shaped(charge_count, atoms, kind=bf16),) * (group - 1),
        (shaped(3, domains, atoms),),
        5_000,
        *columns,
        *force_parts,
        *waves_early,
        *fields[1:],
        wave_index,
        waves,
        scalars=(where,),
    )
    own_part = kernel(
        own_gradient_kernel,
        "own_gradient",
        shaped(charge_count, atoms),
        (),
        1_500,
        errors,
        fields[0],
        back,
        waves_early[0],
    )
    grad_parts = [own_part] + [across(grad_parts[m - 1], m) for m in range(1, group)]

    rows = basis_count + width + charge_count + kinds
    rows = -(-rows // 16) * 16
    packed = kernel(
        lambda *refs: weights_kernel(*refs, group=group, kinds=kinds),
        "weights",
        shaped(rows, width),
        (),
        3_000,
        *grad_parts,
        filtered,
        messages,
        before,
        hidden,
        species_row,
        mix_weight,
        charge_rows,
    )
    packed = kernel(
        lambda *refs: halves_kernel(*refs, first=basis_count, count=width),
        "halves",
        shaped(rows + width, width, kind=bf16),
        (),
        1_000,
        packed,
        *[across(packed, r) for r in range(1, blocks)],
    )
    totals = [packed] + [across(packed, bits) for bits in range(blocks, domains, blocks)]
    radial_step, mix_step, charge_step, species_step = kernel(
        step_kernel,
        "steps",
        (
            shaped(basis_count, width),
            shaped(width, width),
            shaped(charge_count, width),
            shaped(kinds, charge_count),
        ),
        (shaped(rows, width),),
        2_000,
        *totals,
    )
    return forces, radial_step, mix_step, charge_step.T, species_step


def solution(mesh):
    placed = (
        P(("cell", "dom"), None),
        P(None, ("cell", "dom")),
        P(("cell", "dom"), None),
        P(("cell", "dom")),
        P(None, ("cell", "dom")),
        P(("cell", "dom")),
        P(),
        P(None, ("cell", "dom")),
        P(),
        P(),
        P(),
        P(),
    )
    return jax.shard_map(
        on_device,
        mesh=mesh,
        in_specs=placed,
        out_specs=(
            P(None, ("cell", "dom")),
            P("cell", None),
            P("cell", None),
            P("cell", None),
            P("cell", None),
        ),
        check_vma=False,
    )
```

```python
import math

import jax
import jax.numpy as jnp
import numpy as np
from jax import lax
from jax.experimental import pallas as pl
from jax.experimental.pallas import tpu as pltpu
from jax.sharding import PartitionSpec as P

cutoff_radius = 5.0
kernel_width = 1.0
basis_width = 0.5
box_side = 20.0
two_pi = 6.283185307179586
highest = lax.Precision.HIGHEST
f32 = jnp.float32
bf16 = jnp.bfloat16
spare_vmem = 4 * 1024 * 1024
waves_bytes = 8 * 1024 * 1024
own_vmem = 50 * 1024 * 1024


def fitted(function, degrees, reach):
    nodes = reach * np.cos((np.arange(400) + 0.5) * np.pi / 400)
    powers = np.stack([nodes**d for d in degrees], axis=1)
    return [float(c) for c in np.linalg.lstsq(powers, function(nodes), rcond=None)[0]]


sine_terms = fitted(lambda x: np.sin(np.pi * x), (1, 3, 5, 7, 9), 0.5)
short_sine = fitted(lambda x: math.sqrt(2) * np.sin(np.pi * x), (1, 3, 5, 7), 0.5)
short_cosine = fitted(lambda x: math.sqrt(2) * np.cos(np.pi * x), (0, 2, 4, 6), 0.5)


def horner(terms, square):
    value = terms[-1]
    for term in terms[-2::-1]:
        value = value * square + term
    return value


def matmul(left, right, precision=None):
    return lax.dot_general(
        left, right, (((1,), (0,)), ((), ())), precision=precision, preferred_element_type=f32
    )


def matmul_nt(left, right, precision=None):
    return lax.dot_general(
        left, right, (((1,), (1,)), ((), ())), precision=precision, preferred_element_type=f32
    )


def turned(value):
    return jnp.transpose(value.astype(f32)).astype(value.dtype)


def sigmoid(value):
    return 1.0 / (1.0 + jnp.exp(-value))


def pieces_of(value):
    first = value.astype(bf16).astype(f32)
    rest = value - first
    second = rest.astype(bf16).astype(f32)
    return first, second, rest - second


def pack_kernel(feat_ref, positions_ref, ghost_ref, packed_ref):
    atoms, width = feat_ref.shape
    packed_ref[0:atoms, :] = feat_ref[...]
    extra = jnp.concatenate(
        pieces_of(positions_ref[...])
        + (ghost_ref[...].astype(f32), jnp.zeros((5, atoms), f32)),
        axis=0,
    ).astype(bf16)
    for part in range(atoms // width):
        first = atoms + part * 16
        packed_ref[first : first + 16, :] = extra[:, part * width : (part + 1) * width]


def pair_blocks(count, coords_ref, own_rows, words_ref, pair_ref, box_x):
    basis_count, _, atoms = pair_ref.shape
    centers = [
        0.5 + (cutoff_radius - 0.5) * float(b) / (basis_count - 1) for b in range(basis_count)
    ]
    scale = -math.log2(math.e) / (basis_width * basis_width)
    middle = basis_count // 2
    gap = centers[1] - centers[0]
    own_x, own_y, own_z = own_rows[0:1, :], own_rows[1:2, :], own_rows[2:3, :]
    step = 32

    def block(index, carry):
        places = pl.ds(pl.multiple_of(index * step, step), step)
        coords = coords_ref[places, :]
        total = jnp.zeros((step, atoms), f32)
        for axis, (mine, length) in enumerate(
            ((own_x, box_x), (own_y, box_side), (own_z, box_side))
        ):
            away = coords[:, axis : axis + 1] - mine
            away = away - length * jnp.floor(away * (1.0 / length) + 0.5)
            total = total + away * away
        distance = jnp.sqrt(total)
        word = words_ref[pl.ds(index, 1), :]
        sublane = lax.broadcasted_iota(jnp.int32, (step, atoms), 0)
        is_live = (jnp.right_shift(jnp.broadcast_to(word, (step, atoms)), sublane) & 1) != 0
        half = jnp.minimum(distance, cutoff_radius) * (1.0 / cutoff_radius) - 0.5
        fade = 0.5 - 0.5 * (half * horner(sine_terms, half * half))
        weight = jnp.where(jnp.logical_and(is_live, distance < cutoff_radius), fade, 0.0)
        offset = jnp.minimum(distance, cutoff_radius) - centers[middle]
        value = jnp.exp2(offset * offset * scale)
        for direction in (1, -1):
            ratio = jnp.exp2(offset * (-2.0 * direction * gap * scale))
            running = value
            for b in range(middle, basis_count) if direction == 1 else range(middle - 1, -1, -1):
                if b != middle:
                    running = running * ratio
                basis = running * math.exp(-(((b - middle) * gap / basis_width) ** 2))
                basis = basis.astype(bf16).astype(f32)
                pair_ref[b, places, :] = (weight * basis).astype(bf16)
        return carry

    lax.fori_loop(0, count // step, block, 0, unroll=8)


def own_kernel(
    feat_ref,
    positions_ref,
    force_ref,
    slots_ref,
    count_ref,
    species_ref,
    radial_ref,
    mix_ref,
    charge_ref,
    offset_ref,
    filtered_ref,
    words_ref,
    own_ref,
    shift_ref,
    weights_ref,
    extra_ref,
    coords_ref,
    pair_ref,
    *,
    box_x,
):
    atoms, width = feat_ref.shape
    slots = slots_ref.shape[0]
    basis_count = radial_ref.shape[0]
    own_rows = positions_ref[...]
    own_feat = turned(feat_ref[...])
    own_ref[...] = own_feat
    coords_ref[...] = jnp.transpose(
        jnp.concatenate([own_rows, jnp.zeros((5, atoms), f32)], axis=0)
    )

    listed = slots_ref[...]
    live = lax.broadcasted_iota(jnp.int32, (slots, atoms), 0) < count_ref[...]
    word_of = jnp.where(live, listed >> 5, -1)
    bit = jnp.left_shift(jnp.ones_like(listed), listed & 31)
    for word in range(words_ref.shape[0]):
        value = jnp.where(word_of == word, bit, 0)
        rows = slots
        while rows > 1:
            rows //= 2
            value = value[:rows] | value[rows:]
        words_ref[word : word + 1, :] = value

    pair_blocks(atoms, coords_ref, own_rows, words_ref, pair_ref, box_x)
    for b in range(basis_count):
        filtered_ref[b] = matmul(own_feat, pair_ref[b])

    kinds = offset_ref.shape[0]
    one_hot = (
        lax.broadcasted_iota(jnp.int32, (kinds, atoms), 0) == species_ref[...]
    ).astype(f32)
    shift_ref[...] = matmul(jnp.transpose(offset_ref[...]), one_hot, highest)
    charge_count = charge_ref.shape[0]
    weights_ref[0:width, :] = jnp.transpose(mix_ref[...].astype(f32))
    weights_ref[width : width + charge_count, :] = charge_ref[...].astype(f32)
    weights_ref[width + charge_count :, 0:basis_count] = jnp.transpose(
        radial_ref[...].astype(f32)
    )
    lengths = (box_x, box_side, box_side)
    turns = jnp.concatenate([own_rows[a : a + 1, :] * (1.0 / lengths[a]) for a in range(3)], axis=0)
    target = force_ref[...]
    high = target.astype(bf16).astype(f32)
    extra_ref[0:16, :] = jnp.concatenate(
        pieces_of(turns) + (high, target - high, jnp.zeros((1, atoms), f32)), axis=0
    )
    extra_ref[16:24, :] = jnp.concatenate([own_rows, jnp.zeros((5, atoms), f32)], axis=0)


def ghost_pairs(ref, is_low, words_ref, extra_ref, ghost_words_ref, coords_ref, pair_ref, box_x):
    _, ghosts, atoms = pair_ref.shape
    width = ref.shape[1]
    extra = jnp.concatenate(
        [ref[atoms + part * 16 : atoms + part * 16 + 16, :] for part in range(atoms // width)],
        axis=1,
    )
    sends = extra[8:16, :].astype(f32)
    sends = jnp.where(is_low, sends[2:3, :], sends[1:2, :])
    site = lax.broadcasted_iota(jnp.int32, (atoms, ghosts), 0).astype(f32)
    chosen = (site == sends).astype(bf16)
    moved = matmul(extra, chosen)
    moved = moved[0:3, :] + (moved[3:6, :] + moved[6:9, :])
    coords_ref[...] = jnp.transpose(jnp.concatenate([moved, jnp.zeros((5, ghosts), f32)], axis=0))
    count = ghosts // 32
    first = jnp.where(is_low, atoms // 32, atoms // 32 + count)
    ghost_words_ref[...] = words_ref[pl.ds(pl.multiple_of(first, 8), count), :]
    pair_blocks(ghosts, coords_ref, extra_ref[16:24, :], ghost_words_ref, pair_ref, box_x)
    return matmul(turned(ref[0:atoms, :]), chosen).astype(bf16)


def near_kernel(
    where_ref,
    near_ref,
    sofar_ref,
    words_ref,
    extra_ref,
    filtered_ref,
    ghost_words_ref,
    coords_ref,
    pair_ref,
    *,
    box_x,
):
    feat = ghost_pairs(
        near_ref,
        where_ref[0] == 1,
        words_ref,
        extra_ref,
        ghost_words_ref,
        coords_ref,
        pair_ref,
        box_x,
    )
    for b in range(filtered_ref.shape[0]):
        filtered_ref[b] = sofar_ref[b] + matmul(feat, pair_ref[b])


def edge_kernel(
    where_ref,
    far_ref,
    sofar_ref,
    words_ref,
    own_ref,
    shift_ref,
    weights_ref,
    extra_ref,
    filtered_ref,
    messages_ref,
    before_ref,
    hidden_ref,
    shared_ref,
    ghost_words_ref,
    coords_ref,
    pair_ref,
    *,
    box_x,
):
    width, atoms = own_ref.shape
    charge_count = shift_ref.shape[0]
    feat = ghost_pairs(
        far_ref,
        where_ref[0] == 0,
        words_ref,
        extra_ref,
        ghost_words_ref,
        coords_ref,
        pair_ref,
        box_x,
    )
    messages = jnp.zeros((width, atoms), f32)
    for b in range(filtered_ref.shape[0]):
        filtered = sofar_ref[b] + matmul(feat, pair_ref[b])
        filtered_ref[b] = filtered
        messages = messages + weights_ref[width + charge_count :, b : b + 1] * filtered
    messages_ref[...] = messages
    before = matmul(weights_ref[0:width, :], messages, highest)
    before_ref[...] = before
    hidden = (own_ref[...].astype(f32) + before * sigmoid(before)).astype(bf16)
    hidden_ref[...] = hidden
    charges = matmul(weights_ref[width : width + charge_count, :].astype(bf16), hidden)
    shared_ref[0, 0:charge_count, :] = (charges + shift_ref[...]).astype(bf16)
    shared_ref[0, charge_count : charge_count + 16, :] = extra_ref[0:16, :].astype(bf16)


def wave_rows(wave_ref, first, count, box_x, total_atoms):
    index = wave_ref[:, pl.ds(first, count)].astype(f32)
    scales = (two_pi / box_x, two_pi / box_side, two_pi / box_side)
    waves = [index[a : a + 1, :] * scales[a] for a in range(3)]
    squares = waves[0] * waves[0] + waves[1] * waves[1] + waves[2] * waves[2]
    damping = jnp.exp(-0.5 * kernel_width * kernel_width * squares) * (1.0 / total_atoms)
    return index, waves, damping


def wave_columns(wave_ref, first, share):
    index = wave_ref[:, pl.ds(first, share)].astype(f32)
    return jnp.transpose(
        jnp.concatenate([index] * 3 + [jnp.zeros((7, share), f32)], axis=0)
    ).astype(bf16)


def fill_waves(columns, shared_ref, j, charge_count, waves_ref, place):
    share = columns.shape[0]
    shift = 12582912.0
    turns = matmul(columns, shared_ref[j, charge_count : charge_count + 16, :])
    turns = turns - ((turns + shift) - shift)
    square = turns * turns
    half_sine = turns * horner(short_sine, square)
    half_cosine = horner(short_cosine, square)
    waves_ref[place, 0:share, :] = (half_sine * half_cosine).astype(bf16)
    waves_ref[place, share : 2 * share, :] = (1.0 - half_sine * half_sine).astype(bf16)


def phase_kernel(where_ref, shared_ref, wave_ref, waves_ref, part_ref, *, charge_count):
    count = shared_ref.shape[0]
    share = waves_ref.shape[1] // 2
    columns = wave_columns(wave_ref, pl.multiple_of(where_ref[1] * share, share), share)

    def block(j, carry):
        fill_waves(columns, shared_ref, j, charge_count, waves_ref, j)
        return carry

    lax.fori_loop(0, count, block, 0, unroll=4)
    part = jnp.zeros(part_ref.shape, f32)
    for j in range(count):
        part = part + matmul_nt(shared_ref[j, 0:charge_count, :], waves_ref[j])
    part_ref[...] = part


def placed_waves(early, early_refs, late, waves_ref, count):
    return [
        early_refs[early.index(r)].at[j]
        if r in early
        else waves_ref.at[j * len(late) + late.index(r)]
        for j in range(count)
        for r in range(len(early) + len(late))
    ]


def structure_kernel(where_ref, *refs, group, blocks, early, charge_count, box_x):
    shared_refs, early_refs = refs[:blocks], refs[blocks : blocks + len(early)]
    part_refs, refs = refs[blocks + len(early) : blocks + 2 * len(early)], refs[blocks + 2 * len(early) :]
    wave_ref, waves_ref, weights_ref, *force_refs = refs
    late = [r for r in range(blocks) if r not in early]
    count, _, atoms = shared_refs[0].shape
    share = waves_ref.shape[1] // 2
    first = pl.multiple_of(where_ref[1] * share, share)
    _, waves, damping = wave_rows(wave_ref, first, share, box_x, blocks * count * atoms)
    columns = wave_columns(wave_ref, first, share)

    def block(j, carry):
        for i, r in enumerate(late):
            fill_waves(columns, shared_refs[r], j, charge_count, waves_ref, j * len(late) + i)
        return carry

    lax.fori_loop(0, count, block, 0, unroll=4)
    waves_of = placed_waves(early, early_refs, late, waves_ref, count)
    structure = sum(ref[...] for ref in part_refs)
    for d in range(blocks * count):
        j, r = divmod(d, blocks)
        if r in late:
            structure = structure + matmul_nt(
                shared_refs[r][j, 0:charge_count, :], waves_of[d][...]
            )
    along_sin = structure[:, :share] * damping
    along_cos = structure[:, share:] * damping
    to_sine = jnp.concatenate([along_cos * waves[a] for a in range(3)], axis=0)
    to_cosine = jnp.concatenate([-along_sin * waves[a] for a in range(3)], axis=0)
    weights = jnp.concatenate([to_sine, to_cosine], axis=1)
    weights_ref[...] = weights
    weights = weights.astype(bf16)
    for d in range(blocks * count):
        j, r = divmod(d, blocks)
        field = matmul(weights, waves_of[d][...])
        charges = shared_refs[r][j, 0:charge_count, :].astype(f32)
        for a in range(3):
            row = jnp.sum(
                field[a * charge_count : (a + 1) * charge_count, :] * charges,
                axis=0,
                keepdims=True,
            )
            for m in range(group):
                force_refs[m][a, d ^ m : (d ^ m) + 1, :] = row


def field_kernel(*refs, group, blocks, early, count):
    weights_ref, refs = refs[0], refs[1:]
    early_refs, waves_ref, field_refs = refs[: len(early)], refs[len(early)], refs[len(early) + 1 :]
    late = [r for r in range(blocks) if r not in early]
    waves_of = placed_waves(early, early_refs, late, waves_ref, count)
    weights = weights_ref[...]
    weights_high = weights.astype(bf16)
    weights_low = (weights - weights_high.astype(f32)).astype(bf16)
    for m in range(group):
        block = waves_of[m][...]
        field_refs[m][...] = matmul(weights_high, block) + matmul(weights_low, block)


def charge_gradient(errors, field, back, block):
    charge_count = back.shape[0]
    high = back.astype(bf16)
    low = (back - high.astype(f32)).astype(bf16)
    grad = matmul(high, block) + matmul(low, block)
    for a in range(3):
        grad = grad + errors[a] * field[a * charge_count : (a + 1) * charge_count, :]
    return grad


def gradient_kernel(where_ref, *refs, group, blocks, early, charge_count, box_x):
    shared_refs, part_refs = refs[:blocks], refs[blocks : blocks + group]
    refs = refs[blocks + group :]
    early_refs, refs = refs[: len(early)], refs[len(early) :]
    field_refs, refs = refs[: group - 1], refs[group - 1 :]
    wave_ref, waves_ref, forces_ref, errors_ref, back_ref, *grad_refs, total_ref = refs
    late = [r for r in range(blocks) if r not in early]
    count, _, atoms = shared_refs[0].shape
    share = waves_ref.shape[1] // 2
    first = pl.multiple_of(where_ref[1] * share, share)
    _, waves, damping = wave_rows(wave_ref, first, share, box_x, blocks * count * atoms)
    waves_of = placed_waves(early, early_refs, late, waves_ref, count)
    total = part_refs[0][...]
    for m in range(1, group):
        total = total + part_refs[m][...]
    total_ref[...] = total
    for a in range(3):
        forces_ref[a : a + 1, :] = total[a, 0:1, :]

    def errors_of(d):
        j, r = divmod(d, blocks)
        target = shared_refs[r][j, charge_count : charge_count + 16, :].astype(f32)
        target = target[9:12, :] + target[12:15, :]
        return [2.0 * (total_ref[a, d : d + 1, :] - target[a : a + 1, :]) for a in range(3)]

    by_wave = jnp.zeros((3 * charge_count, 2 * share), f32)
    for d in range(blocks * count):
        j, r = divmod(d, blocks)
        charges = shared_refs[r][j, 0:charge_count, :].astype(f32)
        errors = errors_of(d)
        scaled = jnp.concatenate([errors[a] * charges for a in range(3)], axis=0).astype(bf16)
        by_wave = by_wave + matmul_nt(scaled, waves_of[d][...])
        if d == 0:
            errors_ref[...] = jnp.concatenate(errors + [jnp.zeros((5, atoms), f32)], axis=0)

    def along(value):
        return sum(
            waves[a] * value[a * charge_count : (a + 1) * charge_count, :] for a in range(3)
        )

    back_cos = damping * along(by_wave[:, :share])
    back_sin = -damping * along(by_wave[:, share:])
    back = jnp.concatenate([back_sin, back_cos], axis=1)
    back_ref[...] = back
    for m in range(1, group):
        grad_refs[m - 1][...] = charge_gradient(
            errors_of(m), field_refs[m - 1][...], back, waves_of[m][...]
        ).astype(bf16)


def own_gradient_kernel(errors_ref, field_ref, back_ref, waves_ref, grad_ref):
    errors = errors_ref[...]
    grad_ref[...] = charge_gradient(
        [errors[a : a + 1, :] for a in range(3)], field_ref[...], back_ref[...], waves_ref[0]
    )


def summed(values):
    while len(values) > 1:
        values = [values[i] + values[i + 1] for i in range(0, len(values), 2)]
    return values[0]


def split_rows(value, first, count, sums_ref):
    rows = value.shape[0]
    high = value.astype(bf16)
    sums_ref[0:rows, :] = high
    rest = value[first : first + count, :] - high[first : first + count, :].astype(f32)
    sums_ref[rows:, :] = rest.astype(bf16)


def joined_rows(refs, first, count, value_ref):
    total = summed([ref[...].astype(f32) for ref in refs])
    rows = value_ref.shape[0]
    value_ref[...] = total[0:rows, :]
    value_ref[first : first + count, :] += total[rows:, :]


def halves_kernel(*refs, first, count):
    *part_refs, sums_ref, value_ref = refs
    joined_rows(part_refs, first, count, value_ref)
    split_rows(value_ref[...], first, count, sums_ref)


def weights_kernel(*refs, group, kinds):
    part_refs = refs[:group]
    (
        filtered_ref,
        messages_ref,
        before_ref,
        hidden_ref,
        species_ref,
        mix_ref,
        charge_ref,
        sums_ref,
        packed_ref,
    ) = refs[group:]
    charge_count, atoms = part_refs[0].shape
    basis_count, width, _ = filtered_ref.shape
    grad = part_refs[0][...].astype(f32)
    for m in range(1, group):
        grad = grad + part_refs[m][...].astype(f32)
    before = before_ref[...]
    gate = sigmoid(before)
    upstream = matmul(jnp.transpose(charge_ref[...].astype(f32)), grad, highest)
    before_grad = upstream * (gate * (1.0 + before * (1.0 - gate)))
    message_grad = matmul(mix_ref[...].astype(f32), before_grad, highest)
    columns = [
        jnp.sum(message_grad * filtered_ref[b], axis=1, keepdims=True) for b in range(basis_count)
    ]
    radial = jnp.concatenate(columns, axis=1)
    row = 0
    packed_ref[row : row + basis_count, :] = jnp.transpose(radial)
    row += basis_count
    packed_ref[row : row + width, :] = matmul_nt(messages_ref[...], before_grad, highest)
    row += width
    packed_ref[row : row + charge_count, :] = matmul_nt(
        grad, hidden_ref[...].astype(f32), highest
    )
    row += charge_count
    packed_ref[row:, :] = jnp.zeros((packed_ref.shape[0] - row, width), f32)
    one_hot = (
        lax.broadcasted_iota(jnp.int32, (kinds, atoms), 0) == species_ref[...]
    ).astype(f32)
    packed_ref[row : row + kinds, 0:charge_count] = matmul_nt(one_hot, grad, highest)
    split_rows(packed_ref[...], basis_count, width, sums_ref)


def step_kernel(*refs):
    *total_refs, radial_ref, mix_ref, charge_ref, species_ref, total_ref = refs
    basis_count, width = radial_ref.shape
    charge_count = charge_ref.shape[0]
    kinds = species_ref.shape[0]
    joined_rows(total_refs, basis_count, width, total_ref)

    def normalized(gradient):
        mean = jnp.sum(gradient * gradient, keepdims=True) * (1.0 / gradient.size)
        return gradient * lax.rsqrt(mean + 1e-06)

    row = 0
    radial_ref[...] = normalized(total_ref[row : row + basis_count, :])
    row += basis_count
    mix_ref[...] = normalized(total_ref[row : row + width, :])
    row += width
    charge_ref[...] = normalized(total_ref[row : row + charge_count, :])
    row += charge_count
    species_ref[...] = normalized(total_ref[row : row + kinds, 0:charge_count])


def shaped(*dims, kind=f32):
    return jax.ShapeDtypeStruct(dims, kind)


def kernel(body, name, out_shape, scratch, nanoseconds, *operands, scalars=(), wanted=0):
    outs = out_shape if isinstance(out_shape, tuple) else (out_shape,)
    held = sum(math.prod(x.shape) * x.dtype.itemsize for x in (*outs, *scratch, *operands))
    in_vmem = pl.BlockSpec(memory_space=pltpu.VMEM)
    in_smem = pl.BlockSpec(memory_space=pltpu.SMEM)
    return pl.pallas_call(
        body,
        out_shape=out_shape,
        in_specs=[in_smem] * len(scalars) + [in_vmem] * len(operands),
        out_specs=tuple(in_vmem for _ in outs) if isinstance(out_shape, tuple) else in_vmem,
        scratch_shapes=[pltpu.VMEM(x.shape, x.dtype) for x in scratch],
        compiler_params=pltpu.CompilerParams(vmem_limit_bytes=max(held + spare_vmem, wanted)),
        cost_estimate=pl.CostEstimate(
            flops=nanoseconds * 1_000_000, bytes_accessed=held, transcendentals=0
        ),
        name=name,
    )(*scalars, *operands)


def across(value, bits):
    domains = lax.axis_size("dom")
    return lax.ppermute(value, "dom", [(i, i ^ bits) for i in range(domains)])


def on_device(
    features,
    positions,
    neighbours,
    neighbour_count,
    ghost_sends,
    species,
    wave_index,
    force_ref,
    radial_weight,
    mix_weight,
    charge_weight,
    species_charge,
):
    atoms, width = features.shape
    basis_count = radial_weight.shape[0]
    charge_count = charge_weight.shape[1]
    kinds = species_charge.shape[0]
    wave_count = wave_index.shape[1]
    domains = lax.axis_size("dom")
    box_x = 1.25 * (atoms * domains) / 64
    group = 2 if domains % 2 == 0 else 1
    while (
        group < domains
        and 4 * wave_count // group * atoms * domains > waves_bytes
        and wave_count % (256 * group) == 0
    ):
        group *= 2
    share = wave_count // group
    entries = atoms + 2 * ghost_sends.shape[1]

    me = lax.axis_index("dom")
    blocks = 4 if domains % 4 == 0 else 2
    where = jnp.stack([me % 2, me % group, me % blocks]).astype(jnp.int32)
    packed = kernel(
        pack_kernel,
        "pack",
        shaped(atoms + 16 * (atoms // width), width, kind=bf16),
        (),
        1_000,
        features,
        positions,
        ghost_sends,
        wanted=60 * 1024 * 1024,
    )
    near = across(packed, 1)
    beyond = [(i, (i + 1 if i % 2 else i - 1) % domains) for i in range(domains)]
    far = lax.ppermute(packed, "dom", beyond)
    species_row = species[None, :]
    slots = neighbours.T
    charge_rows = charge_weight.T

    sofar, words, *local, extra = kernel(
        lambda *refs: own_kernel(*refs, box_x=box_x),
        "own",
        (
            shaped(basis_count, width, atoms),
            shaped(entries // 32, atoms, kind=jnp.int32),
            shaped(width, atoms, kind=bf16),
            shaped(charge_count, atoms),
            shaped(2 * width + charge_count, width),
            shaped(24, atoms),
        ),
        (
            shaped(atoms, 8),
            shaped(basis_count, atoms, atoms, kind=bf16),
        ),
        4_000,
        features,
        positions,
        force_ref,
        slots,
        neighbour_count[None, :],
        species_row,
        radial_weight,
        mix_weight,
        charge_rows,
        species_charge,
        wanted=own_vmem,
    )
    ghosts = ghost_sends.shape[1]
    scratch = (
        shaped(ghosts // 32, atoms, kind=jnp.int32),
        shaped(ghosts, 8),
        shaped(basis_count, ghosts, atoms, kind=bf16),
    )
    sofar = kernel(
        lambda *refs: near_kernel(*refs, box_x=box_x),
        "near",
        shaped(basis_count, width, atoms),
        scratch,
        3_000,
        near,
        sofar,
        words,
        extra,
        scalars=(where,),
    )
    filtered, messages, before, hidden, shared = kernel(
        lambda *refs: edge_kernel(*refs, box_x=box_x),
        "edges",
        (
            shaped(basis_count, width, atoms),
            shaped(width, atoms),
            shaped(width, atoms),
            shaped(width, atoms, kind=bf16),
            shaped(1, charge_count + 16, atoms, kind=bf16),
        ),
        scratch,
        4_000,
        far,
        sofar,
        words,
        *local,
        extra,
        scalars=(where,),
    )
    column = jnp.concatenate(
        [shared] + [across(shared, bits) for bits in range(blocks, domains, blocks)], axis=0
    )
    columns = [column] + [across(column, bits) for bits in range(1, blocks)]
    early = (0, blocks - 1) if blocks > 2 else (0,)
    waves_early, parts = zip(
        *[
            kernel(
                lambda *refs: phase_kernel(*refs, charge_count=charge_count),
                "phases",
                (
                    shaped(domains // blocks, 2 * share, atoms, kind=bf16),
                    shaped(charge_count, 2 * share),
                ),
                (),
                3_000,
                columns[r],
                wave_index,
                scalars=(where,),
            )
            for r in early
        ]
    )
    waves, weights, *force_parts = kernel(
        lambda *refs: structure_kernel(
            *refs, group=group, blocks=blocks, early=early, charge_count=charge_count, box_x=box_x
        ),
        "structure",
        (
            shaped(domains - len(early) * (domains // blocks), 2 * share, atoms, kind=bf16),
            shaped(3 * charge_count, 2 * share),
        )
        + (shaped(3, domains, atoms),) * group,
        (),
        8_000,
        *columns,
        *waves_early,
        *parts,
        wave_index,
        scalars=(where,),
    )
    force_parts = force_parts[:1] + [across(force_parts[m], m) for m in range(1, group)]
    fields = kernel(
        lambda *refs: field_kernel(
            *refs, group=group, blocks=blocks, early=early, count=domains // blocks
        ),
        "fields",
        (shaped(3 * charge_count, atoms),) * group,
        (),
        2_000,
        weights,
        *waves_early,
        waves,
    )
    forces, errors, back, *grad_parts = kernel(
        lambda *refs: gradient_kernel(
            *refs, group=group, blocks=blocks, early=early, charge_count=charge_count, box_x=box_x
        ),
        "gradient",
        (
            shaped(3, atoms),
            shaped(8, atoms),
            shaped(charge_count, 2 * share),
        )
        + (shaped(charge_count, atoms, kind=bf16),) * (group - 1),
        (shaped(3, domains, atoms),),
        5_000,
        *columns,
        *force_parts,
        *waves_early,
        *fields[1:],
        wave_index,
        waves,
        scalars=(where,),
    )
    own_part = kernel(
        own_gradient_kernel,
        "own_gradient",
        shaped(charge_count, atoms),
        (),
        1_500,
        errors,
        fields[0],
        back,
        waves_early[0],
    )
    grad_parts = [own_part] + [across(grad_parts[m - 1], m) for m in range(1, group)]

    rows = basis_count + width + charge_count + kinds
    rows = -(-rows // 16) * 16
    packed = kernel(
        lambda *refs: weights_kernel(*refs, group=group, kinds=kinds),
        "weights",
        shaped(rows + width, width, kind=bf16),
        (shaped(rows, width),),
        3_000,
        *grad_parts,
        filtered,
        messages,
        before,
        hidden,
        species_row,
        mix_weight,
        charge_rows,
    )
    packed = kernel(
        lambda *refs: halves_kernel(*refs, first=basis_count, count=width),
        "halves",
        shaped(rows + width, width, kind=bf16),
        (shaped(rows, width),),
        1_000,
        packed,
        *[across(packed, r) for r in range(1, blocks)],
    )
    totals = [packed] + [across(packed, bits) for bits in range(blocks, domains, blocks)]
    radial_step, mix_step, charge_step, species_step = kernel(
        step_kernel,
        "steps",
        (
            shaped(basis_count, width),
            shaped(width, width),
            shaped(charge_count, width),
            shaped(kinds, charge_count),
        ),
        (shaped(rows, width),),
        2_000,
        *totals,
    )
    return forces, radial_step, mix_step, charge_step.T, species_step


def solution(mesh):
    placed = (
        P(("cell", "dom"), None),
        P(None, ("cell", "dom")),
        P(("cell", "dom"), None),
        P(("cell", "dom")),
        P(None, ("cell", "dom")),
        P(("cell", "dom")),
        P(),
        P(None, ("cell", "dom")),
        P(),
        P(),
        P(),
        P(),
    )
    return jax.shard_map(
        on_device,
        mesh=mesh,
        in_specs=placed,
        out_specs=(
            P(None, ("cell", "dom")),
            P("cell", None),
            P("cell", None),
            P("cell", None),
            P("cell", None),
        ),
        check_vma=False,
    )
```

```python
import math

import jax
import jax.numpy as jnp
import numpy as np
from jax import lax
from jax.experimental import pallas as pl
from jax.experimental.pallas import tpu as pltpu
from jax.sharding import PartitionSpec as P

cutoff_radius = 5.0
kernel_width = 1.0
basis_width = 0.5
box_side = 20.0
two_pi = 6.283185307179586
highest = lax.Precision.HIGHEST
f32 = jnp.float32
bf16 = jnp.bfloat16
spare_vmem = 4 * 1024 * 1024
waves_bytes = 8 * 1024 * 1024
own_vmem = 50 * 1024 * 1024


def fitted(function, degrees, reach):
    nodes = reach * np.cos((np.arange(400) + 0.5) * np.pi / 400)
    powers = np.stack([nodes**d for d in degrees], axis=1)
    return [float(c) for c in np.linalg.lstsq(powers, function(nodes), rcond=None)[0]]


sine_terms = fitted(lambda x: np.sin(np.pi * x), (1, 3, 5, 7, 9), 0.5)
short_sine = fitted(lambda x: math.sqrt(2) * np.sin(np.pi * x), (1, 3, 5, 7), 0.5)
short_cosine = fitted(lambda x: math.sqrt(2) * np.cos(np.pi * x), (0, 2, 4, 6), 0.5)


def horner(terms, square):
    value = terms[-1]
    for term in terms[-2::-1]:
        value = value * square + term
    return value


def matmul(left, right, precision=None):
    return lax.dot_general(
        left, right, (((1,), (0,)), ((), ())), precision=precision, preferred_element_type=f32
    )


def matmul_nt(left, right, precision=None):
    return lax.dot_general(
        left, right, (((1,), (1,)), ((), ())), precision=precision, preferred_element_type=f32
    )


def terms_of(value):
    high = value.astype(bf16)
    return high, (value - high.astype(f32)).astype(bf16)


def exact_matmul(left, value, product=matmul):
    high, low = terms_of(value)
    return product(left, high) + product(left, low)


def turned(value):
    return jnp.transpose(value.astype(f32)).astype(value.dtype)


def sigmoid(value):
    return 1.0 / (1.0 + jnp.exp(-value))


def pieces_of(value):
    first = value.astype(bf16).astype(f32)
    rest = value - first
    second = rest.astype(bf16).astype(f32)
    return first, second, rest - second


def pack_kernel(feat_ref, positions_ref, ghost_ref, packed_ref):
    atoms, width = feat_ref.shape
    packed_ref[0:atoms, :] = feat_ref[...]
    extra = jnp.concatenate(
        pieces_of(positions_ref[...])
        + (ghost_ref[...].astype(f32), jnp.zeros((5, atoms), f32)),
        axis=0,
    ).astype(bf16)
    for part in range(atoms // width):
        first = atoms + part * 16
        packed_ref[first : first + 16, :] = extra[:, part * width : (part + 1) * width]


def pair_blocks(count, coords_ref, own_rows, words_ref, pair_ref, box_x):
    basis_count, _, atoms = pair_ref.shape
    centers = [
        0.5 + (cutoff_radius - 0.5) * float(b) / (basis_count - 1) for b in range(basis_count)
    ]
    scale = -math.log2(math.e) / (basis_width * basis_width)
    middle = basis_count // 2
    gap = centers[1] - centers[0]
    own_x, own_y, own_z = own_rows[0:1, :], own_rows[1:2, :], own_rows[2:3, :]
    step = 32

    def block(index, carry):
        places = pl.ds(pl.multiple_of(index * step, step), step)
        coords = coords_ref[places, :]
        total = jnp.zeros((step, atoms), f32)
        for axis, (mine, length) in enumerate(
            ((own_x, box_x), (own_y, box_side), (own_z, box_side))
        ):
            away = coords[:, axis : axis + 1] - mine
            away = away - length * jnp.floor(away * (1.0 / length) + 0.5)
            total = total + away * away
        total = jnp.maximum(total, 1e-20)
        distance = total * lax.rsqrt(total)
        word = words_ref[pl.ds(index, 1), :]
        sublane = lax.broadcasted_iota(jnp.int32, (step, atoms), 0)
        is_live = (jnp.right_shift(jnp.broadcast_to(word, (step, atoms)), sublane) & 1) != 0
        half = jnp.minimum(distance, cutoff_radius) * (1.0 / cutoff_radius) - 0.5
        fade = 0.5 - 0.5 * (half * horner(sine_terms, half * half))
        weight = jnp.where(jnp.logical_and(is_live, distance < cutoff_radius), fade, 0.0)
        offset = jnp.minimum(distance, cutoff_radius) - centers[middle]
        value = jnp.exp2(offset * offset * scale)
        for direction in (1, -1):
            ratio = jnp.exp2(offset * (-2.0 * direction * gap * scale))
            running = value
            for b in range(middle, basis_count) if direction == 1 else range(middle - 1, -1, -1):
                if b != middle:
                    running = running * ratio
                basis = running * math.exp(-(((b - middle) * gap / basis_width) ** 2))
                basis = basis.astype(bf16).astype(f32)
                pair_ref[b, places, :] = (weight * basis).astype(bf16)
        return carry

    lax.fori_loop(0, count // step, block, 0, unroll=8)


def own_kernel(
    feat_ref,
    positions_ref,
    force_ref,
    slots_ref,
    count_ref,
    species_ref,
    radial_ref,
    mix_ref,
    charge_ref,
    offset_ref,
    filtered_ref,
    words_ref,
    own_ref,
    shift_ref,
    weights_ref,
    extra_ref,
    coords_ref,
    pair_ref,
    *,
    box_x,
):
    atoms, width = feat_ref.shape
    slots = slots_ref.shape[0]
    basis_count = radial_ref.shape[0]
    own_rows = positions_ref[...]
    own_feat = turned(feat_ref[...])
    own_ref[...] = own_feat
    coords_ref[...] = jnp.transpose(
        jnp.concatenate([own_rows, jnp.zeros((5, atoms), f32)], axis=0)
    )

    listed = slots_ref[...]
    live = lax.broadcasted_iota(jnp.int32, (slots, atoms), 0) < count_ref[...]
    word_of = jnp.where(live, listed >> 5, -1)
    bit = jnp.left_shift(jnp.ones_like(listed), listed & 31)
    for word in range(words_ref.shape[0]):
        value = jnp.where(word_of == word, bit, 0)
        rows = slots
        while rows > 1:
            rows //= 2
            value = value[:rows] | value[rows:]
        words_ref[word : word + 1, :] = value

    pair_blocks(atoms, coords_ref, own_rows, words_ref, pair_ref, box_x)
    for b in range(basis_count):
        filtered_ref[b] = matmul(own_feat, pair_ref[b])

    kinds = offset_ref.shape[0]
    one_hot = (
        lax.broadcasted_iota(jnp.int32, (kinds, atoms), 0) == species_ref[...]
    ).astype(f32)
    shift_ref[...] = matmul(jnp.transpose(offset_ref[...]), one_hot, highest)
    charge_count = charge_ref.shape[0]
    weights_ref[0:width, :] = jnp.transpose(mix_ref[...].astype(f32))
    weights_ref[width : width + charge_count, :] = charge_ref[...].astype(f32)
    weights_ref[width + charge_count :, 0:basis_count] = jnp.transpose(
        radial_ref[...].astype(f32)
    )
    lengths = (box_x, box_side, box_side)
    turns = jnp.concatenate([own_rows[a : a + 1, :] * (1.0 / lengths[a]) for a in range(3)], axis=0)
    target = force_ref[...]
    high = target.astype(bf16).astype(f32)
    extra_ref[0:16, :] = jnp.concatenate(
        pieces_of(turns) + (high, target - high, jnp.zeros((1, atoms), f32)), axis=0
    )
    extra_ref[16:24, :] = jnp.concatenate([own_rows, jnp.zeros((5, atoms), f32)], axis=0)


def ghost_pairs(ref, is_low, words_ref, extra_ref, ghost_words_ref, coords_ref, pair_ref, box_x):
    _, ghosts, atoms = pair_ref.shape
    width = ref.shape[1]
    extra = jnp.concatenate(
        [ref[atoms + part * 16 : atoms + part * 16 + 16, :] for part in range(atoms // width)],
        axis=1,
    )
    sends = extra[8:16, :].astype(f32)
    sends = jnp.where(is_low, sends[2:3, :], sends[1:2, :])
    site = lax.broadcasted_iota(jnp.int32, (atoms, ghosts), 0).astype(f32)
    chosen = (site == sends).astype(bf16)
    moved = matmul(extra, chosen)
    moved = moved[0:3, :] + (moved[3:6, :] + moved[6:9, :])
    coords_ref[...] = jnp.transpose(jnp.concatenate([moved, jnp.zeros((5, ghosts), f32)], axis=0))
    count = ghosts // 32
    first = jnp.where(is_low, atoms // 32, atoms // 32 + count)
    ghost_words_ref[...] = words_ref[pl.ds(pl.multiple_of(first, 8), count), :]
    pair_blocks(ghosts, coords_ref, extra_ref[16:24, :], ghost_words_ref, pair_ref, box_x)
    return matmul(turned(ref[0:atoms, :]), chosen).astype(bf16)


def near_kernel(
    where_ref,
    near_ref,
    sofar_ref,
    words_ref,
    extra_ref,
    filtered_ref,
    ghost_words_ref,
    coords_ref,
    pair_ref,
    *,
    box_x,
):
    feat = ghost_pairs(
        near_ref,
        where_ref[0] == 1,
        words_ref,
        extra_ref,
        ghost_words_ref,
        coords_ref,
        pair_ref,
        box_x,
    )
    for b in range(filtered_ref.shape[0]):
        filtered_ref[b] = sofar_ref[b] + matmul(feat, pair_ref[b])


def edge_kernel(
    where_ref,
    far_ref,
    sofar_ref,
    words_ref,
    own_ref,
    shift_ref,
    weights_ref,
    extra_ref,
    filtered_ref,
    messages_ref,
    before_ref,
    hidden_ref,
    shared_ref,
    ghost_words_ref,
    coords_ref,
    pair_ref,
    *,
    box_x,
):
    width, atoms = own_ref.shape
    charge_count = shift_ref.shape[0]
    feat = ghost_pairs(
        far_ref,
        where_ref[0] == 0,
        words_ref,
        extra_ref,
        ghost_words_ref,
        coords_ref,
        pair_ref,
        box_x,
    )
    messages = jnp.zeros((width, atoms), f32)
    for b in range(filtered_ref.shape[0]):
        filtered = sofar_ref[b] + matmul(feat, pair_ref[b])
        filtered_ref[b] = filtered
        messages = messages + weights_ref[width + charge_count :, b : b + 1] * filtered
    messages_ref[...] = messages
    before = exact_matmul(weights_ref[0:width, :].astype(bf16), messages)
    before_ref[...] = before
    hidden = (own_ref[...].astype(f32) + before * sigmoid(before)).astype(bf16)
    hidden_ref[...] = hidden
    charges = matmul(weights_ref[width : width + charge_count, :].astype(bf16), hidden)
    shared_ref[0, 0:charge_count, :] = (charges + shift_ref[...]).astype(bf16)
    shared_ref[0, charge_count : charge_count + 16, :] = extra_ref[0:16, :].astype(bf16)


def wave_rows(wave_ref, first, count, box_x, total_atoms):
    index = wave_ref[:, pl.ds(first, count)].astype(f32)
    scales = (two_pi / box_x, two_pi / box_side, two_pi / box_side)
    waves = [index[a : a + 1, :] * scales[a] for a in range(3)]
    squares = waves[0] * waves[0] + waves[1] * waves[1] + waves[2] * waves[2]
    damping = jnp.exp(-0.5 * kernel_width * kernel_width * squares) * (1.0 / total_atoms)
    return index, waves, damping


def wave_columns(wave_ref, first, share):
    index = wave_ref[:, pl.ds(first, share)].astype(f32)
    return jnp.transpose(
        jnp.concatenate([index] * 3 + [jnp.zeros((7, share), f32)], axis=0)
    ).astype(bf16)


def fill_waves(columns, shared_ref, j, charge_count, waves_ref, place):
    share = columns.shape[0]
    shift = 12582912.0
    turns = matmul(columns, shared_ref[j, charge_count : charge_count + 16, :])
    turns = turns - ((turns + shift) - shift)
    square = turns * turns
    half_sine = turns * horner(short_sine, square)
    half_cosine = horner(short_cosine, square)
    waves_ref[place, 0:share, :] = (half_sine * half_cosine).astype(bf16)
    waves_ref[place, share : 2 * share, :] = (1.0 - half_sine * half_sine).astype(bf16)


def phase_kernel(where_ref, shared_ref, wave_ref, waves_ref, part_ref, *, charge_count):
    count = shared_ref.shape[0]
    share = waves_ref.shape[1] // 2
    columns = wave_columns(wave_ref, pl.multiple_of(where_ref[1] * share, share), share)

    def block(j, carry):
        fill_waves(columns, shared_ref, j, charge_count, waves_ref, j)
        return carry

    lax.fori_loop(0, count, block, 0, unroll=4)
    part = jnp.zeros(part_ref.shape, f32)
    for j in range(count):
        part = part + matmul_nt(shared_ref[j, 0:charge_count, :], waves_ref[j])
    part_ref[...] = part


def placed_waves(early, early_refs, late, waves_ref, count):
    return [
        early_refs[early.index(r)].at[j]
        if r in early
        else waves_ref.at[j * len(late) + late.index(r)]
        for j in range(count)
        for r in range(len(early) + len(late))
    ]


def structure_kernel(where_ref, *refs, group, blocks, early, charge_count, box_x):
    shared_refs, early_refs = refs[:blocks], refs[blocks : blocks + len(early)]
    part_refs, refs = refs[blocks + len(early) : blocks + 2 * len(early)], refs[blocks + 2 * len(early) :]
    wave_ref, waves_ref, weights_ref, *force_refs = refs
    late = [r for r in range(blocks) if r not in early]
    count, _, atoms = shared_refs[0].shape
    share = waves_ref.shape[1] // 2
    first = pl.multiple_of(where_ref[1] * share, share)
    _, waves, damping = wave_rows(wave_ref, first, share, box_x, blocks * count * atoms)
    columns = wave_columns(wave_ref, first, share)

    def block(j, carry):
        for i, r in enumerate(late):
            fill_waves(columns, shared_refs[r], j, charge_count, waves_ref, j * len(late) + i)
        return carry

    lax.fori_loop(0, count, block, 0, unroll=4)
    waves_of = placed_waves(early, early_refs, late, waves_ref, count)
    structure = sum(ref[...] for ref in part_refs)
    for d in range(blocks * count):
        j, r = divmod(d, blocks)
        if r in late:
            structure = structure + matmul_nt(
                shared_refs[r][j, 0:charge_count, :], waves_of[d][...]
            )
    along_sin = structure[:, :share] * damping
    along_cos = structure[:, share:] * damping
    to_sine = jnp.concatenate([along_cos * waves[a] for a in range(3)], axis=0)
    to_cosine = jnp.concatenate([-along_sin * waves[a] for a in range(3)], axis=0)
    weights = jnp.concatenate([to_sine, to_cosine], axis=1)
    weights_ref[...] = weights
    weights = weights.astype(bf16)
    for d in range(blocks * count):
        j, r = divmod(d, blocks)
        field = matmul(weights, waves_of[d][...])
        charges = shared_refs[r][j, 0:charge_count, :].astype(f32)
        for a in range(3):
            row = jnp.sum(
                field[a * charge_count : (a + 1) * charge_count, :] * charges,
                axis=0,
                keepdims=True,
            )
            for m in range(group):
                force_refs[m][a, d ^ m : (d ^ m) + 1, :] = row


def field_kernel(*refs, group, blocks, early, count):
    weights_ref, refs = refs[0], refs[1:]
    early_refs, waves_ref, field_refs = refs[: len(early)], refs[len(early)], refs[len(early) + 1 :]
    late = [r for r in range(blocks) if r not in early]
    waves_of = placed_waves(early, early_refs, late, waves_ref, count)
    weights = weights_ref[...]
    weights_high = weights.astype(bf16)
    weights_low = (weights - weights_high.astype(f32)).astype(bf16)
    for m in range(group):
        block = waves_of[m][...]
        field_refs[m][...] = matmul(weights_high, block) + matmul(weights_low, block)


def charge_gradient(errors, field, back, block):
    charge_count = back.shape[0]
    high = back.astype(bf16)
    low = (back - high.astype(f32)).astype(bf16)
    grad = matmul(high, block) + matmul(low, block)
    for a in range(3):
        grad = grad + errors[a] * field[a * charge_count : (a + 1) * charge_count, :]
    return grad


def gradient_kernel(where_ref, *refs, group, blocks, early, charge_count, box_x):
    shared_refs, part_refs = refs[:blocks], refs[blocks : blocks + group]
    refs = refs[blocks + group :]
    early_refs, refs = refs[: len(early)], refs[len(early) :]
    field_refs, refs = refs[: group - 1], refs[group - 1 :]
    wave_ref, waves_ref, forces_ref, errors_ref, back_ref, *grad_refs, total_ref = refs
    late = [r for r in range(blocks) if r not in early]
    count, _, atoms = shared_refs[0].shape
    share = waves_ref.shape[1] // 2
    first = pl.multiple_of(where_ref[1] * share, share)
    _, waves, damping = wave_rows(wave_ref, first, share, box_x, blocks * count * atoms)
    waves_of = placed_waves(early, early_refs, late, waves_ref, count)
    total = part_refs[0][...]
    for m in range(1, group):
        total = total + part_refs[m][...]
    total_ref[...] = total
    for a in range(3):
        forces_ref[a : a + 1, :] = total[a, 0:1, :]

    def errors_of(d):
        j, r = divmod(d, blocks)
        target = shared_refs[r][j, charge_count : charge_count + 16, :].astype(f32)
        target = target[9:12, :] + target[12:15, :]
        return [2.0 * (total_ref[a, d : d + 1, :] - target[a : a + 1, :]) for a in range(3)]

    by_wave = jnp.zeros((3 * charge_count, 2 * share), f32)
    for d in range(blocks * count):
        j, r = divmod(d, blocks)
        charges = shared_refs[r][j, 0:charge_count, :].astype(f32)
        errors = errors_of(d)
        scaled = jnp.concatenate([errors[a] * charges for a in range(3)], axis=0).astype(bf16)
        by_wave = by_wave + matmul_nt(scaled, waves_of[d][...])
        if d == 0:
            errors_ref[...] = jnp.concatenate(errors + [jnp.zeros((5, atoms), f32)], axis=0)

    def along(value):
        return sum(
            waves[a] * value[a * charge_count : (a + 1) * charge_count, :] for a in range(3)
        )

    back_cos = damping * along(by_wave[:, :share])
    back_sin = -damping * along(by_wave[:, share:])
    back = jnp.concatenate([back_sin, back_cos], axis=1)
    back_ref[...] = back
    for m in range(1, group):
        grad_refs[m - 1][...] = charge_gradient(
            errors_of(m), field_refs[m - 1][...], back, waves_of[m][...]
        ).astype(bf16)


def own_gradient_kernel(errors_ref, field_ref, back_ref, waves_ref, grad_ref):
    errors = errors_ref[...]
    grad_ref[...] = charge_gradient(
        [errors[a : a + 1, :] for a in range(3)], field_ref[...], back_ref[...], waves_ref[0]
    )


def summed(values):
    while len(values) > 1:
        values = [values[i] + values[i + 1] for i in range(0, len(values), 2)]
    return values[0]


def split_rows(value, first, count, sums_ref):
    rows = value.shape[0]
    high = value.astype(bf16)
    sums_ref[0:rows, :] = high
    rest = value[first : first + count, :] - high[first : first + count, :].astype(f32)
    sums_ref[rows:, :] = rest.astype(bf16)


def joined_rows(refs, first, count, value_ref):
    total = summed([ref[...].astype(f32) for ref in refs])
    rows = value_ref.shape[0]
    value_ref[...] = total[0:rows, :]
    value_ref[first : first + count, :] += total[rows:, :]


def halves_kernel(*refs, first, count):
    *part_refs, sums_ref, value_ref = refs
    joined_rows(part_refs, first, count, value_ref)
    split_rows(value_ref[...], first, count, sums_ref)


def weights_kernel(*refs, group, kinds):
    part_refs = refs[:group]
    (
        filtered_ref,
        messages_ref,
        before_ref,
        hidden_ref,
        species_ref,
        mix_ref,
        charge_ref,
        sums_ref,
        packed_ref,
    ) = refs[group:]
    charge_count, atoms = part_refs[0].shape
    basis_count, width, _ = filtered_ref.shape
    grad = part_refs[0][...].astype(f32)
    for m in range(1, group):
        grad = grad + part_refs[m][...].astype(f32)
    before = before_ref[...]
    gate = sigmoid(before)
    upstream = exact_matmul(turned(charge_ref[...]), grad)
    before_grad = upstream * (gate * (1.0 + before * (1.0 - gate)))
    message_grad = exact_matmul(mix_ref[...], before_grad)
    columns = [
        jnp.sum(message_grad * filtered_ref[b], axis=1, keepdims=True) for b in range(basis_count)
    ]
    radial = jnp.concatenate(columns, axis=1)
    row = 0
    packed_ref[row : row + basis_count, :] = jnp.transpose(radial)
    row += basis_count
    high, low = terms_of(messages_ref[...])
    packed_ref[row : row + width, :] = exact_matmul(high, before_grad, matmul_nt) + matmul_nt(
        low, before_grad.astype(bf16)
    )
    row += width
    high, low = terms_of(grad)
    packed_ref[row : row + charge_count, :] = matmul_nt(high, hidden_ref[...]) + matmul_nt(
        low, hidden_ref[...]
    )
    row += charge_count
    packed_ref[row:, :] = jnp.zeros((packed_ref.shape[0] - row, width), f32)
    one_hot = (
        lax.broadcasted_iota(jnp.int32, (kinds, atoms), 0) == species_ref[...]
    ).astype(f32)
    packed_ref[row : row + kinds, 0:charge_count] = matmul_nt(one_hot, grad, highest)
    split_rows(packed_ref[...], basis_count, width, sums_ref)


def step_kernel(*refs):
    *total_refs, radial_ref, mix_ref, charge_ref, species_ref, total_ref = refs
    basis_count, width = radial_ref.shape
    charge_count = charge_ref.shape[0]
    kinds = species_ref.shape[0]
    joined_rows(total_refs, basis_count, width, total_ref)

    def normalized(gradient):
        mean = jnp.sum(gradient * gradient, keepdims=True) * (1.0 / gradient.size)
        return gradient * lax.rsqrt(mean + 1e-06)

    row = 0
    radial_ref[...] = normalized(total_ref[row : row + basis_count, :])
    row += basis_count
    mix_ref[...] = normalized(total_ref[row : row + width, :])
    row += width
    charge_ref[...] = normalized(total_ref[row : row + charge_count, :])
    row += charge_count
    species_ref[...] = normalized(total_ref[row : row + kinds, 0:charge_count])


def shaped(*dims, kind=f32):
    return jax.ShapeDtypeStruct(dims, kind)


def kernel(body, name, out_shape, scratch, nanoseconds, *operands, scalars=(), wanted=0):
    outs = out_shape if isinstance(out_shape, tuple) else (out_shape,)
    held = sum(math.prod(x.shape) * x.dtype.itemsize for x in (*outs, *scratch, *operands))
    in_vmem = pl.BlockSpec(memory_space=pltpu.VMEM)
    in_smem = pl.BlockSpec(memory_space=pltpu.SMEM)
    return pl.pallas_call(
        body,
        out_shape=out_shape,
        in_specs=[in_smem] * len(scalars) + [in_vmem] * len(operands),
        out_specs=tuple(in_vmem for _ in outs) if isinstance(out_shape, tuple) else in_vmem,
        scratch_shapes=[pltpu.VMEM(x.shape, x.dtype) for x in scratch],
        compiler_params=pltpu.CompilerParams(vmem_limit_bytes=max(held + spare_vmem, wanted)),
        cost_estimate=pl.CostEstimate(
            flops=nanoseconds * 1_000_000, bytes_accessed=held, transcendentals=0
        ),
        name=name,
    )(*scalars, *operands)


def across(value, bits):
    domains = lax.axis_size("dom")
    return lax.ppermute(value, "dom", [(i, i ^ bits) for i in range(domains)])


def on_device(
    features,
    positions,
    neighbours,
    neighbour_count,
    ghost_sends,
    species,
    wave_index,
    force_ref,
    radial_weight,
    mix_weight,
    charge_weight,
    species_charge,
):
    atoms, width = features.shape
    basis_count = radial_weight.shape[0]
    charge_count = charge_weight.shape[1]
    kinds = species_charge.shape[0]
    wave_count = wave_index.shape[1]
    domains = lax.axis_size("dom")
    box_x = 1.25 * (atoms * domains) / 64
    group = 2 if domains % 2 == 0 else 1
    while (
        group < domains
        and 4 * wave_count // group * atoms * domains > waves_bytes
        and wave_count % (256 * group) == 0
    ):
        group *= 2
    share = wave_count // group
    entries = atoms + 2 * ghost_sends.shape[1]

    me = lax.axis_index("dom")
    blocks = 4 if domains % 4 == 0 else 2
    where = jnp.stack([me % 2, me % group, me % blocks]).astype(jnp.int32)
    packed = kernel(
        pack_kernel,
        "pack",
        shaped(atoms + 16 * (atoms // width), width, kind=bf16),
        (),
        1_000,
        features,
        positions,
        ghost_sends,
        wanted=60 * 1024 * 1024,
    )
    near = across(packed, 1)
    beyond = [(i, (i + 1 if i % 2 else i - 1) % domains) for i in range(domains)]
    far = lax.ppermute(packed, "dom", beyond)
    species_row = species[None, :]
    slots = neighbours.T
    charge_rows = charge_weight.T

    sofar, words, *local, extra = kernel(
        lambda *refs: own_kernel(*refs, box_x=box_x),
        "own",
        (
            shaped(basis_count, width, atoms),
            shaped(entries // 32, atoms, kind=jnp.int32),
            shaped(width, atoms, kind=bf16),
            shaped(charge_count, atoms),
            shaped(2 * width + charge_count, width),
            shaped(24, atoms),
        ),
        (
            shaped(atoms, 8),
            shaped(basis_count, atoms, atoms, kind=bf16),
        ),
        4_000,
        features,
        positions,
        force_ref,
        slots,
        neighbour_count[None, :],
        species_row,
        radial_weight,
        mix_weight,
        charge_rows,
        species_charge,
        wanted=own_vmem,
    )
    ghosts = ghost_sends.shape[1]
    scratch = (
        shaped(ghosts // 32, atoms, kind=jnp.int32),
        shaped(ghosts, 8),
        shaped(basis_count, ghosts, atoms, kind=bf16),
    )
    sofar = kernel(
        lambda *refs: near_kernel(*refs, box_x=box_x),
        "near",
        shaped(basis_count, width, atoms),
        scratch,
        3_000,
        near,
        sofar,
        words,
        extra,
        scalars=(where,),
    )
    filtered, messages, before, hidden, shared = kernel(
        lambda *refs: edge_kernel(*refs, box_x=box_x),
        "edges",
        (
            shaped(basis_count, width, atoms),
            shaped(width, atoms),
            shaped(width, atoms),
            shaped(width, atoms, kind=bf16),
            shaped(1, charge_count + 16, atoms, kind=bf16),
        ),
        scratch,
        4_000,
        far,
        sofar,
        words,
        *local,
        extra,
        scalars=(where,),
    )
    column = jnp.concatenate(
        [shared] + [across(shared, bits) for bits in range(blocks, domains, blocks)], axis=0
    )
    columns = [column] + [across(column, bits) for bits in range(1, blocks)]
    early = (0, blocks - 1) if blocks > 2 else (0,)
    waves_early, parts = zip(
        *[
            kernel(
                lambda *refs: phase_kernel(*refs, charge_count=charge_count),
                "phases",
                (
                    shaped(domains // blocks, 2 * share, atoms, kind=bf16),
                    shaped(charge_count, 2 * share),
                ),
                (),
                3_000,
                columns[r],
                wave_index,
                scalars=(where,),
            )
            for r in early
        ]
    )
    waves, weights, *force_parts = kernel(
        lambda *refs: structure_kernel(
            *refs, group=group, blocks=blocks, early=early, charge_count=charge_count, box_x=box_x
        ),
        "structure",
        (
            shaped(domains - len(early) * (domains // blocks), 2 * share, atoms, kind=bf16),
            shaped(3 * charge_count, 2 * share),
        )
        + (shaped(3, domains, atoms),) * group,
        (),
        8_000,
        *columns,
        *waves_early,
        *parts,
        wave_index,
        scalars=(where,),
    )
    force_parts = force_parts[:1] + [across(force_parts[m], m) for m in range(1, group)]
    fields = kernel(
        lambda *refs: field_kernel(
            *refs, group=group, blocks=blocks, early=early, count=domains // blocks
        ),
        "fields",
        (shaped(3 * charge_count, atoms),) * group,
        (),
        2_000,
        weights,
        *waves_early,
        waves,
    )
    forces, errors, back, *grad_parts = kernel(
        lambda *refs: gradient_kernel(
            *refs, group=group, blocks=blocks, early=early, charge_count=charge_count, box_x=box_x
        ),
        "gradient",
        (
            shaped(3, atoms),
            shaped(8, atoms),
            shaped(charge_count, 2 * share),
        )
        + (shaped(charge_count, atoms, kind=bf16),) * (group - 1),
        (shaped(3, domains, atoms),),
        5_000,
        *columns,
        *force_parts,
        *waves_early,
        *fields[1:],
        wave_index,
        waves,
        scalars=(where,),
    )
    own_part = kernel(
        own_gradient_kernel,
        "own_gradient",
        shaped(charge_count, atoms),
        (),
        1_500,
        errors,
        fields[0],
        back,
        waves_early[0],
    )
    grad_parts = [own_part] + [across(grad_parts[m - 1], m) for m in range(1, group)]

    rows = basis_count + width + charge_count + kinds
    rows = -(-rows // 16) * 16
    packed = kernel(
        lambda *refs: weights_kernel(*refs, group=group, kinds=kinds),
        "weights",
        shaped(rows + width, width, kind=bf16),
        (shaped(rows, width),),
        3_000,
        *grad_parts,
        filtered,
        messages,
        before,
        hidden,
        species_row,
        mix_weight,
        charge_rows,
    )
    packed = kernel(
        lambda *refs: halves_kernel(*refs, first=basis_count, count=width),
        "halves",
        shaped(rows + width, width, kind=bf16),
        (shaped(rows, width),),
        1_000,
        packed,
        *[across(packed, r) for r in range(1, blocks)],
    )
    totals = [packed] + [across(packed, bits) for bits in range(blocks, domains, blocks)]
    radial_step, mix_step, charge_step, species_step = kernel(
        step_kernel,
        "steps",
        (
            shaped(basis_count, width),
            shaped(width, width),
            shaped(charge_count, width),
            shaped(kinds, charge_count),
        ),
        (shaped(rows, width),),
        2_000,
        *totals,
    )
    return forces, radial_step, mix_step, charge_step.T, species_step


def solution(mesh):
    placed = (
        P(("cell", "dom"), None),
        P(None, ("cell", "dom")),
        P(("cell", "dom"), None),
        P(("cell", "dom")),
        P(None, ("cell", "dom")),
        P(("cell", "dom")),
        P(),
        P(None, ("cell", "dom")),
        P(),
        P(),
        P(),
        P(),
    )
    return jax.shard_map(
        on_device,
        mesh=mesh,
        in_specs=placed,
        out_specs=(
            P(None, ("cell", "dom")),
            P("cell", None),
            P("cell", None),
            P("cell", None),
            P("cell", None),
        ),
        check_vma=False,
    )
```

```python
import math

import jax
import jax.numpy as jnp
import numpy as np
from jax import lax
from jax.experimental import pallas as pl
from jax.experimental.pallas import tpu as pltpu
from jax.sharding import PartitionSpec as P

cutoff_radius = 5.0
kernel_width = 1.0
basis_width = 0.5
box_side = 20.0
two_pi = 6.283185307179586
highest = lax.Precision.HIGHEST
f32 = jnp.float32
bf16 = jnp.bfloat16
spare_vmem = 4 * 1024 * 1024
waves_bytes = 8 * 1024 * 1024
own_vmem = 50 * 1024 * 1024


def fitted(function, degrees, reach):
    nodes = reach * np.cos((np.arange(400) + 0.5) * np.pi / 400)
    powers = np.stack([nodes**d for d in degrees], axis=1)
    return [float(c) for c in np.linalg.lstsq(powers, function(nodes), rcond=None)[0]]


sine_terms = fitted(lambda x: np.sin(np.pi * x), (1, 3, 5, 7, 9), 0.5)
short_sine = fitted(lambda x: math.sqrt(2) * np.sin(np.pi * x), (1, 3, 5, 7), 0.5)
short_cosine = fitted(lambda x: math.sqrt(2) * np.cos(np.pi * x), (0, 2, 4, 6), 0.5)


def horner(terms, square):
    value = terms[-1]
    for term in terms[-2::-1]:
        value = value * square + term
    return value


def matmul(left, right, precision=None):
    return lax.dot_general(
        left, right, (((1,), (0,)), ((), ())), precision=precision, preferred_element_type=f32
    )


def matmul_nt(left, right, precision=None):
    return lax.dot_general(
        left, right, (((1,), (1,)), ((), ())), precision=precision, preferred_element_type=f32
    )


def terms_of(value):
    high = value.astype(bf16)
    return high, (value - high.astype(f32)).astype(bf16)


def exact_matmul(left, value, product=matmul):
    high, low = terms_of(value)
    return product(left, high) + product(left, low)


def turned(value):
    return jnp.transpose(value.astype(f32)).astype(value.dtype)


def sigmoid(value):
    return 1.0 / (1.0 + jnp.exp(-value))


def pieces_of(value):
    first = value.astype(bf16).astype(f32)
    rest = value - first
    second = rest.astype(bf16).astype(f32)
    return first, second, rest - second


def pack_kernel(feat_ref, positions_ref, ghost_ref, packed_ref):
    atoms, width = feat_ref.shape
    packed_ref[0:atoms, :] = feat_ref[...]
    extra = jnp.concatenate(
        pieces_of(positions_ref[...])
        + (ghost_ref[...].astype(f32), jnp.zeros((5, atoms), f32)),
        axis=0,
    ).astype(bf16)
    for part in range(atoms // width):
        first = atoms + part * 16
        packed_ref[first : first + 16, :] = extra[:, part * width : (part + 1) * width]


def pair_blocks(count, coords_ref, own_rows, words_ref, pair_ref, box_x, rest_ref=None):
    basis_count, _, atoms = pair_ref.shape
    centers = [
        0.5 + (cutoff_radius - 0.5) * float(b) / (basis_count - 1) for b in range(basis_count)
    ]
    scale = -math.log2(math.e) / (basis_width * basis_width)
    middle = basis_count // 2
    gap = centers[1] - centers[0]
    own_x, own_y, own_z = own_rows[0:1, :], own_rows[1:2, :], own_rows[2:3, :]
    step = 32

    def block(index, carry):
        places = pl.ds(pl.multiple_of(index * step, step), step)
        coords = coords_ref[places, :]
        total = jnp.zeros((step, atoms), f32)
        for axis, (mine, length) in enumerate(
            ((own_x, box_x), (own_y, box_side), (own_z, box_side))
        ):
            away = coords[:, axis : axis + 1] - mine
            away = away - length * jnp.floor(away * (1.0 / length) + 0.5)
            total = total + away * away
        total = jnp.maximum(total, 1e-20)
        distance = total * lax.rsqrt(total)
        word = words_ref[pl.ds(index, 1), :]
        sublane = lax.broadcasted_iota(jnp.int32, (step, atoms), 0)
        is_live = (jnp.right_shift(jnp.broadcast_to(word, (step, atoms)), sublane) & 1) != 0
        half = jnp.minimum(distance, cutoff_radius) * (1.0 / cutoff_radius) - 0.5
        fade = 0.5 - 0.5 * (half * horner(sine_terms, half * half))
        weight = jnp.where(jnp.logical_and(is_live, distance < cutoff_radius), fade, 0.0)
        offset = jnp.minimum(distance, cutoff_radius) - centers[middle]
        value = jnp.exp2(offset * offset * scale)
        for direction in (1, -1):
            ratio = jnp.exp2(offset * (-2.0 * direction * gap * scale))
            running = value
            for b in range(middle, basis_count) if direction == 1 else range(middle - 1, -1, -1):
                if b != middle:
                    running = running * ratio
                basis = running * math.exp(-(((b - middle) * gap / basis_width) ** 2))
                basis = basis.astype(bf16).astype(f32)
                pair = weight * basis
                high = pair.astype(bf16)
                pair_ref[b, places, :] = high
                if rest_ref is not None:
                    rest_ref[b, places, :] = (pair - high.astype(f32)).astype(bf16)
        return carry

    lax.fori_loop(0, count // step, block, 0, unroll=8)


def own_kernel(
    feat_ref,
    positions_ref,
    force_ref,
    slots_ref,
    count_ref,
    species_ref,
    radial_ref,
    mix_ref,
    charge_ref,
    offset_ref,
    filtered_ref,
    words_ref,
    own_ref,
    shift_ref,
    weights_ref,
    extra_ref,
    coords_ref,
    pair_ref,
    rest_ref,
    *,
    box_x,
):
    atoms, width = feat_ref.shape
    slots = slots_ref.shape[0]
    basis_count = radial_ref.shape[0]
    own_rows = positions_ref[...]
    own_feat = turned(feat_ref[...])
    own_ref[...] = own_feat
    coords_ref[...] = jnp.transpose(
        jnp.concatenate([own_rows, jnp.zeros((5, atoms), f32)], axis=0)
    )

    listed = slots_ref[...]
    live = lax.broadcasted_iota(jnp.int32, (slots, atoms), 0) < count_ref[...]
    word_of = jnp.where(live, listed >> 5, -1)
    bit = jnp.left_shift(jnp.ones_like(listed), listed & 31)
    for word in range(words_ref.shape[0]):
        value = jnp.where(word_of == word, bit, 0)
        rows = slots
        while rows > 1:
            rows //= 2
            value = value[:rows] | value[rows:]
        words_ref[word : word + 1, :] = value

    pair_blocks(atoms, coords_ref, own_rows, words_ref, pair_ref, box_x, rest_ref)
    for b in range(basis_count):
        filtered_ref[b] = matmul(own_feat, pair_ref[b]) + matmul(own_feat, rest_ref[b])

    kinds = offset_ref.shape[0]
    one_hot = (
        lax.broadcasted_iota(jnp.int32, (kinds, atoms), 0) == species_ref[...]
    ).astype(f32)
    shift_ref[...] = matmul(jnp.transpose(offset_ref[...]), one_hot, highest)
    charge_count = charge_ref.shape[0]
    weights_ref[0:width, :] = jnp.transpose(mix_ref[...].astype(f32))
    weights_ref[width : width + charge_count, :] = charge_ref[...].astype(f32)
    weights_ref[width + charge_count :, 0:basis_count] = jnp.transpose(
        radial_ref[...].astype(f32)
    )
    lengths = (box_x, box_side, box_side)
    turns = jnp.concatenate([own_rows[a : a + 1, :] * (1.0 / lengths[a]) for a in range(3)], axis=0)
    target = force_ref[...]
    high = target.astype(bf16).astype(f32)
    extra_ref[0:16, :] = jnp.concatenate(
        pieces_of(turns) + (high, target - high, jnp.zeros((1, atoms), f32)), axis=0
    )
    extra_ref[16:24, :] = jnp.concatenate([own_rows, jnp.zeros((5, atoms), f32)], axis=0)


def ghost_pairs(ref, is_low, words_ref, extra_ref, ghost_words_ref, coords_ref, pair_ref, box_x):
    _, ghosts, atoms = pair_ref.shape
    width = ref.shape[1]
    extra = jnp.concatenate(
        [ref[atoms + part * 16 : atoms + part * 16 + 16, :] for part in range(atoms // width)],
        axis=1,
    )
    sends = extra[8:16, :].astype(f32)
    sends = jnp.where(is_low, sends[2:3, :], sends[1:2, :])
    site = lax.broadcasted_iota(jnp.int32, (atoms, ghosts), 0).astype(f32)
    chosen = (site == sends).astype(bf16)
    moved = matmul(extra, chosen)
    moved = moved[0:3, :] + (moved[3:6, :] + moved[6:9, :])
    coords_ref[...] = jnp.transpose(jnp.concatenate([moved, jnp.zeros((5, ghosts), f32)], axis=0))
    count = ghosts // 32
    first = jnp.where(is_low, atoms // 32, atoms // 32 + count)
    ghost_words_ref[...] = words_ref[pl.ds(pl.multiple_of(first, 8), count), :]
    pair_blocks(ghosts, coords_ref, extra_ref[16:24, :], ghost_words_ref, pair_ref, box_x)
    return matmul(turned(ref[0:atoms, :]), chosen).astype(bf16)


def near_kernel(
    where_ref,
    near_ref,
    sofar_ref,
    words_ref,
    extra_ref,
    filtered_ref,
    ghost_words_ref,
    coords_ref,
    pair_ref,
    *,
    box_x,
):
    feat = ghost_pairs(
        near_ref,
        where_ref[0] == 1,
        words_ref,
        extra_ref,
        ghost_words_ref,
        coords_ref,
        pair_ref,
        box_x,
    )
    for b in range(filtered_ref.shape[0]):
        filtered_ref[b] = sofar_ref[b] + matmul(feat, pair_ref[b])


def edge_kernel(
    where_ref,
    far_ref,
    sofar_ref,
    words_ref,
    own_ref,
    shift_ref,
    weights_ref,
    extra_ref,
    filtered_ref,
    messages_ref,
    before_ref,
    hidden_ref,
    shared_ref,
    ghost_words_ref,
    coords_ref,
    pair_ref,
    *,
    box_x,
):
    width, atoms = own_ref.shape
    charge_count = shift_ref.shape[0]
    feat = ghost_pairs(
        far_ref,
        where_ref[0] == 0,
        words_ref,
        extra_ref,
        ghost_words_ref,
        coords_ref,
        pair_ref,
        box_x,
    )
    messages = jnp.zeros((width, atoms), f32)
    for b in range(filtered_ref.shape[0]):
        filtered = sofar_ref[b] + matmul(feat, pair_ref[b])
        filtered_ref[b] = filtered
        messages = messages + weights_ref[width + charge_count :, b : b + 1] * filtered
    messages_ref[...] = messages
    before = exact_matmul(weights_ref[0:width, :].astype(bf16), messages)
    before_ref[...] = before
    hidden = (own_ref[...].astype(f32) + before * sigmoid(before)).astype(bf16)
    hidden_ref[...] = hidden
    charges = matmul(weights_ref[width : width + charge_count, :].astype(bf16), hidden)
    shared_ref[0, 0:charge_count, :] = (charges + shift_ref[...]).astype(bf16)
    shared_ref[0, charge_count : charge_count + 16, :] = extra_ref[0:16, :].astype(bf16)


def wave_rows(wave_ref, first, count, box_x, total_atoms):
    index = wave_ref[:, pl.ds(first, count)].astype(f32)
    scales = (two_pi / box_x, two_pi / box_side, two_pi / box_side)
    waves = [index[a : a + 1, :] * scales[a] for a in range(3)]
    squares = waves[0] * waves[0] + waves[1] * waves[1] + waves[2] * waves[2]
    damping = jnp.exp(-0.5 * kernel_width * kernel_width * squares) * (1.0 / total_atoms)
    return index, waves, damping


def wave_columns(wave_ref, first, share):
    index = wave_ref[:, pl.ds(first, share)].astype(f32)
    return jnp.transpose(
        jnp.concatenate([index] * 3 + [jnp.zeros((7, share), f32)], axis=0)
    ).astype(bf16)


def fill_waves(columns, shared_ref, j, charge_count, waves_ref, place):
    share = columns.shape[0]
    shift = 12582912.0
    turns = matmul(columns, shared_ref[j, charge_count : charge_count + 16, :])
    turns = turns - ((turns + shift) - shift)
    square = turns * turns
    half_sine = turns * horner(short_sine, square)
    half_cosine = horner(short_cosine, square)
    waves_ref[place, 0:share, :] = (half_sine * half_cosine).astype(bf16)
    waves_ref[place, share : 2 * share, :] = (1.0 - half_sine * half_sine).astype(bf16)


def phase_kernel(where_ref, shared_ref, wave_ref, waves_ref, part_ref, *, charge_count):
    count = shared_ref.shape[0]
    share = waves_ref.shape[1] // 2
    columns = wave_columns(wave_ref, pl.multiple_of(where_ref[1] * share, share), share)

    def block(j, carry):
        fill_waves(columns, shared_ref, j, charge_count, waves_ref, j)
        return carry

    lax.fori_loop(0, count, block, 0, unroll=4)
    part = jnp.zeros(part_ref.shape, f32)
    for j in range(count):
        part = part + matmul_nt(shared_ref[j, 0:charge_count, :], waves_ref[j])
    part_ref[...] = part


def placed_waves(early, early_refs, late, waves_ref, count):
    return [
        early_refs[early.index(r)].at[j]
        if r in early
        else waves_ref.at[j * len(late) + late.index(r)]
        for j in range(count)
        for r in range(len(early) + len(late))
    ]


def structure_kernel(where_ref, *refs, group, blocks, early, charge_count, box_x):
    shared_refs, early_refs = refs[:blocks], refs[blocks : blocks + len(early)]
    part_refs, refs = refs[blocks + len(early) : blocks + 2 * len(early)], refs[blocks + 2 * len(early) :]
    wave_ref, waves_ref, weights_ref, *force_refs = refs
    late = [r for r in range(blocks) if r not in early]
    count, _, atoms = shared_refs[0].shape
    share = waves_ref.shape[1] // 2
    first = pl.multiple_of(where_ref[1] * share, share)
    _, waves, damping = wave_rows(wave_ref, first, share, box_x, blocks * count * atoms)
    columns = wave_columns(wave_ref, first, share)

    def block(j, carry):
        for i, r in enumerate(late):
            fill_waves(columns, shared_refs[r], j, charge_count, waves_ref, j * len(late) + i)
        return carry

    lax.fori_loop(0, count, block, 0, unroll=4)
    waves_of = placed_waves(early, early_refs, late, waves_ref, count)
    structure = sum(ref[...] for ref in part_refs)
    for d in range(blocks * count):
        j, r = divmod(d, blocks)
        if r in late:
            structure = structure + matmul_nt(
                shared_refs[r][j, 0:charge_count, :], waves_of[d][...]
            )
    along_sin = structure[:, :share] * damping
    along_cos = structure[:, share:] * damping
    to_sine = jnp.concatenate([along_cos * waves[a] for a in range(3)], axis=0)
    to_cosine = jnp.concatenate([-along_sin * waves[a] for a in range(3)], axis=0)
    weights = jnp.concatenate([to_sine, to_cosine], axis=1)
    weights_ref[...] = weights
    weights = weights.astype(bf16)
    for d in range(blocks * count):
        j, r = divmod(d, blocks)
        field = matmul(weights, waves_of[d][...])
        charges = shared_refs[r][j, 0:charge_count, :].astype(f32)
        for a in range(3):
            row = jnp.sum(
                field[a * charge_count : (a + 1) * charge_count, :] * charges,
                axis=0,
                keepdims=True,
            )
            for m in range(group):
                force_refs[m][a, d ^ m : (d ^ m) + 1, :] = row


def field_kernel(*refs, group, blocks, early, count):
    weights_ref, refs = refs[0], refs[1:]
    early_refs, waves_ref, field_refs = refs[: len(early)], refs[len(early)], refs[len(early) + 1 :]
    late = [r for r in range(blocks) if r not in early]
    waves_of = placed_waves(early, early_refs, late, waves_ref, count)
    weights = weights_ref[...]
    weights_high = weights.astype(bf16)
    weights_low = (weights - weights_high.astype(f32)).astype(bf16)
    for m in range(group):
        block = waves_of[m][...]
        field_refs[m][...] = matmul(weights_high, block) + matmul(weights_low, block)


def charge_gradient(errors, field, back, block):
    charge_count = back.shape[0]
    high = back.astype(bf16)
    low = (back - high.astype(f32)).astype(bf16)
    grad = matmul(high, block) + matmul(low, block)
    for a in range(3):
        grad = grad + errors[a] * field[a * charge_count : (a + 1) * charge_count, :]
    return grad


def gradient_kernel(where_ref, *refs, group, blocks, early, charge_count, box_x):
    shared_refs, part_refs = refs[:blocks], refs[blocks : blocks + group]
    refs = refs[blocks + group :]
    early_refs, refs = refs[: len(early)], refs[len(early) :]
    field_refs, refs = refs[: group - 1], refs[group - 1 :]
    wave_ref, waves_ref, forces_ref, errors_ref, back_ref, *grad_refs, total_ref = refs
    late = [r for r in range(blocks) if r not in early]
    count, _, atoms = shared_refs[0].shape
    share = waves_ref.shape[1] // 2
    first = pl.multiple_of(where_ref[1] * share, share)
    _, waves, damping = wave_rows(wave_ref, first, share, box_x, blocks * count * atoms)
    waves_of = placed_waves(early, early_refs, late, waves_ref, count)
    total = part_refs[0][...]
    for m in range(1, group):
        total = total + part_refs[m][...]
    total_ref[...] = total
    for a in range(3):
        forces_ref[a : a + 1, :] = total[a, 0:1, :]

    def errors_of(d):
        j, r = divmod(d, blocks)
        target = shared_refs[r][j, charge_count : charge_count + 16, :].astype(f32)
        target = target[9:12, :] + target[12:15, :]
        return [2.0 * (total_ref[a, d : d + 1, :] - target[a : a + 1, :]) for a in range(3)]

    by_wave = jnp.zeros((3 * charge_count, 2 * share), f32)
    for d in range(blocks * count):
        j, r = divmod(d, blocks)
        charges = shared_refs[r][j, 0:charge_count, :].astype(f32)
        errors = errors_of(d)
        scaled = jnp.concatenate([errors[a] * charges for a in range(3)], axis=0).astype(bf16)
        by_wave = by_wave + matmul_nt(scaled, waves_of[d][...])
        if d == 0:
            errors_ref[...] = jnp.concatenate(errors + [jnp.zeros((5, atoms), f32)], axis=0)

    def along(value):
        return sum(
            waves[a] * value[a * charge_count : (a + 1) * charge_count, :] for a in range(3)
        )

    back_cos = damping * along(by_wave[:, :share])
    back_sin = -damping * along(by_wave[:, share:])
    back = jnp.concatenate([back_sin, back_cos], axis=1)
    back_ref[...] = back
    for m in range(1, group):
        grad_refs[m - 1][...] = charge_gradient(
            errors_of(m), field_refs[m - 1][...], back, waves_of[m][...]
        ).astype(bf16)


def own_gradient_kernel(errors_ref, field_ref, back_ref, waves_ref, grad_ref):
    errors = errors_ref[...]
    grad_ref[...] = charge_gradient(
        [errors[a : a + 1, :] for a in range(3)], field_ref[...], back_ref[...], waves_ref[0]
    )


def summed(values):
    while len(values) > 1:
        values = [values[i] + values[i + 1] for i in range(0, len(values), 2)]
    return values[0]


def split_rows(value, first, count, sums_ref):
    rows = value.shape[0]
    high = value.astype(bf16)
    sums_ref[0:rows, :] = high
    rest = value[first : first + count, :] - high[first : first + count, :].astype(f32)
    sums_ref[rows:, :] = rest.astype(bf16)


def joined_rows(refs, first, count, value_ref):
    total = summed([ref[...].astype(f32) for ref in refs])
    rows = value_ref.shape[0]
    value_ref[...] = total[0:rows, :]
    value_ref[first : first + count, :] += total[rows:, :]


def rounded_kernel(*refs, first, count):
    *part_refs, sums_ref, value_ref = refs
    joined_rows(part_refs, first, count, value_ref)
    sums_ref[...] = value_ref[...].astype(bf16)


def weights_kernel(*refs, group, kinds):
    part_refs = refs[:group]
    (
        filtered_ref,
        messages_ref,
        before_ref,
        hidden_ref,
        species_ref,
        mix_ref,
        charge_ref,
        sums_ref,
        packed_ref,
    ) = refs[group:]
    charge_count, atoms = part_refs[0].shape
    basis_count, width, _ = filtered_ref.shape
    grad = part_refs[0][...].astype(f32)
    for m in range(1, group):
        grad = grad + part_refs[m][...].astype(f32)
    before = before_ref[...]
    gate = sigmoid(before)
    upstream = exact_matmul(turned(charge_ref[...]), grad)
    before_grad = upstream * (gate * (1.0 + before * (1.0 - gate)))
    message_grad = exact_matmul(mix_ref[...], before_grad)
    columns = [
        jnp.sum(message_grad * filtered_ref[b], axis=1, keepdims=True) for b in range(basis_count)
    ]
    radial = jnp.concatenate(columns, axis=1)
    row = 0
    packed_ref[row : row + basis_count, :] = jnp.transpose(radial)
    row += basis_count
    high, low = terms_of(messages_ref[...])
    packed_ref[row : row + width, :] = exact_matmul(high, before_grad, matmul_nt) + matmul_nt(
        low, before_grad.astype(bf16)
    )
    row += width
    high, low = terms_of(grad)
    packed_ref[row : row + charge_count, :] = matmul_nt(high, hidden_ref[...]) + matmul_nt(
        low, hidden_ref[...]
    )
    row += charge_count
    packed_ref[row:, :] = jnp.zeros((packed_ref.shape[0] - row, width), f32)
    one_hot = (
        lax.broadcasted_iota(jnp.int32, (kinds, atoms), 0) == species_ref[...]
    ).astype(f32)
    packed_ref[row : row + kinds, 0:charge_count] = matmul_nt(one_hot, grad, highest)
    split_rows(packed_ref[...], basis_count, width, sums_ref)


def step_kernel(*refs):
    *total_refs, radial_ref, mix_ref, charge_ref, species_ref, total_ref = refs
    basis_count, width = radial_ref.shape
    charge_count = charge_ref.shape[0]
    kinds = species_ref.shape[0]
    total_ref[...] = summed([ref[...].astype(f32) for ref in total_refs])

    def normalized(gradient):
        mean = jnp.sum(gradient * gradient, keepdims=True) * (1.0 / gradient.size)
        return gradient * lax.rsqrt(mean + 1e-06)

    row = 0
    radial_ref[...] = normalized(total_ref[row : row + basis_count, :])
    row += basis_count
    mix_ref[...] = normalized(total_ref[row : row + width, :])
    row += width
    charge_ref[...] = normalized(total_ref[row : row + charge_count, :])
    row += charge_count
    species_ref[...] = normalized(total_ref[row : row + kinds, 0:charge_count])


def shaped(*dims, kind=f32):
    return jax.ShapeDtypeStruct(dims, kind)


def kernel(body, name, out_shape, scratch, nanoseconds, *operands, scalars=(), wanted=0):
    outs = out_shape if isinstance(out_shape, tuple) else (out_shape,)
    held = sum(math.prod(x.shape) * x.dtype.itemsize for x in (*outs, *scratch, *operands))
    in_vmem = pl.BlockSpec(memory_space=pltpu.VMEM)
    in_smem = pl.BlockSpec(memory_space=pltpu.SMEM)
    return pl.pallas_call(
        body,
        out_shape=out_shape,
        in_specs=[in_smem] * len(scalars) + [in_vmem] * len(operands),
        out_specs=tuple(in_vmem for _ in outs) if isinstance(out_shape, tuple) else in_vmem,
        scratch_shapes=[pltpu.VMEM(x.shape, x.dtype) for x in scratch],
        compiler_params=pltpu.CompilerParams(vmem_limit_bytes=max(held + spare_vmem, wanted)),
        cost_estimate=pl.CostEstimate(
            flops=nanoseconds * 1_000_000, bytes_accessed=held, transcendentals=0
        ),
        name=name,
    )(*scalars, *operands)


def across(value, bits):
    domains = lax.axis_size("dom")
    return lax.ppermute(value, "dom", [(i, i ^ bits) for i in range(domains)])


def on_device(
    features,
    positions,
    neighbours,
    neighbour_count,
    ghost_sends,
    species,
    wave_index,
    force_ref,
    radial_weight,
    mix_weight,
    charge_weight,
    species_charge,
):
    atoms, width = features.shape
    basis_count = radial_weight.shape[0]
    charge_count = charge_weight.shape[1]
    kinds = species_charge.shape[0]
    wave_count = wave_index.shape[1]
    domains = lax.axis_size("dom")
    box_x = 1.25 * (atoms * domains) / 64
    group = 2 if domains % 2 == 0 else 1
    while (
        group < domains
        and 4 * wave_count // group * atoms * domains > waves_bytes
        and wave_count % (256 * group) == 0
    ):
        group *= 2
    share = wave_count // group
    entries = atoms + 2 * ghost_sends.shape[1]

    me = lax.axis_index("dom")
    blocks = 4 if domains % 4 == 0 else 2
    where = jnp.stack([me % 2, me % group, me % blocks]).astype(jnp.int32)
    packed = kernel(
        pack_kernel,
        "pack",
        shaped(atoms + 16 * (atoms // width), width, kind=bf16),
        (),
        1_000,
        features,
        positions,
        ghost_sends,
        wanted=60 * 1024 * 1024,
    )
    near = across(packed, 1)
    beyond = [(i, (i + 1 if i % 2 else i - 1) % domains) for i in range(domains)]
    far = lax.ppermute(packed, "dom", beyond)
    species_row = species[None, :]
    slots = neighbours.T
    charge_rows = charge_weight.T

    sofar, words, *local, extra = kernel(
        lambda *refs: own_kernel(*refs, box_x=box_x),
        "own",
        (
            shaped(basis_count, width, atoms),
            shaped(entries // 32, atoms, kind=jnp.int32),
            shaped(width, atoms, kind=bf16),
            shaped(charge_count, atoms),
            shaped(2 * width + charge_count, width),
            shaped(24, atoms),
        ),
        (
            shaped(atoms, 8),
            shaped(basis_count, atoms, atoms, kind=bf16),
            shaped(basis_count, atoms, atoms, kind=bf16),
        ),
        4_000,
        features,
        positions,
        force_ref,
        slots,
        neighbour_count[None, :],
        species_row,
        radial_weight,
        mix_weight,
        charge_rows,
        species_charge,
        wanted=own_vmem,
    )
    ghosts = ghost_sends.shape[1]
    scratch = (
        shaped(ghosts // 32, atoms, kind=jnp.int32),
        shaped(ghosts, 8),
        shaped(basis_count, ghosts, atoms, kind=bf16),
    )
    sofar = kernel(
        lambda *refs: near_kernel(*refs, box_x=box_x),
        "near",
        shaped(basis_count, width, atoms),
        scratch,
        3_000,
        near,
        sofar,
        words,
        extra,
        scalars=(where,),
    )
    filtered, messages, before, hidden, shared = kernel(
        lambda *refs: edge_kernel(*refs, box_x=box_x),
        "edges",
        (
            shaped(basis_count, width, atoms),
            shaped(width, atoms),
            shaped(width, atoms),
            shaped(width, atoms, kind=bf16),
            shaped(1, charge_count + 16, atoms, kind=bf16),
        ),
        scratch,
        4_000,
        far,
        sofar,
        words,
        *local,
        extra,
        scalars=(where,),
    )
    column = jnp.concatenate(
        [shared] + [across(shared, bits) for bits in range(blocks, domains, blocks)], axis=0
    )
    columns = [column] + [across(column, bits) for bits in range(1, blocks)]
    early = (0, blocks - 1) if blocks > 2 else (0,)
    waves_early, parts = zip(
        *[
            kernel(
                lambda *refs: phase_kernel(*refs, charge_count=charge_count),
                "phases",
                (
                    shaped(domains // blocks, 2 * share, atoms, kind=bf16),
                    shaped(charge_count, 2 * share),
                ),
                (),
                3_000,
                columns[r],
                wave_index,
                scalars=(where,),
            )
            for r in early
        ]
    )
    waves, weights, *force_parts = kernel(
        lambda *refs: structure_kernel(
            *refs, group=group, blocks=blocks, early=early, charge_count=charge_count, box_x=box_x
        ),
        "structure",
        (
            shaped(domains - len(early) * (domains // blocks), 2 * share, atoms, kind=bf16),
            shaped(3 * charge_count, 2 * share),
        )
        + (shaped(3, domains, atoms),) * group,
        (),
        8_000,
        *columns,
        *waves_early,
        *parts,
        wave_index,
        scalars=(where,),
    )
    force_parts = force_parts[:1] + [across(force_parts[m], m) for m in range(1, group)]
    fields = kernel(
        lambda *refs: field_kernel(
            *refs, group=group, blocks=blocks, early=early, count=domains // blocks
        ),
        "fields",
        (shaped(3 * charge_count, atoms),) * group,
        (),
        2_000,
        weights,
        *waves_early,
        waves,
    )
    forces, errors, back, *grad_parts = kernel(
        lambda *refs: gradient_kernel(
            *refs, group=group, blocks=blocks, early=early, charge_count=charge_count, box_x=box_x
        ),
        "gradient",
        (
            shaped(3, atoms),
            shaped(8, atoms),
            shaped(charge_count, 2 * share),
        )
        + (shaped(charge_count, atoms, kind=bf16),) * (group - 1),
        (shaped(3, domains, atoms),),
        5_000,
        *columns,
        *force_parts,
        *waves_early,
        *fields[1:],
        wave_index,
        waves,
        scalars=(where,),
    )
    own_part = kernel(
        own_gradient_kernel,
        "own_gradient",
        shaped(charge_count, atoms),
        (),
        1_500,
        errors,
        fields[0],
        back,
        waves_early[0],
    )
    grad_parts = [own_part] + [across(grad_parts[m - 1], m) for m in range(1, group)]

    rows = basis_count + width + charge_count + kinds
    rows = -(-rows // 16) * 16
    packed = kernel(
        lambda *refs: weights_kernel(*refs, group=group, kinds=kinds),
        "weights",
        shaped(rows + width, width, kind=bf16),
        (shaped(rows, width),),
        3_000,
        *grad_parts,
        filtered,
        messages,
        before,
        hidden,
        species_row,
        mix_weight,
        charge_rows,
    )
    packed = kernel(
        lambda *refs: rounded_kernel(*refs, first=basis_count, count=width),
        "rounded",
        shaped(rows, width, kind=bf16),
        (shaped(rows, width),),
        1_000,
        packed,
        *[across(packed, r) for r in range(1, blocks)],
    )
    totals = [packed] + [across(packed, bits) for bits in range(blocks, domains, blocks)]
    radial_step, mix_step, charge_step, species_step = kernel(
        step_kernel,
        "steps",
        (
            shaped(basis_count, width),
            shaped(width, width),
            shaped(charge_count, width),
            shaped(kinds, charge_count),
        ),
        (shaped(rows, width),),
        2_000,
        *totals,
    )
    return forces, radial_step, mix_step, charge_step.T, species_step


def solution(mesh):
    placed = (
        P(("cell", "dom"), None),
        P(None, ("cell", "dom")),
        P(("cell", "dom"), None),
        P(("cell", "dom")),
        P(None, ("cell", "dom")),
        P(("cell", "dom")),
        P(),
        P(None, ("cell", "dom")),
        P(),
        P(),
        P(),
        P(),
    )
    return jax.shard_map(
        on_device,
        mesh=mesh,
        in_specs=placed,
        out_specs=(
            P(None, ("cell", "dom")),
            P("cell", None),
            P("cell", None),
            P("cell", None),
            P("cell", None),
        ),
        check_vma=False,
    )
```

```python
import math

import jax
import jax.numpy as jnp
import numpy as np
from jax import lax
from jax.experimental import pallas as pl
from jax.experimental.pallas import tpu as pltpu
from jax.sharding import PartitionSpec as P

cutoff_radius = 5.0
kernel_width = 1.0
basis_width = 0.5
box_side = 20.0
two_pi = 6.283185307179586
highest = lax.Precision.HIGHEST
f32 = jnp.float32
bf16 = jnp.bfloat16
spare_vmem = 4 * 1024 * 1024
waves_bytes = 8 * 1024 * 1024
own_vmem = 50 * 1024 * 1024


def fitted(function, degrees, reach):
    nodes = reach * np.cos((np.arange(400) + 0.5) * np.pi / 400)
    powers = np.stack([nodes**d for d in degrees], axis=1)
    return [float(c) for c in np.linalg.lstsq(powers, function(nodes), rcond=None)[0]]


sine_terms = fitted(lambda x: np.sin(np.pi * x), (1, 3, 5, 7, 9), 0.5)
short_sine = fitted(lambda x: math.sqrt(2) * np.sin(np.pi * x), (1, 3, 5, 7), 0.5)
short_cosine = fitted(lambda x: math.sqrt(2) * np.cos(np.pi * x), (0, 2, 4, 6), 0.5)


def horner(terms, square):
    value = terms[-1]
    for term in terms[-2::-1]:
        value = value * square + term
    return value


def matmul(left, right, precision=None):
    return lax.dot_general(
        left, right, (((1,), (0,)), ((), ())), precision=precision, preferred_element_type=f32
    )


def matmul_nt(left, right, precision=None):
    return lax.dot_general(
        left, right, (((1,), (1,)), ((), ())), precision=precision, preferred_element_type=f32
    )


def terms_of(value):
    high = value.astype(bf16)
    return high, (value - high.astype(f32)).astype(bf16)


def exact_matmul(left, value, product=matmul):
    high, low = terms_of(value)
    return product(left, high) + product(left, low)


def turned(value):
    return jnp.transpose(value.astype(f32)).astype(value.dtype)


def sigmoid(value):
    return 1.0 / (1.0 + jnp.exp(-value))


def pieces_of(value):
    first = value.astype(bf16).astype(f32)
    rest = value - first
    second = rest.astype(bf16).astype(f32)
    return first, second, rest - second


def pack_kernel(feat_ref, positions_ref, ghost_ref, packed_ref):
    atoms, width = feat_ref.shape
    packed_ref[0:atoms, :] = feat_ref[...]
    extra = jnp.concatenate(
        pieces_of(positions_ref[...])
        + (ghost_ref[...].astype(f32), jnp.zeros((5, atoms), f32)),
        axis=0,
    ).astype(bf16)
    for part in range(atoms // width):
        first = atoms + part * 16
        packed_ref[first : first + 16, :] = extra[:, part * width : (part + 1) * width]


def pair_blocks(count, coords_ref, own_rows, words_ref, pair_ref, box_x, rest_ref=None):
    basis_count, _, atoms = pair_ref.shape
    centers = [
        0.5 + (cutoff_radius - 0.5) * float(b) / (basis_count - 1) for b in range(basis_count)
    ]
    scale = -math.log2(math.e) / (basis_width * basis_width)
    middle = basis_count // 2
    gap = centers[1] - centers[0]
    own_x, own_y, own_z = own_rows[0:1, :], own_rows[1:2, :], own_rows[2:3, :]
    step = 32

    def block(index, carry):
        places = pl.ds(pl.multiple_of(index * step, step), step)
        coords = coords_ref[places, :]
        total = jnp.zeros((step, atoms), f32)
        for axis, (mine, length) in enumerate(
            ((own_x, box_x), (own_y, box_side), (own_z, box_side))
        ):
            away = coords[:, axis : axis + 1] - mine
            away = away - length * jnp.floor(away * (1.0 / length) + 0.5)
            total = total + away * away
        total = jnp.maximum(total, 1e-20)
        distance = total * lax.rsqrt(total)
        word = words_ref[pl.ds(index, 1), :]
        sublane = lax.broadcasted_iota(jnp.int32, (step, atoms), 0)
        is_live = (jnp.right_shift(jnp.broadcast_to(word, (step, atoms)), sublane) & 1) != 0
        half = jnp.minimum(distance, cutoff_radius) * (1.0 / cutoff_radius) - 0.5
        fade = 0.5 - 0.5 * (half * horner(sine_terms, half * half))
        weight = jnp.where(jnp.logical_and(is_live, distance < cutoff_radius), fade, 0.0)
        offset = jnp.minimum(distance, cutoff_radius) - centers[middle]
        value = jnp.exp2(offset * offset * scale)
        for direction in (1, -1):
            ratio = jnp.exp2(offset * (-2.0 * direction * gap * scale))
            running = value
            for b in range(middle, basis_count) if direction == 1 else range(middle - 1, -1, -1):
                if b != middle:
                    running = running * ratio
                basis = running * math.exp(-(((b - middle) * gap / basis_width) ** 2))
                basis = basis.astype(bf16).astype(f32)
                pair = weight * basis
                high = pair.astype(bf16)
                pair_ref[b, places, :] = high
                if rest_ref is not None:
                    rest_ref[b, places, :] = (pair - high.astype(f32)).astype(bf16)
        return carry

    lax.fori_loop(0, count // step, block, 0, unroll=8)


def own_kernel(
    feat_ref,
    positions_ref,
    force_ref,
    slots_ref,
    count_ref,
    species_ref,
    radial_ref,
    mix_ref,
    charge_ref,
    offset_ref,
    filtered_ref,
    words_ref,
    own_ref,
    shift_ref,
    weights_ref,
    extra_ref,
    coords_ref,
    pair_ref,
    rest_ref,
    *,
    box_x,
):
    atoms, width = feat_ref.shape
    slots = slots_ref.shape[0]
    basis_count = radial_ref.shape[0]
    own_rows = positions_ref[...]
    own_feat = turned(feat_ref[...])
    own_ref[...] = own_feat
    coords_ref[...] = jnp.transpose(
        jnp.concatenate([own_rows, jnp.zeros((5, atoms), f32)], axis=0)
    )

    listed = slots_ref[...]
    live = lax.broadcasted_iota(jnp.int32, (slots, atoms), 0) < count_ref[...]
    word_of = jnp.where(live, listed >> 5, -1)
    bit = jnp.left_shift(jnp.ones_like(listed), listed & 31)
    for word in range(words_ref.shape[0]):
        value = jnp.where(word_of == word, bit, 0)
        rows = slots
        while rows > 1:
            rows //= 2
            value = value[:rows] | value[rows:]
        words_ref[word : word + 1, :] = value

    pair_blocks(atoms, coords_ref, own_rows, words_ref, pair_ref, box_x, rest_ref)
    for b in range(basis_count):
        filtered_ref[b] = matmul(own_feat, pair_ref[b]) + matmul(own_feat, rest_ref[b])

    kinds = offset_ref.shape[0]
    one_hot = (
        lax.broadcasted_iota(jnp.int32, (kinds, atoms), 0) == species_ref[...]
    ).astype(f32)
    shift_ref[...] = matmul(jnp.transpose(offset_ref[...]), one_hot, highest)
    charge_count = charge_ref.shape[0]
    weights_ref[0:width, :] = jnp.transpose(mix_ref[...].astype(f32))
    weights_ref[width : width + charge_count, :] = charge_ref[...].astype(f32)
    weights_ref[width + charge_count :, 0:basis_count] = jnp.transpose(
        radial_ref[...].astype(f32)
    )
    lengths = (box_x, box_side, box_side)
    turns = jnp.concatenate([own_rows[a : a + 1, :] * (1.0 / lengths[a]) for a in range(3)], axis=0)
    target = force_ref[...]
    high = target.astype(bf16).astype(f32)
    extra_ref[0:16, :] = jnp.concatenate(
        pieces_of(turns) + (high, target - high, jnp.zeros((1, atoms), f32)), axis=0
    )
    extra_ref[16:24, :] = jnp.concatenate([own_rows, jnp.zeros((5, atoms), f32)], axis=0)


def ghost_pairs(ref, is_low, words_ref, extra_ref, ghost_words_ref, coords_ref, pair_ref, box_x):
    _, ghosts, atoms = pair_ref.shape
    width = ref.shape[1]
    extra = jnp.concatenate(
        [ref[atoms + part * 16 : atoms + part * 16 + 16, :] for part in range(atoms // width)],
        axis=1,
    )
    sends = extra[8:16, :].astype(f32)
    sends = jnp.where(is_low, sends[2:3, :], sends[1:2, :])
    site = lax.broadcasted_iota(jnp.int32, (atoms, ghosts), 0).astype(f32)
    chosen = (site == sends).astype(bf16)
    moved = matmul(extra, chosen)
    moved = moved[0:3, :] + (moved[3:6, :] + moved[6:9, :])
    coords_ref[...] = jnp.transpose(jnp.concatenate([moved, jnp.zeros((5, ghosts), f32)], axis=0))
    count = ghosts // 32
    first = jnp.where(is_low, atoms // 32, atoms // 32 + count)
    ghost_words_ref[...] = words_ref[pl.ds(pl.multiple_of(first, 8), count), :]
    pair_blocks(ghosts, coords_ref, extra_ref[16:24, :], ghost_words_ref, pair_ref, box_x)
    return matmul(turned(ref[0:atoms, :]), chosen).astype(bf16)


def near_kernel(
    where_ref,
    near_ref,
    sofar_ref,
    words_ref,
    extra_ref,
    filtered_ref,
    ghost_words_ref,
    coords_ref,
    pair_ref,
    *,
    box_x,
):
    feat = ghost_pairs(
        near_ref,
        where_ref[0] == 1,
        words_ref,
        extra_ref,
        ghost_words_ref,
        coords_ref,
        pair_ref,
        box_x,
    )
    for b in range(filtered_ref.shape[0]):
        filtered_ref[b] = sofar_ref[b] + matmul(feat, pair_ref[b])


def edge_kernel(
    where_ref,
    far_ref,
    sofar_ref,
    words_ref,
    own_ref,
    shift_ref,
    weights_ref,
    extra_ref,
    filtered_ref,
    messages_ref,
    before_ref,
    hidden_ref,
    shared_ref,
    ghost_words_ref,
    coords_ref,
    pair_ref,
    *,
    box_x,
):
    width, atoms = own_ref.shape
    charge_count = shift_ref.shape[0]
    feat = ghost_pairs(
        far_ref,
        where_ref[0] == 0,
        words_ref,
        extra_ref,
        ghost_words_ref,
        coords_ref,
        pair_ref,
        box_x,
    )
    messages = jnp.zeros((width, atoms), f32)
    for b in range(filtered_ref.shape[0]):
        filtered = sofar_ref[b] + matmul(feat, pair_ref[b])
        filtered_ref[b] = filtered
        messages = messages + weights_ref[width + charge_count :, b : b + 1] * filtered
    messages_ref[...] = messages
    before = exact_matmul(weights_ref[0:width, :].astype(bf16), messages)
    before_ref[...] = before
    hidden = (own_ref[...].astype(f32) + before * sigmoid(before)).astype(bf16)
    hidden_ref[...] = hidden
    charges = matmul(weights_ref[width : width + charge_count, :].astype(bf16), hidden)
    shared_ref[0, 0:charge_count, :] = (charges + shift_ref[...]).astype(bf16)
    shared_ref[0, charge_count : charge_count + 16, :] = extra_ref[0:16, :].astype(bf16)


def wave_rows(wave_ref, first, count, box_x, total_atoms):
    index = wave_ref[:, pl.ds(first, count)].astype(f32)
    scales = (two_pi / box_x, two_pi / box_side, two_pi / box_side)
    waves = [index[a : a + 1, :] * scales[a] for a in range(3)]
    squares = waves[0] * waves[0] + waves[1] * waves[1] + waves[2] * waves[2]
    damping = jnp.exp(-0.5 * kernel_width * kernel_width * squares) * (1.0 / total_atoms)
    return index, waves, damping


def wave_columns(wave_ref, first, share):
    index = wave_ref[:, pl.ds(first, share)].astype(f32)
    return jnp.transpose(
        jnp.concatenate([index] * 3 + [jnp.zeros((7, share), f32)], axis=0)
    ).astype(bf16)


def fill_waves(columns, shared_ref, j, charge_count, waves_ref, place):
    share = columns.shape[0]
    shift = 12582912.0
    turns = matmul(columns, shared_ref[j, charge_count : charge_count + 16, :])
    turns = turns - ((turns + shift) - shift)
    square = turns * turns
    half_sine = turns * horner(short_sine, square)
    half_cosine = horner(short_cosine, square)
    waves_ref[place, 0:share, :] = (half_sine * half_cosine).astype(bf16)
    waves_ref[place, share : 2 * share, :] = (1.0 - half_sine * half_sine).astype(bf16)


def phase_kernel(where_ref, shared_ref, wave_ref, waves_ref, part_ref, *, charge_count):
    count = shared_ref.shape[0]
    share = waves_ref.shape[1] // 2
    columns = wave_columns(wave_ref, pl.multiple_of(where_ref[1] * share, share), share)

    def block(j, carry):
        fill_waves(columns, shared_ref, j, charge_count, waves_ref, j)
        return carry

    lax.fori_loop(0, count, block, 0, unroll=4)
    part = jnp.zeros(part_ref.shape, f32)
    for j in range(count):
        part = part + matmul_nt(shared_ref[j, 0:charge_count, :], waves_ref[j])
    part_ref[...] = part


def placed_waves(early, early_refs, late, waves_ref, count):
    return [
        early_refs[early.index(r)].at[j]
        if r in early
        else waves_ref.at[j * len(late) + late.index(r)]
        for j in range(count)
        for r in range(len(early) + len(late))
    ]


def structure_kernel(where_ref, *refs, group, blocks, early, charge_count, box_x):
    shared_refs, early_refs = refs[:blocks], refs[blocks : blocks + len(early)]
    part_refs, refs = refs[blocks + len(early) : blocks + 2 * len(early)], refs[blocks + 2 * len(early) :]
    wave_ref, waves_ref, weights_ref, *force_refs = refs
    late = [r for r in range(blocks) if r not in early]
    count, _, atoms = shared_refs[0].shape
    share = waves_ref.shape[1] // 2
    first = pl.multiple_of(where_ref[1] * share, share)
    _, waves, damping = wave_rows(wave_ref, first, share, box_x, blocks * count * atoms)
    columns = wave_columns(wave_ref, first, share)

    def block(j, carry):
        for i, r in enumerate(late):
            fill_waves(columns, shared_refs[r], j, charge_count, waves_ref, j * len(late) + i)
        return carry

    lax.fori_loop(0, count, block, 0, unroll=4)
    waves_of = placed_waves(early, early_refs, late, waves_ref, count)
    structure = sum(ref[...] for ref in part_refs)
    for d in range(blocks * count):
        j, r = divmod(d, blocks)
        if r in late:
            structure = structure + matmul_nt(
                shared_refs[r][j, 0:charge_count, :], waves_of[d][...]
            )
    along_sin = structure[:, :share] * damping
    along_cos = structure[:, share:] * damping
    to_sine = jnp.concatenate([along_cos * waves[a] for a in range(3)], axis=0)
    to_cosine = jnp.concatenate([-along_sin * waves[a] for a in range(3)], axis=0)
    weights = jnp.concatenate([to_sine, to_cosine], axis=1)
    weights_ref[...] = weights
    weights = weights.astype(bf16)
    for d in range(blocks * count):
        j, r = divmod(d, blocks)
        field = matmul(weights, waves_of[d][...])
        charges = shared_refs[r][j, 0:charge_count, :].astype(f32)
        for a in range(3):
            row = jnp.sum(
                field[a * charge_count : (a + 1) * charge_count, :] * charges,
                axis=0,
                keepdims=True,
            )
            for m in range(group):
                force_refs[m][a, d ^ m : (d ^ m) + 1, :] = row


def field_kernel(*refs, group, blocks, early, count):
    weights_ref, refs = refs[0], refs[1:]
    early_refs, waves_ref, field_refs = refs[: len(early)], refs[len(early)], refs[len(early) + 1 :]
    late = [r for r in range(blocks) if r not in early]
    waves_of = placed_waves(early, early_refs, late, waves_ref, count)
    weights = weights_ref[...]
    weights_high = weights.astype(bf16)
    weights_low = (weights - weights_high.astype(f32)).astype(bf16)
    for m in range(group):
        block = waves_of[m][...]
        field_refs[m][...] = matmul(weights_high, block) + matmul(weights_low, block)


def charge_gradient(errors, field, back, block):
    charge_count = back.shape[0]
    high = back.astype(bf16)
    low = (back - high.astype(f32)).astype(bf16)
    grad = matmul(high, block) + matmul(low, block)
    for a in range(3):
        grad = grad + errors[a] * field[a * charge_count : (a + 1) * charge_count, :]
    return grad


def gradient_kernel(where_ref, *refs, group, blocks, early, charge_count, box_x):
    shared_refs, part_refs = refs[:blocks], refs[blocks : blocks + group]
    refs = refs[blocks + group :]
    early_refs, refs = refs[: len(early)], refs[len(early) :]
    field_refs, refs = refs[: group - 1], refs[group - 1 :]
    wave_ref, waves_ref, forces_ref, errors_ref, back_ref, *grad_refs, total_ref = refs
    late = [r for r in range(blocks) if r not in early]
    count, _, atoms = shared_refs[0].shape
    share = waves_ref.shape[1] // 2
    first = pl.multiple_of(where_ref[1] * share, share)
    _, waves, damping = wave_rows(wave_ref, first, share, box_x, blocks * count * atoms)
    waves_of = placed_waves(early, early_refs, late, waves_ref, count)
    total = part_refs[0][...]
    for m in range(1, group):
        total = total + part_refs[m][...]
    total_ref[...] = total
    for a in range(3):
        forces_ref[a : a + 1, :] = total[a, 0:1, :]

    def errors_of(d):
        j, r = divmod(d, blocks)
        target = shared_refs[r][j, charge_count : charge_count + 16, :].astype(f32)
        target = target[9:12, :] + target[12:15, :]
        return [2.0 * (total_ref[a, d : d + 1, :] - target[a : a + 1, :]) for a in range(3)]

    by_wave = jnp.zeros((3 * charge_count, 2 * share), f32)
    for d in range(blocks * count):
        j, r = divmod(d, blocks)
        charges = shared_refs[r][j, 0:charge_count, :].astype(f32)
        errors = errors_of(d)
        scaled = jnp.concatenate([errors[a] * charges for a in range(3)], axis=0).astype(bf16)
        by_wave = by_wave + matmul_nt(scaled, waves_of[d][...])
        if d == 0:
            errors_ref[...] = jnp.concatenate(errors + [jnp.zeros((5, atoms), f32)], axis=0)

    def along(value):
        return sum(
            waves[a] * value[a * charge_count : (a + 1) * charge_count, :] for a in range(3)
        )

    back_cos = damping * along(by_wave[:, :share])
    back_sin = -damping * along(by_wave[:, share:])
    back = jnp.concatenate([back_sin, back_cos], axis=1)
    back_ref[...] = back
    for m in range(1, group):
        grad_refs[m - 1][...] = charge_gradient(
            errors_of(m), field_refs[m - 1][...], back, waves_of[m][...]
        ).astype(bf16)


def own_gradient_kernel(errors_ref, field_ref, back_ref, waves_ref, grad_ref):
    errors = errors_ref[...]
    grad_ref[...] = charge_gradient(
        [errors[a : a + 1, :] for a in range(3)], field_ref[...], back_ref[...], waves_ref[0]
    )


def summed(values):
    while len(values) > 1:
        values = [values[i] + values[i + 1] for i in range(0, len(values), 2)]
    return values[0]


def split_rows(value, first, count, sums_ref):
    rows = value.shape[0]
    high = value.astype(bf16)
    sums_ref[0:rows, :] = high
    rest = value[first : first + count, :] - high[first : first + count, :].astype(f32)
    sums_ref[rows:, :] = rest.astype(bf16)


def joined_rows(refs, first, count, value_ref):
    total = summed([ref[...].astype(f32) for ref in refs])
    rows = value_ref.shape[0]
    value_ref[...] = total[0:rows, :]
    value_ref[first : first + count, :] += total[rows:, :]


def column_kernel(*refs, first, count):
    *part_refs, sums_ref = refs
    split_rows(summed([ref[...].astype(f32) for ref in part_refs]), first, count, sums_ref)


def weights_kernel(*refs, group, kinds):
    part_refs = refs[:group]
    (
        filtered_ref,
        messages_ref,
        before_ref,
        hidden_ref,
        species_ref,
        mix_ref,
        charge_ref,
        sums_ref,
        packed_ref,
    ) = refs[group:]
    charge_count, atoms = part_refs[0].shape
    basis_count, width, _ = filtered_ref.shape
    grad = part_refs[0][...].astype(f32)
    for m in range(1, group):
        grad = grad + part_refs[m][...].astype(f32)
    before = before_ref[...]
    gate = sigmoid(before)
    upstream = exact_matmul(turned(charge_ref[...]), grad)
    before_grad = upstream * (gate * (1.0 + before * (1.0 - gate)))
    message_grad = exact_matmul(mix_ref[...], before_grad)
    columns = [
        jnp.sum(message_grad * filtered_ref[b], axis=1, keepdims=True) for b in range(basis_count)
    ]
    radial = jnp.concatenate(columns, axis=1)
    row = 0
    packed_ref[row : row + basis_count, :] = jnp.transpose(radial)
    row += basis_count
    high, low = terms_of(messages_ref[...])
    packed_ref[row : row + width, :] = exact_matmul(high, before_grad, matmul_nt) + matmul_nt(
        low, before_grad.astype(bf16)
    )
    row += width
    high, low = terms_of(grad)
    packed_ref[row : row + charge_count, :] = matmul_nt(high, hidden_ref[...]) + matmul_nt(
        low, hidden_ref[...]
    )
    row += charge_count
    packed_ref[row:, :] = jnp.zeros((packed_ref.shape[0] - row, width), f32)
    one_hot = (
        lax.broadcasted_iota(jnp.int32, (kinds, atoms), 0) == species_ref[...]
    ).astype(f32)
    packed_ref[row : row + kinds, 0:charge_count] = matmul_nt(one_hot, grad, highest)
    sums_ref[...] = packed_ref[...].astype(bf16)


def step_kernel(*refs):
    *total_refs, radial_ref, mix_ref, charge_ref, species_ref, total_ref = refs
    basis_count, width = radial_ref.shape
    charge_count = charge_ref.shape[0]
    kinds = species_ref.shape[0]
    joined_rows(total_refs, basis_count, width, total_ref)

    def normalized(gradient):
        mean = jnp.sum(gradient * gradient, keepdims=True) * (1.0 / gradient.size)
        return gradient * lax.rsqrt(mean + 1e-06)

    row = 0
    radial_ref[...] = normalized(total_ref[row : row + basis_count, :])
    row += basis_count
    mix_ref[...] = normalized(total_ref[row : row + width, :])
    row += width
    charge_ref[...] = normalized(total_ref[row : row + charge_count, :])
    row += charge_count
    species_ref[...] = normalized(total_ref[row : row + kinds, 0:charge_count])


def shaped(*dims, kind=f32):
    return jax.ShapeDtypeStruct(dims, kind)


def kernel(body, name, out_shape, scratch, nanoseconds, *operands, scalars=(), wanted=0):
    outs = out_shape if isinstance(out_shape, tuple) else (out_shape,)
    held = sum(math.prod(x.shape) * x.dtype.itemsize for x in (*outs, *scratch, *operands))
    in_vmem = pl.BlockSpec(memory_space=pltpu.VMEM)
    in_smem = pl.BlockSpec(memory_space=pltpu.SMEM)
    return pl.pallas_call(
        body,
        out_shape=out_shape,
        in_specs=[in_smem] * len(scalars) + [in_vmem] * len(operands),
        out_specs=tuple(in_vmem for _ in outs) if isinstance(out_shape, tuple) else in_vmem,
        scratch_shapes=[pltpu.VMEM(x.shape, x.dtype) for x in scratch],
        compiler_params=pltpu.CompilerParams(vmem_limit_bytes=max(held + spare_vmem, wanted)),
        cost_estimate=pl.CostEstimate(
            flops=nanoseconds * 1_000_000, bytes_accessed=held, transcendentals=0
        ),
        name=name,
    )(*scalars, *operands)


def across(value, bits):
    domains = lax.axis_size("dom")
    return lax.ppermute(value, "dom", [(i, i ^ bits) for i in range(domains)])


def on_device(
    features,
    positions,
    neighbours,
    neighbour_count,
    ghost_sends,
    species,
    wave_index,
    force_ref,
    radial_weight,
    mix_weight,
    charge_weight,
    species_charge,
):
    atoms, width = features.shape
    basis_count = radial_weight.shape[0]
    charge_count = charge_weight.shape[1]
    kinds = species_charge.shape[0]
    wave_count = wave_index.shape[1]
    domains = lax.axis_size("dom")
    box_x = 1.25 * (atoms * domains) / 64
    group = 2 if domains % 2 == 0 else 1
    while (
        group < domains
        and 4 * wave_count // group * atoms * domains > waves_bytes
        and wave_count % (256 * group) == 0
    ):
        group *= 2
    share = wave_count // group
    entries = atoms + 2 * ghost_sends.shape[1]

    me = lax.axis_index("dom")
    blocks = 4 if domains % 4 == 0 else 2
    where = jnp.stack([me % 2, me % group, me % blocks]).astype(jnp.int32)
    packed = kernel(
        pack_kernel,
        "pack",
        shaped(atoms + 16 * (atoms // width), width, kind=bf16),
        (),
        1_000,
        features,
        positions,
        ghost_sends,
        wanted=60 * 1024 * 1024,
    )
    near = across(packed, 1)
    beyond = [(i, (i + 1 if i % 2 else i - 1) % domains) for i in range(domains)]
    far = lax.ppermute(packed, "dom", beyond)
    species_row = species[None, :]
    slots = neighbours.T
    charge_rows = charge_weight.T

    sofar, words, *local, extra = kernel(
        lambda *refs: own_kernel(*refs, box_x=box_x),
        "own",
        (
            shaped(basis_count, width, atoms),
            shaped(entries // 32, atoms, kind=jnp.int32),
            shaped(width, atoms, kind=bf16),
            shaped(charge_count, atoms),
            shaped(2 * width + charge_count, width),
            shaped(24, atoms),
        ),
        (
            shaped(atoms, 8),
            shaped(basis_count, atoms, atoms, kind=bf16),
            shaped(basis_count, atoms, atoms, kind=bf16),
        ),
        4_000,
        features,
        positions,
        force_ref,
        slots,
        neighbour_count[None, :],
        species_row,
        radial_weight,
        mix_weight,
        charge_rows,
        species_charge,
        wanted=own_vmem,
    )
    ghosts = ghost_sends.shape[1]
    scratch = (
        shaped(ghosts // 32, atoms, kind=jnp.int32),
        shaped(ghosts, 8),
        shaped(basis_count, ghosts, atoms, kind=bf16),
    )
    sofar = kernel(
        lambda *refs: near_kernel(*refs, box_x=box_x),
        "near",
        shaped(basis_count, width, atoms),
        scratch,
        3_000,
        near,
        sofar,
        words,
        extra,
        scalars=(where,),
    )
    filtered, messages, before, hidden, shared = kernel(
        lambda *refs: edge_kernel(*refs, box_x=box_x),
        "edges",
        (
            shaped(basis_count, width, atoms),
            shaped(width, atoms),
            shaped(width, atoms),
            shaped(width, atoms, kind=bf16),
            shaped(1, charge_count + 16, atoms, kind=bf16),
        ),
        scratch,
        4_000,
        far,
        sofar,
        words,
        *local,
        extra,
        scalars=(where,),
    )
    column = jnp.concatenate(
        [shared] + [across(shared, bits) for bits in range(blocks, domains, blocks)], axis=0
    )
    columns = [column] + [across(column, bits) for bits in range(1, blocks)]
    early = (0, blocks - 1) if blocks > 2 else (0,)
    waves_early, parts = zip(
        *[
            kernel(
                lambda *refs: phase_kernel(*refs, charge_count=charge_count),
                "phases",
                (
                    shaped(domains // blocks, 2 * share, atoms, kind=bf16),
                    shaped(charge_count, 2 * share),
                ),
                (),
                3_000,
                columns[r],
                wave_index,
                scalars=(where,),
            )
            for r in early
        ]
    )
    waves, weights, *force_parts = kernel(
        lambda *refs: structure_kernel(
            *refs, group=group, blocks=blocks, early=early, charge_count=charge_count, box_x=box_x
        ),
        "structure",
        (
            shaped(domains - len(early) * (domains // blocks), 2 * share, atoms, kind=bf16),
            shaped(3 * charge_count, 2 * share),
        )
        + (shaped(3, domains, atoms),) * group,
        (),
        8_000,
        *columns,
        *waves_early,
        *parts,
        wave_index,
        scalars=(where,),
    )
    force_parts = force_parts[:1] + [across(force_parts[m], m) for m in range(1, group)]
    fields = kernel(
        lambda *refs: field_kernel(
            *refs, group=group, blocks=blocks, early=early, count=domains // blocks
        ),
        "fields",
        (shaped(3 * charge_count, atoms),) * group,
        (),
        2_000,
        weights,
        *waves_early,
        waves,
    )
    forces, errors, back, *grad_parts = kernel(
        lambda *refs: gradient_kernel(
            *refs, group=group, blocks=blocks, early=early, charge_count=charge_count, box_x=box_x
        ),
        "gradient",
        (
            shaped(3, atoms),
            shaped(8, atoms),
            shaped(charge_count, 2 * share),
        )
        + (shaped(charge_count, atoms, kind=bf16),) * (group - 1),
        (shaped(3, domains, atoms),),
        5_000,
        *columns,
        *force_parts,
        *waves_early,
        *fields[1:],
        wave_index,
        waves,
        scalars=(where,),
    )
    own_part = kernel(
        own_gradient_kernel,
        "own_gradient",
        shaped(charge_count, atoms),
        (),
        1_500,
        errors,
        fields[0],
        back,
        waves_early[0],
    )
    grad_parts = [own_part] + [across(grad_parts[m - 1], m) for m in range(1, group)]

    rows = basis_count + width + charge_count + kinds
    rows = -(-rows // 16) * 16
    packed = kernel(
        lambda *refs: weights_kernel(*refs, group=group, kinds=kinds),
        "weights",
        shaped(rows, width, kind=bf16),
        (shaped(rows, width),),
        3_000,
        *grad_parts,
        filtered,
        messages,
        before,
        hidden,
        species_row,
        mix_weight,
        charge_rows,
    )
    packed = kernel(
        lambda *refs: column_kernel(*refs, first=basis_count, count=width),
        "column",
        shaped(rows + width, width, kind=bf16),
        (),
        1_000,
        packed,
        *[across(packed, bits) for bits in range(blocks, domains, blocks)],
    )
    totals = [packed] + [across(packed, r) for r in range(1, blocks)]
    radial_step, mix_step, charge_step, species_step = kernel(
        step_kernel,
        "steps",
        (
            shaped(basis_count, width),
            shaped(width, width),
            shaped(charge_count, width),
            shaped(kinds, charge_count),
        ),
        (shaped(rows, width),),
        2_000,
        *totals,
    )
    return forces, radial_step, mix_step, charge_step.T, species_step


def solution(mesh):
    placed = (
        P(("cell", "dom"), None),
        P(None, ("cell", "dom")),
        P(("cell", "dom"), None),
        P(("cell", "dom")),
        P(None, ("cell", "dom")),
        P(("cell", "dom")),
        P(),
        P(None, ("cell", "dom")),
        P(),
        P(),
        P(),
        P(),
    )
    return jax.shard_map(
        on_device,
        mesh=mesh,
        in_specs=placed,
        out_specs=(
            P(None, ("cell", "dom")),
            P("cell", None),
            P("cell", None),
            P("cell", None),
            P("cell", None),
        ),
        check_vma=False,
    )
```

```python
import math

import jax
import jax.numpy as jnp
import numpy as np
from jax import lax
from jax.experimental import pallas as pl
from jax.experimental.pallas import tpu as pltpu
from jax.sharding import PartitionSpec as P

cutoff_radius = 5.0
kernel_width = 1.0
basis_width = 0.5
box_side = 20.0
two_pi = 6.283185307179586
highest = lax.Precision.HIGHEST
f32 = jnp.float32
bf16 = jnp.bfloat16
spare_vmem = 4 * 1024 * 1024
waves_bytes = 8 * 1024 * 1024
own_vmem = 50 * 1024 * 1024


def fitted(function, degrees, reach):
    nodes = reach * np.cos((np.arange(400) + 0.5) * np.pi / 400)
    powers = np.stack([nodes**d for d in degrees], axis=1)
    return [float(c) for c in np.linalg.lstsq(powers, function(nodes), rcond=None)[0]]


sine_terms = fitted(lambda x: np.sin(np.pi * x), (1, 3, 5, 7, 9), 0.5)
short_sine = fitted(lambda x: math.sqrt(2) * np.sin(np.pi * x), (1, 3, 5, 7), 0.5)
short_cosine = fitted(lambda x: math.sqrt(2) * np.cos(np.pi * x), (0, 2, 4, 6), 0.5)


def horner(terms, square):
    value = terms[-1]
    for term in terms[-2::-1]:
        value = value * square + term
    return value


def matmul(left, right, precision=None):
    return lax.dot_general(
        left, right, (((1,), (0,)), ((), ())), precision=precision, preferred_element_type=f32
    )


def matmul_nt(left, right, precision=None):
    return lax.dot_general(
        left, right, (((1,), (1,)), ((), ())), precision=precision, preferred_element_type=f32
    )


def terms_of(value):
    high = value.astype(bf16)
    return high, (value - high.astype(f32)).astype(bf16)


def exact_matmul(left, value, product=matmul):
    high, low = terms_of(value)
    return product(left, high) + product(left, low)


def turned(value):
    return jnp.transpose(value.astype(f32)).astype(value.dtype)


def sigmoid(value):
    return 1.0 / (1.0 + jnp.exp(-value))


def pieces_of(value):
    first = value.astype(bf16).astype(f32)
    rest = value - first
    second = rest.astype(bf16).astype(f32)
    return first, second, rest - second


def pack_kernel(feat_ref, positions_ref, ghost_ref, packed_ref):
    atoms, width = feat_ref.shape
    packed_ref[0:atoms, :] = feat_ref[...]
    extra = jnp.concatenate(
        pieces_of(positions_ref[...])
        + (ghost_ref[...].astype(f32), jnp.zeros((5, atoms), f32)),
        axis=0,
    ).astype(bf16)
    for part in range(atoms // width):
        first = atoms + part * 16
        packed_ref[first : first + 16, :] = extra[:, part * width : (part + 1) * width]


def pair_blocks(count, coords_ref, own_rows, words_ref, pair_ref, box_x, rest_ref=None):
    basis_count, _, atoms = pair_ref.shape
    centers = [
        0.5 + (cutoff_radius - 0.5) * float(b) / (basis_count - 1) for b in range(basis_count)
    ]
    scale = -math.log2(math.e) / (basis_width * basis_width)
    middle = basis_count // 2
    gap = centers[1] - centers[0]
    own_x, own_y, own_z = own_rows[0:1, :], own_rows[1:2, :], own_rows[2:3, :]
    step = 32

    def block(index, carry):
        places = pl.ds(pl.multiple_of(index * step, step), step)
        coords = coords_ref[places, :]
        total = jnp.zeros((step, atoms), f32)
        for axis, (mine, length) in enumerate(
            ((own_x, box_x), (own_y, box_side), (own_z, box_side))
        ):
            away = coords[:, axis : axis + 1] - mine
            away = away - length * jnp.floor(away * (1.0 / length) + 0.5)
            total = total + away * away
        total = jnp.maximum(total, 1e-20)
        distance = total * lax.rsqrt(total)
        word = words_ref[pl.ds(index, 1), :]
        sublane = lax.broadcasted_iota(jnp.int32, (step, atoms), 0)
        is_live = (jnp.right_shift(jnp.broadcast_to(word, (step, atoms)), sublane) & 1) != 0
        half = jnp.minimum(distance, cutoff_radius) * (1.0 / cutoff_radius) - 0.5
        fade = 0.5 - 0.5 * (half * horner(sine_terms, half * half))
        weight = jnp.where(jnp.logical_and(is_live, distance < cutoff_radius), fade, 0.0)
        offset = jnp.minimum(distance, cutoff_radius) - centers[middle]
        value = jnp.exp2(offset * offset * scale)
        for direction in (1, -1):
            ratio = jnp.exp2(offset * (-2.0 * direction * gap * scale))
            running = value
            for b in range(middle, basis_count) if direction == 1 else range(middle - 1, -1, -1):
                if b != middle:
                    running = running * ratio
                basis = running * math.exp(-(((b - middle) * gap / basis_width) ** 2))
                basis = basis.astype(bf16).astype(f32)
                pair = weight * basis
                high = pair.astype(bf16)
                pair_ref[b, places, :] = high
                if rest_ref is not None:
                    rest_ref[b, places, :] = (pair - high.astype(f32)).astype(bf16)
        return carry

    lax.fori_loop(0, count // step, block, 0, unroll=8)


def own_kernel(
    feat_ref,
    positions_ref,
    force_ref,
    slots_ref,
    count_ref,
    species_ref,
    radial_ref,
    mix_ref,
    charge_ref,
    offset_ref,
    filtered_ref,
    words_ref,
    own_ref,
    shift_ref,
    weights_ref,
    extra_ref,
    coords_ref,
    pair_ref,
    rest_ref,
    *,
    box_x,
):
    atoms, width = feat_ref.shape
    slots = slots_ref.shape[0]
    basis_count = radial_ref.shape[0]
    own_rows = positions_ref[...]
    own_feat = turned(feat_ref[...])
    own_ref[...] = own_feat
    coords_ref[...] = jnp.transpose(
        jnp.concatenate([own_rows, jnp.zeros((5, atoms), f32)], axis=0)
    )

    listed = slots_ref[...]
    live = lax.broadcasted_iota(jnp.int32, (slots, atoms), 0) < count_ref[...]
    word_of = jnp.where(live, listed >> 5, -1)
    bit = jnp.left_shift(jnp.ones_like(listed), listed & 31)
    for word in range(words_ref.shape[0]):
        value = jnp.where(word_of == word, bit, 0)
        rows = slots
        while rows > 1:
            rows //= 2
            value = value[:rows] | value[rows:]
        words_ref[word : word + 1, :] = value

    pair_blocks(atoms, coords_ref, own_rows, words_ref, pair_ref, box_x, rest_ref)
    for b in range(basis_count):
        filtered_ref[b] = matmul(own_feat, pair_ref[b]) + matmul(own_feat, rest_ref[b])

    kinds = offset_ref.shape[0]
    one_hot = (
        lax.broadcasted_iota(jnp.int32, (kinds, atoms), 0) == species_ref[...]
    ).astype(f32)
    shift_ref[...] = matmul(jnp.transpose(offset_ref[...]), one_hot, highest)
    charge_count = charge_ref.shape[0]
    weights_ref[0:width, :] = jnp.transpose(mix_ref[...].astype(f32))
    weights_ref[width : width + charge_count, :] = charge_ref[...].astype(f32)
    weights_ref[width + charge_count :, 0:basis_count] = jnp.transpose(
        radial_ref[...].astype(f32)
    )
    lengths = (box_x, box_side, box_side)
    turns = jnp.concatenate([own_rows[a : a + 1, :] * (1.0 / lengths[a]) for a in range(3)], axis=0)
    target = force_ref[...]
    high = target.astype(bf16).astype(f32)
    extra_ref[0:16, :] = jnp.concatenate(
        pieces_of(turns) + (high, target - high, jnp.zeros((1, atoms), f32)), axis=0
    )
    extra_ref[16:24, :] = jnp.concatenate([own_rows, jnp.zeros((5, atoms), f32)], axis=0)


def ghost_pairs(ref, is_low, words_ref, extra_ref, ghost_words_ref, coords_ref, pair_ref, box_x):
    _, ghosts, atoms = pair_ref.shape
    width = ref.shape[1]
    extra = jnp.concatenate(
        [ref[atoms + part * 16 : atoms + part * 16 + 16, :] for part in range(atoms // width)],
        axis=1,
    )
    sends = extra[8:16, :].astype(f32)
    sends = jnp.where(is_low, sends[2:3, :], sends[1:2, :])
    site = lax.broadcasted_iota(jnp.int32, (atoms, ghosts), 0).astype(f32)
    chosen = (site == sends).astype(bf16)
    moved = matmul(extra, chosen)
    moved = moved[0:3, :] + (moved[3:6, :] + moved[6:9, :])
    coords_ref[...] = jnp.transpose(jnp.concatenate([moved, jnp.zeros((5, ghosts), f32)], axis=0))
    count = ghosts // 32
    first = jnp.where(is_low, atoms // 32, atoms // 32 + count)
    ghost_words_ref[...] = words_ref[pl.ds(pl.multiple_of(first, 8), count), :]
    pair_blocks(ghosts, coords_ref, extra_ref[16:24, :], ghost_words_ref, pair_ref, box_x)
    return matmul(turned(ref[0:atoms, :]), chosen).astype(bf16)


def near_kernel(
    where_ref,
    near_ref,
    sofar_ref,
    words_ref,
    extra_ref,
    filtered_ref,
    ghost_words_ref,
    coords_ref,
    pair_ref,
    *,
    box_x,
):
    feat = ghost_pairs(
        near_ref,
        where_ref[0] == 1,
        words_ref,
        extra_ref,
        ghost_words_ref,
        coords_ref,
        pair_ref,
        box_x,
    )
    for b in range(filtered_ref.shape[0]):
        filtered_ref[b] = sofar_ref[b] + matmul(feat, pair_ref[b])


def edge_kernel(
    where_ref,
    far_ref,
    sofar_ref,
    words_ref,
    own_ref,
    shift_ref,
    weights_ref,
    extra_ref,
    filtered_ref,
    messages_ref,
    before_ref,
    hidden_ref,
    shared_ref,
    ghost_words_ref,
    coords_ref,
    pair_ref,
    *,
    box_x,
):
    width, atoms = own_ref.shape
    charge_count = shift_ref.shape[0]
    feat = ghost_pairs(
        far_ref,
        where_ref[0] == 0,
        words_ref,
        extra_ref,
        ghost_words_ref,
        coords_ref,
        pair_ref,
        box_x,
    )
    messages = jnp.zeros((width, atoms), f32)
    for b in range(filtered_ref.shape[0]):
        filtered = sofar_ref[b] + matmul(feat, pair_ref[b])
        filtered_ref[b] = filtered
        messages = messages + weights_ref[width + charge_count :, b : b + 1] * filtered
    messages_ref[...] = messages
    before = exact_matmul(weights_ref[0:width, :].astype(bf16), messages)
    before_ref[...] = before
    hidden = (own_ref[...].astype(f32) + before * sigmoid(before)).astype(bf16)
    hidden_ref[...] = hidden
    charges = matmul(weights_ref[width : width + charge_count, :].astype(bf16), hidden)
    shared_ref[0, 0:charge_count, :] = (charges + shift_ref[...]).astype(bf16)
    shared_ref[0, charge_count : charge_count + 16, :] = extra_ref[0:16, :].astype(bf16)


def wave_rows(wave_ref, first, count, box_x, total_atoms):
    index = wave_ref[:, pl.ds(first, count)].astype(f32)
    scales = (two_pi / box_x, two_pi / box_side, two_pi / box_side)
    waves = [index[a : a + 1, :] * scales[a] for a in range(3)]
    squares = waves[0] * waves[0] + waves[1] * waves[1] + waves[2] * waves[2]
    damping = jnp.exp(-0.5 * kernel_width * kernel_width * squares) * (1.0 / total_atoms)
    return index, waves, damping


def wave_columns(wave_ref, first, share):
    index = wave_ref[:, pl.ds(first, share)].astype(f32)
    return jnp.transpose(
        jnp.concatenate([index] * 3 + [jnp.zeros((7, share), f32)], axis=0)
    ).astype(bf16)


def fill_waves(columns, shared_ref, j, charge_count, waves_ref, place):
    share = columns.shape[0]
    shift = 12582912.0
    turns = matmul(columns, shared_ref[j, charge_count : charge_count + 16, :])
    turns = turns - ((turns + shift) - shift)
    square = turns * turns
    half_sine = turns * horner(short_sine, square)
    half_cosine = horner(short_cosine, square)
    waves_ref[place, 0:share, :] = (half_sine * half_cosine).astype(bf16)
    waves_ref[place, share : 2 * share, :] = (1.0 - half_sine * half_sine).astype(bf16)


def phase_kernel(where_ref, shared_ref, wave_ref, waves_ref, part_ref, *, charge_count):
    count = shared_ref.shape[0]
    share = waves_ref.shape[1] // 2
    columns = wave_columns(wave_ref, pl.multiple_of(where_ref[1] * share, share), share)

    def block(j, carry):
        fill_waves(columns, shared_ref, j, charge_count, waves_ref, j)
        return carry

    lax.fori_loop(0, count, block, 0, unroll=4)
    part = jnp.zeros(part_ref.shape, f32)
    for j in range(count):
        part = part + matmul_nt(shared_ref[j, 0:charge_count, :], waves_ref[j])
    part_ref[...] = part


def placed_waves(early, early_refs, late, waves_ref, count):
    return [
        early_refs[early.index(r)].at[j]
        if r in early
        else waves_ref.at[j * len(late) + late.index(r)]
        for j in range(count)
        for r in range(len(early) + len(late))
    ]


def structure_kernel(where_ref, *refs, group, blocks, early, charge_count, box_x):
    shared_refs, early_refs = refs[:blocks], refs[blocks : blocks + len(early)]
    part_refs, refs = refs[blocks + len(early) : blocks + 2 * len(early)], refs[blocks + 2 * len(early) :]
    wave_ref, waves_ref, weights_ref, *refs = refs
    force_refs, sent_refs = refs[:group], refs[group:]
    rows_refs = [force_refs[0], *sent_refs]
    late = [r for r in range(blocks) if r not in early]
    count, _, atoms = shared_refs[0].shape
    share = waves_ref.shape[1] // 2
    first = pl.multiple_of(where_ref[1] * share, share)
    _, waves, damping = wave_rows(wave_ref, first, share, box_x, blocks * count * atoms)
    columns = wave_columns(wave_ref, first, share)

    def block(j, carry):
        for i, r in enumerate(late):
            fill_waves(columns, shared_refs[r], j, charge_count, waves_ref, j * len(late) + i)
        return carry

    lax.fori_loop(0, count, block, 0, unroll=4)
    waves_of = placed_waves(early, early_refs, late, waves_ref, count)
    structure = sum(ref[...] for ref in part_refs)
    for d in range(blocks * count):
        j, r = divmod(d, blocks)
        if r in late:
            structure = structure + matmul_nt(
                shared_refs[r][j, 0:charge_count, :], waves_of[d][...]
            )
    along_sin = structure[:, :share] * damping
    along_cos = structure[:, share:] * damping
    to_sine = jnp.concatenate([along_cos * waves[a] for a in range(3)], axis=0)
    to_cosine = jnp.concatenate([-along_sin * waves[a] for a in range(3)], axis=0)
    weights = jnp.concatenate([to_sine, to_cosine], axis=1)
    weights_ref[...] = weights
    weights = weights.astype(bf16)
    for d in range(blocks * count):
        j, r = divmod(d, blocks)
        field = matmul(weights, waves_of[d][...])
        charges = shared_refs[r][j, 0:charge_count, :].astype(f32)
        for a in range(3):
            row = jnp.sum(
                field[a * charge_count : (a + 1) * charge_count, :] * charges,
                axis=0,
                keepdims=True,
            )
            for m in range(group):
                rows_refs[m][a, d ^ m : (d ^ m) + 1, :] = row
    for m in range(1, group):
        force_refs[m][...] = rows_refs[m][...].astype(bf16)


def field_kernel(*refs, group, blocks, early, count):
    weights_ref, refs = refs[0], refs[1:]
    early_refs, waves_ref, field_refs = refs[: len(early)], refs[len(early)], refs[len(early) + 1 :]
    late = [r for r in range(blocks) if r not in early]
    waves_of = placed_waves(early, early_refs, late, waves_ref, count)
    weights = weights_ref[...]
    weights_high = weights.astype(bf16)
    weights_low = (weights - weights_high.astype(f32)).astype(bf16)
    for m in range(group):
        block = waves_of[m][...]
        field_refs[m][...] = matmul(weights_high, block) + matmul(weights_low, block)


def charge_gradient(errors, field, back, block):
    charge_count = back.shape[0]
    high = back.astype(bf16)
    low = (back - high.astype(f32)).astype(bf16)
    grad = matmul(high, block) + matmul(low, block)
    for a in range(3):
        grad = grad + errors[a] * field[a * charge_count : (a + 1) * charge_count, :]
    return grad


def gradient_kernel(where_ref, *refs, group, blocks, early, charge_count, box_x):
    shared_refs, part_refs = refs[:blocks], refs[blocks : blocks + group]
    refs = refs[blocks + group :]
    early_refs, refs = refs[: len(early)], refs[len(early) :]
    field_refs, refs = refs[: group - 1], refs[group - 1 :]
    wave_ref, waves_ref, forces_ref, errors_ref, back_ref, *grad_refs, total_ref = refs
    late = [r for r in range(blocks) if r not in early]
    count, _, atoms = shared_refs[0].shape
    share = waves_ref.shape[1] // 2
    first = pl.multiple_of(where_ref[1] * share, share)
    _, waves, damping = wave_rows(wave_ref, first, share, box_x, blocks * count * atoms)
    waves_of = placed_waves(early, early_refs, late, waves_ref, count)
    total = part_refs[0][...]
    for m in range(1, group):
        total = total + part_refs[m][...].astype(f32)
    total_ref[...] = total
    for a in range(3):
        forces_ref[a : a + 1, :] = total[a, 0:1, :]

    def errors_of(d):
        j, r = divmod(d, blocks)
        target = shared_refs[r][j, charge_count : charge_count + 16, :].astype(f32)
        target = target[9:12, :] + target[12:15, :]
        return [2.0 * (total_ref[a, d : d + 1, :] - target[a : a + 1, :]) for a in range(3)]

    by_wave = jnp.zeros((3 * charge_count, 2 * share), f32)
    for d in range(blocks * count):
        j, r = divmod(d, blocks)
        charges = shared_refs[r][j, 0:charge_count, :].astype(f32)
        errors = errors_of(d)
        scaled = jnp.concatenate([errors[a] * charges for a in range(3)], axis=0).astype(bf16)
        by_wave = by_wave + matmul_nt(scaled, waves_of[d][...])
        if d == 0:
            errors_ref[...] = jnp.concatenate(errors + [jnp.zeros((5, atoms), f32)], axis=0)

    def along(value):
        return sum(
            waves[a] * value[a * charge_count : (a + 1) * charge_count, :] for a in range(3)
        )

    back_cos = damping * along(by_wave[:, :share])
    back_sin = -damping * along(by_wave[:, share:])
    back = jnp.concatenate([back_sin, back_cos], axis=1)
    back_ref[...] = back
    for m in range(1, group):
        grad_refs[m - 1][...] = charge_gradient(
            errors_of(m), field_refs[m - 1][...], back, waves_of[m][...]
        ).astype(bf16)


def own_gradient_kernel(errors_ref, field_ref, back_ref, waves_ref, grad_ref):
    errors = errors_ref[...]
    grad_ref[...] = charge_gradient(
        [errors[a : a + 1, :] for a in range(3)], field_ref[...], back_ref[...], waves_ref[0]
    )


def summed(values):
    while len(values) > 1:
        values = [values[i] + values[i + 1] for i in range(0, len(values), 2)]
    return values[0]


def split_rows(value, first, count, sums_ref):
    rows = value.shape[0]
    high = value.astype(bf16)
    sums_ref[0:rows, :] = high
    rest = value[first : first + count, :] - high[first : first + count, :].astype(f32)
    sums_ref[rows:, :] = rest.astype(bf16)


def joined_rows(refs, first, count, value_ref):
    total = summed([ref[...].astype(f32) for ref in refs])
    rows = value_ref.shape[0]
    value_ref[...] = total[0:rows, :]
    value_ref[first : first + count, :] += total[rows:, :]


def column_kernel(*refs, first, count):
    *part_refs, sums_ref = refs
    split_rows(summed([ref[...].astype(f32) for ref in part_refs]), first, count, sums_ref)


def weights_kernel(*refs, group, kinds):
    part_refs = refs[:group]
    (
        filtered_ref,
        messages_ref,
        before_ref,
        hidden_ref,
        species_ref,
        mix_ref,
        charge_ref,
        sums_ref,
        packed_ref,
    ) = refs[group:]
    charge_count, atoms = part_refs[0].shape
    basis_count, width, _ = filtered_ref.shape
    grad = part_refs[0][...].astype(f32)
    for m in range(1, group):
        grad = grad + part_refs[m][...].astype(f32)
    before = before_ref[...]
    gate = sigmoid(before)
    upstream = exact_matmul(turned(charge_ref[...]), grad)
    before_grad = upstream * (gate * (1.0 + before * (1.0 - gate)))
    message_grad = exact_matmul(mix_ref[...], before_grad)
    columns = [
        jnp.sum(message_grad * filtered_ref[b], axis=1, keepdims=True) for b in range(basis_count)
    ]
    radial = jnp.concatenate(columns, axis=1)
    row = 0
    packed_ref[row : row + basis_count, :] = jnp.transpose(radial)
    row += basis_count
    high, low = terms_of(messages_ref[...])
    packed_ref[row : row + width, :] = exact_matmul(high, before_grad, matmul_nt) + matmul_nt(
        low, before_grad.astype(bf16)
    )
    row += width
    high, low = terms_of(grad)
    packed_ref[row : row + charge_count, :] = matmul_nt(high, hidden_ref[...]) + matmul_nt(
        low, hidden_ref[...]
    )
    row += charge_count
    packed_ref[row:, :] = jnp.zeros((packed_ref.shape[0] - row, width), f32)
    one_hot = (
        lax.broadcasted_iota(jnp.int32, (kinds, atoms), 0) == species_ref[...]
    ).astype(f32)
    packed_ref[row : row + kinds, 0:charge_count] = matmul_nt(one_hot, grad, highest)
    sums_ref[...] = packed_ref[...].astype(bf16)


def step_kernel(*refs):
    *total_refs, radial_ref, mix_ref, charge_ref, species_ref, total_ref = refs
    basis_count, width = radial_ref.shape
    charge_count = charge_ref.shape[0]
    kinds = species_ref.shape[0]
    joined_rows(total_refs, basis_count, width, total_ref)

    def normalized(gradient):
        mean = jnp.sum(gradient * gradient, keepdims=True) * (1.0 / gradient.size)
        return gradient * lax.rsqrt(mean + 1e-06)

    row = 0
    radial_ref[...] = normalized(total_ref[row : row + basis_count, :])
    row += basis_count
    mix_ref[...] = normalized(total_ref[row : row + width, :])
    row += width
    charge_ref[...] = normalized(total_ref[row : row + charge_count, :])
    row += charge_count
    species_ref[...] = normalized(total_ref[row : row + kinds, 0:charge_count])


def shaped(*dims, kind=f32):
    return jax.ShapeDtypeStruct(dims, kind)


def kernel(body, name, out_shape, scratch, nanoseconds, *operands, scalars=(), wanted=0):
    outs = out_shape if isinstance(out_shape, tuple) else (out_shape,)
    held = sum(math.prod(x.shape) * x.dtype.itemsize for x in (*outs, *scratch, *operands))
    in_vmem = pl.BlockSpec(memory_space=pltpu.VMEM)
    in_smem = pl.BlockSpec(memory_space=pltpu.SMEM)
    return pl.pallas_call(
        body,
        out_shape=out_shape,
        in_specs=[in_smem] * len(scalars) + [in_vmem] * len(operands),
        out_specs=tuple(in_vmem for _ in outs) if isinstance(out_shape, tuple) else in_vmem,
        scratch_shapes=[pltpu.VMEM(x.shape, x.dtype) for x in scratch],
        compiler_params=pltpu.CompilerParams(vmem_limit_bytes=max(held + spare_vmem, wanted)),
        cost_estimate=pl.CostEstimate(
            flops=nanoseconds * 1_000_000, bytes_accessed=held, transcendentals=0
        ),
        name=name,
    )(*scalars, *operands)


def across(value, bits):
    domains = lax.axis_size("dom")
    return lax.ppermute(value, "dom", [(i, i ^ bits) for i in range(domains)])


def on_device(
    features,
    positions,
    neighbours,
    neighbour_count,
    ghost_sends,
    species,
    wave_index,
    force_ref,
    radial_weight,
    mix_weight,
    charge_weight,
    species_charge,
):
    atoms, width = features.shape
    basis_count = radial_weight.shape[0]
    charge_count = charge_weight.shape[1]
    kinds = species_charge.shape[0]
    wave_count = wave_index.shape[1]
    domains = lax.axis_size("dom")
    box_x = 1.25 * (atoms * domains) / 64
    group = 2 if domains % 2 == 0 else 1
    while (
        group < domains
        and 4 * wave_count // group * atoms * domains > waves_bytes
        and wave_count % (256 * group) == 0
    ):
        group *= 2
    share = wave_count // group
    entries = atoms + 2 * ghost_sends.shape[1]

    me = lax.axis_index("dom")
    blocks = 4 if domains % 4 == 0 else 2
    where = jnp.stack([me % 2, me % group, me % blocks]).astype(jnp.int32)
    packed = kernel(
        pack_kernel,
        "pack",
        shaped(atoms + 16 * (atoms // width), width, kind=bf16),
        (),
        1_000,
        features,
        positions,
        ghost_sends,
        wanted=60 * 1024 * 1024,
    )
    near = across(packed, 1)
    beyond = [(i, (i + 1 if i % 2 else i - 1) % domains) for i in range(domains)]
    far = lax.ppermute(packed, "dom", beyond)
    species_row = species[None, :]
    slots = neighbours.T
    charge_rows = charge_weight.T

    sofar, words, *local, extra = kernel(
        lambda *refs: own_kernel(*refs, box_x=box_x),
        "own",
        (
            shaped(basis_count, width, atoms),
            shaped(entries // 32, atoms, kind=jnp.int32),
            shaped(width, atoms, kind=bf16),
            shaped(charge_count, atoms),
            shaped(2 * width + charge_count, width),
            shaped(24, atoms),
        ),
        (
            shaped(atoms, 8),
            shaped(basis_count, atoms, atoms, kind=bf16),
            shaped(basis_count, atoms, atoms, kind=bf16),
        ),
        4_000,
        features,
        positions,
        force_ref,
        slots,
        neighbour_count[None, :],
        species_row,
        radial_weight,
        mix_weight,
        charge_rows,
        species_charge,
        wanted=own_vmem,
    )
    ghosts = ghost_sends.shape[1]
    scratch = (
        shaped(ghosts // 32, atoms, kind=jnp.int32),
        shaped(ghosts, 8),
        shaped(basis_count, ghosts, atoms, kind=bf16),
    )
    sofar = kernel(
        lambda *refs: near_kernel(*refs, box_x=box_x),
        "near",
        shaped(basis_count, width, atoms),
        scratch,
        3_000,
        near,
        sofar,
        words,
        extra,
        scalars=(where,),
    )
    filtered, messages, before, hidden, shared = kernel(
        lambda *refs: edge_kernel(*refs, box_x=box_x),
        "edges",
        (
            shaped(basis_count, width, atoms),
            shaped(width, atoms),
            shaped(width, atoms),
            shaped(width, atoms, kind=bf16),
            shaped(1, charge_count + 16, atoms, kind=bf16),
        ),
        scratch,
        4_000,
        far,
        sofar,
        words,
        *local,
        extra,
        scalars=(where,),
    )
    column = jnp.concatenate(
        [shared] + [across(shared, bits) for bits in range(blocks, domains, blocks)], axis=0
    )
    columns = [column] + [across(column, bits) for bits in range(1, blocks)]
    early = (0, blocks - 1) if blocks > 2 else (0,)
    waves_early, parts = zip(
        *[
            kernel(
                lambda *refs: phase_kernel(*refs, charge_count=charge_count),
                "phases",
                (
                    shaped(domains // blocks, 2 * share, atoms, kind=bf16),
                    shaped(charge_count, 2 * share),
                ),
                (),
                3_000,
                columns[r],
                wave_index,
                scalars=(where,),
            )
            for r in early
        ]
    )
    waves, weights, *force_parts = kernel(
        lambda *refs: structure_kernel(
            *refs, group=group, blocks=blocks, early=early, charge_count=charge_count, box_x=box_x
        ),
        "structure",
        (
            shaped(domains - len(early) * (domains // blocks), 2 * share, atoms, kind=bf16),
            shaped(3 * charge_count, 2 * share),
        )
        + (shaped(3, domains, atoms),)
        + (shaped(3, domains, atoms, kind=bf16),) * (group - 1),
        (shaped(3, domains, atoms),) * (group - 1),
        8_000,
        *columns,
        *waves_early,
        *parts,
        wave_index,
        scalars=(where,),
    )
    force_parts = force_parts[:1] + [across(force_parts[m], m) for m in range(1, group)]
    fields = kernel(
        lambda *refs: field_kernel(
            *refs, group=group, blocks=blocks, early=early, count=domains // blocks
        ),
        "fields",
        (shaped(3 * charge_count, atoms),) * group,
        (),
        2_000,
        weights,
        *waves_early,
        waves,
    )
    forces, errors, back, *grad_parts = kernel(
        lambda *refs: gradient_kernel(
            *refs, group=group, blocks=blocks, early=early, charge_count=charge_count, box_x=box_x
        ),
        "gradient",
        (
            shaped(3, atoms),
            shaped(8, atoms),
            shaped(charge_count, 2 * share),
        )
        + (shaped(charge_count, atoms, kind=bf16),) * (group - 1),
        (shaped(3, domains, atoms),),
        5_000,
        *columns,
        *force_parts,
        *waves_early,
        *fields[1:],
        wave_index,
        waves,
        scalars=(where,),
    )
    own_part = kernel(
        own_gradient_kernel,
        "own_gradient",
        shaped(charge_count, atoms),
        (),
        1_500,
        errors,
        fields[0],
        back,
        waves_early[0],
    )
    grad_parts = [own_part] + [across(grad_parts[m - 1], m) for m in range(1, group)]

    rows = basis_count + width + charge_count + kinds
    rows = -(-rows // 16) * 16
    packed = kernel(
        lambda *refs: weights_kernel(*refs, group=group, kinds=kinds),
        "weights",
        shaped(rows, width, kind=bf16),
        (shaped(rows, width),),
        3_000,
        *grad_parts,
        filtered,
        messages,
        before,
        hidden,
        species_row,
        mix_weight,
        charge_rows,
    )
    packed = kernel(
        lambda *refs: column_kernel(*refs, first=basis_count, count=width),
        "column",
        shaped(rows + width, width, kind=bf16),
        (),
        1_000,
        packed,
        *[across(packed, bits) for bits in range(blocks, domains, blocks)],
    )
    totals = [packed] + [across(packed, r) for r in range(1, blocks)]
    radial_step, mix_step, charge_step, species_step = kernel(
        step_kernel,
        "steps",
        (
            shaped(basis_count, width),
            shaped(width, width),
            shaped(charge_count, width),
            shaped(kinds, charge_count),
        ),
        (shaped(rows, width),),
        2_000,
        *totals,
    )
    return forces, radial_step, mix_step, charge_step.T, species_step


def solution(mesh):
    placed = (
        P(("cell", "dom"), None),
        P(None, ("cell", "dom")),
        P(("cell", "dom"), None),
        P(("cell", "dom")),
        P(None, ("cell", "dom")),
        P(("cell", "dom")),
        P(),
        P(None, ("cell", "dom")),
        P(),
        P(),
        P(),
        P(),
    )
    return jax.shard_map(
        on_device,
        mesh=mesh,
        in_specs=placed,
        out_specs=(
            P(None, ("cell", "dom")),
            P("cell", None),
            P("cell", None),
            P("cell", None),
            P("cell", None),
        ),
        check_vma=False,
    )
```
